32 devices in a mesh: dom: 4 (over x, core), tile: 8 (over z, y).
Axes of the slice: x: 2, y: 2, z: 4, core: 2. Of those that a mesh axis runs over, the one named last changes fastest.
Arguments:
- embedding: bfloat16 [8192, 1152], P(('dom', 'tile')), may hold values from -6 to 6
- ghost_index: int32 [8192], P(('dom', 'tile')), may hold values from 0 to 255
- tile_count: int32 [4, 8], P('dom'), may hold values from 1 to 96, 384 in all within a row
- edge_source: int32 [393216], P(('dom', 'tile')), may hold values from 0 to 4095
- edge_target: int32 [393216], P(('dom', 'tile')), may hold values from 0 to 255
- edge_features: bfloat16 [393216, 128], P(('dom', 'tile')), may hold values from -6 to 6
- radial_in: bfloat16 [128, 128], replicated, may hold values from -0.5 to 0.5
- radial_out: bfloat16 [128, 384], replicated, may hold values from -0.5 to 0.5
- mix_weight: bfloat16 [3, 256, 128], replicated, may hold values from -0.375 to 0.375
Outputs:
- update: bfloat16 [8192, 1152], P(('dom', 'tile'))
The draws below stay inside these ranges and needn't reach their ends.
Inputs may be any that keep to these rules, and one draw needn't show every extreme that they name: `tile_count`: each row of 8 counts sums to 384 and its largest equals 96.
All inputs are finite; a program needn't handle non-finite values.
Results may differ from the reference program's by a relative error of at most 0.0044.
Values may be sent and summed in bfloat16 or wider, within the bound.
No kernel may reach another device: no remote copies, remote signals or barrier semaphores. Data moves between devices by JAX's collectives and lax.ppermute only.
A program may use at most 128 MiB of HBM per device.

```python
import math
import jax
import jax.numpy as jnp
import numpy as np
from jax import lax

C = 128
K = 9
EC = 128
HID = 128
ATOM_DEV = 256
GHOST = 128
MAXT = 96
TE = 128
ATOMS = 8192
LOCAL = 512
DOMROWS = 4096
EDGES = 393216
N_DOM = 4
N_TILE = 8


def plant(result, own_key, smallest, largest):
    longest = result.shape.index(max(result.shape))
    spots = []
    for shift in (0, 1):
        where = [jax.random.randint(jax.random.fold_in(own_key, axis), (), 0, length) for axis, length in enumerate(result.shape)]
        where[longest] = (where[longest] + shift) % result.shape[longest]
        spots.append(tuple(where))
    return result.at[spots[0]].set(smallest).at[spots[1]].set(largest)


def block_levels(stream_key, shape, split, low, high):
    gain = 1.0
    for axis_at, shards_of in split:
        heights = jax.random.uniform(jax.random.fold_in(jax.random.fold_in(stream_key, 6), axis_at), (shards_of,), jnp.float32, low / len(split), high / len(split))
        gain = gain * jnp.repeat(jnp.exp(heights), shape[axis_at] // shards_of).reshape((-1,) + (1,) * (len(shape) - 1 - axis_at))
    return gain


def split_up(count, total, reach, lean):
    portions = [(1 << 20) // math.isqrt(rank ** lean) + 1 for rank in range(2, count + 1)]
    spare, holding = total - reach - (count - 1), [1] * (count - 1)
    while spare > 0:
        movable = [i for i in range(count - 1) if holding[i] < reach]
        whole, left = sum([portions[i] for i in movable]), spare
        for i in movable:
            extra = min(reach - holding[i], max(1, left * portions[i] // whole), spare)
            holding[i] = holding[i] + extra
            spare = spare - extra
    return np.array([reach] + holding)


def uneven(own_key, amount, total, most, slope):
    if amount == 2:
        one = jax.random.randint(own_key, (), max(1, total - most), min(most, total - 1) + 1)
        return jnp.stack([one, total - one])
    tallies = jnp.asarray(split_up(amount, total, most, slope), jnp.int32)
    twos = (amount - 1) // 2
    source_of, sink = tallies[1:1 + 2 * twos:2], tallies[2:2 + 2 * twos:2]
    margin = jnp.minimum(source_of - 1, most - sink)
    shifted = jax.random.randint(jax.random.fold_in(own_key, 1), (twos,), 0, 1 << 20) % (margin + 1)
    tallies = tallies.at[1:1 + 2 * twos:2].set(source_of - shifted).at[2:2 + 2 * twos:2].set(sink + shifted)
    return tallies[jax.random.permutation(jax.random.fold_in(own_key, 2), amount)]


def bell_draw(rng, shape, spread, bound, cuts=(), kind=jnp.bfloat16):
    drawn = spread * jax.random.normal(rng, shape, jnp.float32)
    if cuts:
        drawn = drawn * block_levels(rng, shape, cuts, -0.22, 0.18)
    return jnp.clip(drawn, -bound, bound).astype(kind)


def setup_inputs(seed: int = 0) -> dict:
    streams_of = jax.random.split(jax.random.key(seed), 10)
    return {
        "embedding": bell_draw(streams_of[0], (ATOMS, K * C), 1.0, 6.0, ((0, 32),)),
        "ghost_index": plant(jax.random.randint(streams_of[1], (ATOMS * 2 * GHOST // ATOM_DEV,), 0, ATOM_DEV), jax.random.fold_in(streams_of[1], 1), 0, ATOM_DEV - 1).astype(jnp.int32),
        "tile_count": jax.vmap(lambda own: uneven(own, N_TILE, N_TILE * MAXT // 2, MAXT, 2))(jax.random.split(streams_of[2], N_DOM)).reshape((N_DOM, N_TILE)).astype(jnp.int32),
        "edge_source": plant(jax.random.randint(streams_of[3], (EDGES,), 0, DOMROWS), jax.random.fold_in(streams_of[3], 1), 0, DOMROWS - 1).astype(jnp.int32),
        "edge_target": plant(jax.random.randint(streams_of[4], (EDGES,), 0, ATOM_DEV), jax.random.fold_in(streams_of[4], 1), 0, ATOM_DEV - 1).astype(jnp.int32),
        "edge_features": bell_draw(streams_of[5], (EDGES, EC), 1.0, 6.0, ((0, 32),)),
        "radial_in": bell_draw(streams_of[6], (EC, HID), EC ** -0.5, 0.5),
        "radial_out": bell_draw(streams_of[7], (HID, 3 * C), HID ** -0.5, 0.5),
        "mix_weight": bell_draw(streams_of[8], (3, 2 * C, C), (2 * C) ** -0.5, 0.375),
    }


degree_bounds = ((0, 1), (1, 4), (4, 9))
inv_scale = 0.125


def edge_messages(rows_table, source_index, target_row, features, live_mask, radial_in, radial_out, mix_weight):
    channels = mix_weight.shape[2]
    radial = jax.nn.silu(jnp.dot(features, radial_in, preferred_element_type=jnp.float32)).astype(jnp.bfloat16)
    gate_values = jnp.dot(radial, radial_out, preferred_element_type=jnp.float32)
    source = jnp.take(rows_table, source_index, axis=0).reshape(-1, K, channels)
    target = jnp.take(rows_table, target_row, axis=0).reshape(-1, K, channels)
    joined = jnp.concatenate([source, target], axis=2).astype(jnp.float32)
    pieces = []
    for degree in range(3):
        lower_row, upper_row = degree_bounds[degree]
        mixing = jnp.einsum("ekc,cd->ekd", joined[:, lower_row:upper_row], mix_weight[degree].astype(jnp.float32))
        pieces.append(mixing * gate_values[:, None, degree * channels:(degree + 1) * channels])
    message = jnp.concatenate(pieces, axis=1).reshape(-1, K * channels)
    return jnp.where(live_mask[:, None], message, 0.0).astype(jnp.bfloat16)


def select_rows(rows_block, picked_rows):
    return jnp.take(rows_block, picked_rows, axis=0)


def reference(embedding, ghost_index, tile_count, edge_source, edge_target, edge_features, radial_in, radial_out, mix_weight):
    row_width = K * C
    grid_embed = embedding.reshape(N_DOM, N_TILE, ATOM_DEV, row_width)
    ghost_grid = ghost_index.reshape(N_DOM, N_TILE, 2 * GHOST)
    outgoing = jax.vmap(jax.vmap(select_rows))(grid_embed, ghost_grid)
    blank_rows = jnp.zeros((1, N_TILE, GHOST, row_width), embedding.dtype)
    from_lower = jnp.concatenate([blank_rows, outgoing[:-1, :, GHOST:]], axis=0)
    from_upper = jnp.concatenate([outgoing[1:, :, :GHOST], blank_rows], axis=0)
    local_rows = jnp.concatenate([grid_embed, from_lower, from_upper], axis=2)
    domain_tables = local_rows.reshape(N_DOM, DOMROWS, row_width)
    sources = edge_source.reshape(N_DOM * N_TILE, MAXT * TE)
    targets = edge_target.reshape(N_DOM * N_TILE, MAXT * TE)
    feature_rows = edge_features.reshape(N_DOM * N_TILE, MAXT * TE, EC)
    counts = tile_count.reshape(N_DOM * N_TILE)
    block_tiles = max(1, min(MAXT, 1024 // TE))
    block_edges = block_tiles * TE

    def one_device(device):
        domain = device // N_TILE
        tile_pos = device % N_TILE
        rows_table = domain_tables[domain]
        count_here = counts[device]
        total_blocks = (count_here + block_tiles - 1) // block_tiles

        def add_block(block_number, running):
            first_edge = (block_number * block_edges).astype(jnp.int32)
            source_index = lax.dynamic_slice_in_dim(sources[device], first_edge, block_edges)
            target_local = lax.dynamic_slice_in_dim(targets[device], first_edge, block_edges)
            features = lax.dynamic_slice_in_dim(feature_rows[device], first_edge, block_edges)
            live_mask = (first_edge + jnp.arange(block_edges, dtype=jnp.int32)) // TE < count_here
            target_row = (tile_pos * LOCAL + target_local).astype(jnp.int32)
            message = edge_messages(rows_table, source_index, target_row, features, live_mask, radial_in, radial_out, mix_weight)
            return running + jax.ops.segment_sum(message.astype(jnp.float32), target_local, num_segments=ATOM_DEV)

        running = lax.fori_loop(0, total_blocks, add_block, jnp.zeros((ATOM_DEV, row_width), jnp.float32))
        return (inv_scale * running).astype(jnp.bfloat16)

    updates = lax.map(one_device, jnp.arange(N_DOM * N_TILE, dtype=jnp.int32))
    return updates.reshape(ATOMS, row_width)
```

```python
import functools
import jax
import jax.numpy as jnp
from jax import lax
from jax.experimental import pallas as pl
from jax.experimental.pallas import tpu as pltpu
from jax.sharding import PartitionSpec as P

C = 128
K = 9
ATOM_DEV = 256
GHOST = 128
TE = 128
BE = 256
CHUNK = 256
CHUNK_BITS = 8
WIDTH = K * C
degree_of = (0, 1, 1, 1, 2, 2, 2, 2, 2)
inv_scale = 0.125

F32 = jnp.float32
BF16 = jnp.bfloat16
I32 = jnp.int32

PARAMS = pltpu.CompilerParams(vmem_limit_bytes=58 * 1024 * 1024)


def vmem():
    return pl.BlockSpec(memory_space=pltpu.VMEM)


def smem():
    return pl.BlockSpec(memory_space=pltpu.SMEM)


def cols(k):
    return slice(k * C, (k + 1) * C)


def iota(shape, dim):
    return lax.broadcasted_iota(I32, shape, dim)


def as_bf16(mask):
    return jnp.where(mask, 1.0, 0.0).astype(BF16)


def dot(a, b):
    return jnp.dot(a, b, preferred_element_type=F32)


def mix_kernel(x_ref, mix_ref, pick_ref, mixed_ref, out_ref):
    for k in range(K):
        mixed_ref[:, cols(k)] = dot(x_ref[:, cols(k)], mix_ref[degree_of[k], :C]).astype(BF16)
    half = GHOST
    for part in range(2):
        picks = pick_ref[pl.ds(part, 1), :]
        chosen_t = as_bf16(iota((ATOM_DEV, half), 0) == picks)
        chosen = chosen_t.astype(F32).T.astype(BF16)
        out_ref[part * half : (part + 1) * half, :] = dot(chosen, mixed_ref[...]).astype(BF16)


def rank_kernel(count_ref, src_ref, pos_ref, span_ref, oh_ref, cum_ref):
    tiles = src_ref.shape[0]
    nb = span_ref.shape[0] // 2
    count = count_ref[0]
    bucket_id = iota((nb, TE), 0)

    def mark(t, carry):
        bucket = src_ref[pl.ds(t, 1), :] >> CHUNK_BITS
        bucket = jnp.where(t < count, bucket, -1)
        oh_ref[pl.ds(pl.multiple_of(t * nb, nb), nb), :] = as_bf16(bucket_id == bucket)
        return carry

    lax.fori_loop(0, tiles, mark, 0, unroll=8)
    upto = as_bf16(iota((TE, TE), 0) <= iota((TE, TE), 1))
    both = jnp.concatenate([upto, jnp.ones((TE, TE), BF16)], axis=1)
    step = 256
    for r in range(0, tiles * nb, step):
        cum_ref[r : r + step, :] = dot(oh_ref[r : r + step, :], both)

    def add(t, total):
        return total + cum_ref[pl.ds(pl.multiple_of(t * nb, nb), nb), TE:]

    total = lax.fori_loop(0, tiles, add, jnp.zeros((nb, TE), F32), unroll=8)
    blocks = jnp.floor((total + (BE - 1)) * (1.0 / BE))
    below = as_bf16(iota((nb, nb), 1) < iota((nb, nb), 0))
    first = dot(below, blocks.astype(BF16))
    span_ref[:nb, :] = first.astype(I32)
    span_ref[nb:, :] = blocks.astype(I32)

    def place(t, run):
        rows = pl.ds(pl.multiple_of(t * nb, nb), nb)
        oh = oh_ref[rows, :].astype(F32)
        value = oh * (cum_ref[rows, :TE] + run)
        pos_ref[pl.ds(t, 1), :] = jnp.sum(value, axis=0, keepdims=True).astype(I32)
        return run + cum_ref[rows, TE:]

    lax.fori_loop(0, tiles, place, first * BE - 1.0, unroll=8)


def sort_kernel(
    count_ref,
    pos_ref,
    span_ref,
    src_ref,
    tgt_ref,
    feat_ref,
    rin_ref,
    rad_ref,
    srcb_ref,
    tgts_ref,
    rsum_ref,
    rad32,
    code32,
    tmp_r,
    tmp_c,
):
    nb = span_ref.shape[0] // 2
    count = count_ref[0]
    rsum_ref[...] = jnp.zeros_like(rsum_ref)

    def clear(b, carry):
        blocks = span_ref[nb + b, 0]

        @pl.when(blocks > 0)
        def _():
            last = pl.multiple_of((span_ref[b, 0] + blocks - 1) * BE, BE)
            rad32[pl.ds(last, BE), :] = jnp.zeros((BE, C), F32)
            code32[pl.ds(last, BE), :] = jnp.full((BE, C), -1.0, F32)

        return carry

    lax.fori_loop(0, nb, clear, 0)
    eye = iota((TE, TE), 0) == iota((TE, TE), 1)
    spread = jnp.concatenate(
        [jnp.ones((TE, C), BF16), jnp.full((TE, C), float(CHUNK), BF16)], axis=0
    )

    def tile(t, carry):
        rows = pl.ds(pl.multiple_of(t * TE, TE), TE)
        hidden = dot(feat_ref[rows, :], rin_ref[...])
        radial = (hidden / (1.0 + jnp.exp(-hidden))).astype(BF16)
        tmp_r[...] = radial.astype(F32)
        src = src_ref[pl.ds(t, 1), :] & (CHUNK - 1)
        tgt = tgt_ref[pl.ds(t, 1), :]
        diag_s = jnp.where(eye, src.astype(F32), 0.0).astype(BF16)
        diag_t = jnp.where(eye, tgt.astype(F32), 0.0).astype(BF16)
        tmp_c[...] = dot(jnp.concatenate([diag_s, diag_t], axis=1), spread)
        rsum_ref[...] += dot(as_bf16(iota((ATOM_DEV, TE), 0) == tgt), radial)
        for e in range(TE):
            p = pos_ref[t, e]
            rad32[pl.ds(p, 1), :] = tmp_r[e : e + 1, :]
            code32[pl.ds(p, 1), :] = tmp_c[e : e + 1, :]
        return carry

    lax.fori_loop(0, count, tile, 0)

    def finish(j, carry):
        rows = pl.ds(pl.multiple_of(j * TE, TE), TE)
        rad_ref[rows, :] = rad32[rows, :].astype(BF16)
        code = code32[rows, :].astype(I32)
        srcb_ref[rows, :] = (code & (CHUNK - 1)).astype(F32).astype(BF16)
        tgt = (code >> CHUNK_BITS).astype(F32)
        tgts_ref[pl.ds(j, 1), :] = jnp.sum(
            jnp.where(eye, tgt, 0.0), axis=0, keepdims=True
        ).astype(I32)
        return carry

    used = (span_ref[nb - 1, 0] + span_ref[2 * nb - 1, 0]) * (BE // TE)
    lax.fori_loop(0, used, finish, 0)


def main_kernel(
    span_ref,
    table_ref,
    rad_hbm,
    src_hbm,
    tgt_ref,
    rout_ref,
    rsum_ref,
    x_ref,
    mix_ref,
    out_ref,
    acc_ref,
    rbuf,
    sbuf,
    sems,
):
    nb = span_ref.shape[0] // 2
    total = span_ref[nb - 1, 0] + span_ref[2 * nb - 1, 0]
    acc_ref[...] = jnp.zeros_like(acc_ref)

    def copies(j, slot):
        rows = pl.ds(pl.multiple_of(j * BE, BE), BE)
        return (
            pltpu.make_async_copy(rad_hbm.at[rows, :], rbuf.at[slot], sems.at[0, slot]),
            pltpu.make_async_copy(src_hbm.at[rows, :], sbuf.at[slot], sems.at[1, slot]),
        )

    for copy in copies(0, 0):
        copy.start()

    row_id = iota((BE, TE), 1).astype(F32)
    atom_id = iota((ATOM_DEV, TE), 0)

    def chunk(c, carry):
        table_rows = pl.ds(pl.multiple_of(c * CHUNK, CHUNK), CHUNK)

        def block(j, inner):
            slot = j & 1
            for copy in copies(j, slot):
                copy.wait()

            @pl.when(j + 1 < total)
            def _():
                for copy in copies(j + 1, 1 - slot):
                    copy.start()

            src = sbuf[slot].astype(F32)
            pick = jnp.concatenate(
                [as_bf16(src == row_id), as_bf16(src == row_id + float(TE))], axis=1
            )
            gate = dot(rbuf[slot], rout_ref[...])
            land = jnp.concatenate(
                [
                    as_bf16(atom_id == tgt_ref[pl.ds(2 * j, 1), :]),
                    as_bf16(atom_id == tgt_ref[pl.ds(2 * j + 1, 1), :]),
                ],
                axis=1,
            )
            for k in range(K):
                rows = dot(pick, table_ref[table_rows, cols(k)])
                message = (rows * gate[:, cols(degree_of[k])]).astype(BF16)
                acc_ref[:, cols(k)] += dot(land, message)
            return inner

        first = span_ref[c, 0]
        return lax.fori_loop(first, first + span_ref[nb + c, 0], block, carry)

    lax.fori_loop(0, nb, chunk, 0)
    gate_sum = jnp.dot(
        rsum_ref[...],
        rout_ref[...].astype(F32),
        preferred_element_type=F32,
        precision=lax.Precision.HIGHEST,
    )
    for k in range(K):
        own = dot(x_ref[:, cols(k)], mix_ref[degree_of[k], C:])
        full = acc_ref[:, cols(k)] + own * gate_sum[:, cols(degree_of[k])]
        out_ref[:, cols(k)] = (inv_scale * full).astype(BF16)


def shape(dims, kind):
    return jax.ShapeDtypeStruct(dims, kind)


def cost(flops, size):
    return pl.CostEstimate(flops=int(flops), bytes_accessed=int(size), transcendentals=0)


def body(
    embedding,
    ghost_index,
    tile_count,
    edge_source,
    edge_target,
    edge_features,
    radial_in,
    radial_out,
    mix_weight,
):
    n_dom, n_tile = lax.axis_size("dom"), lax.axis_size("tile")
    tiles = edge_source.shape[0] // TE
    table_rows = n_tile * (ATOM_DEV + 2 * GHOST)
    nb = table_rows // CHUNK
    slots = (tiles * TE // BE + nb) * BE
    count = lax.dynamic_slice_in_dim(tile_count[0], lax.axis_index("tile"), 1)
    source = edge_source.reshape(tiles, TE)
    target = edge_target.reshape(tiles, TE)

    mixed, outgoing = pl.pallas_call(
        mix_kernel,
        out_shape=(shape((ATOM_DEV, WIDTH), BF16), shape((2 * GHOST, WIDTH), BF16)),
        in_specs=[vmem(), vmem(), vmem()],
        out_specs=(vmem(), vmem()),
        compiler_params=PARAMS,
        cost_estimate=cost(2 * 256 * 256 * 1152, 2e6),
        name="mix",
    )(embedding, mix_weight, ghost_index.reshape(2, GHOST))
    up = [(i, i + 1) for i in range(n_dom - 1)]
    down = [(i + 1, i) for i in range(n_dom - 1)]
    low = lax.ppermute(outgoing[GHOST:], "dom", up)
    high = lax.ppermute(outgoing[:GHOST], "dom", down)
    local_rows = jnp.concatenate([mixed, low, high], axis=0)
    table = lax.all_gather(local_rows, "tile", axis=0, tiled=True)

    pos, span = pl.pallas_call(
        rank_kernel,
        out_shape=(shape((tiles, TE), I32), shape((2 * nb, TE), I32)),
        in_specs=[smem(), vmem()],
        out_specs=(vmem(), vmem()),
        scratch_shapes=[
            pltpu.VMEM((tiles * nb, TE), BF16),
            pltpu.VMEM((tiles * nb, 2 * TE), F32),
        ],
        compiler_params=PARAMS,
        cost_estimate=cost(5e9, 1e6),
        name="rank",
    )(count, source)
    radial, source_sorted, target_sorted, radial_sum = pl.pallas_call(
        sort_kernel,
        out_shape=(
            shape((slots, C), BF16),
            shape((slots, C), BF16),
            shape((slots // TE, TE), I32),
            shape((ATOM_DEV, C), F32),
        ),
        in_specs=[smem(), smem(), smem(), vmem(), vmem(), vmem(), vmem()],
        out_specs=(vmem(), vmem(), vmem(), vmem()),
        scratch_shapes=[
            pltpu.VMEM((slots, C), F32),
            pltpu.VMEM((slots, C), F32),
            pltpu.VMEM((TE, C), F32),
            pltpu.VMEM((TE, C), F32),
        ],
        compiler_params=PARAMS,
        cost_estimate=cost(20e9, 12e6),
        name="sort",
    )(count, pos, span, source, target, edge_features, radial_in)
    return pl.pallas_call(
        main_kernel,
        out_shape=shape((ATOM_DEV, WIDTH), BF16),
        in_specs=[smem(), vmem(), pl.BlockSpec(memory_space=pl.ANY), pl.BlockSpec(memory_space=pl.ANY)]
        + [vmem()] * 5,
        out_specs=vmem(),
        scratch_shapes=[
            pltpu.VMEM((ATOM_DEV, WIDTH), F32),
            pltpu.VMEM((2, BE, C), BF16),
            pltpu.VMEM((2, BE, C), BF16),
            pltpu.SemaphoreType.DMA((2, 2)),
        ],
        compiler_params=PARAMS,
        cost_estimate=cost(15e9, 20e6),
        name="main",
    )(span, table, radial, source_sorted, target_sorted, radial_out, radial_sum, embedding, mix_weight)


def solution(mesh):
    both = ("dom", "tile")
    return jax.shard_map(
        body,
        mesh=mesh,
        in_specs=(
            P(both, None),
            P(both),
            P("dom", None),
            P(both),
            P(both),
            P(both, None),
            P(),
            P(),
            P(),
        ),
        out_specs=P(both, None),
        check_vma=False,
    )
```

```python
import functools
import jax
import jax.numpy as jnp
from jax import lax
from jax.experimental import pallas as pl
from jax.experimental.pallas import tpu as pltpu
from jax.sharding import PartitionSpec as P

C = 128
K = 9
ATOM_DEV = 256
GHOST = 128
TE = 128
BE = 256
CHUNK = 256
CHUNK_BITS = 8
WIDTH = K * C
degree_of = (0, 1, 1, 1, 2, 2, 2, 2, 2)
inv_scale = 0.125

F32 = jnp.float32
BF16 = jnp.bfloat16
I32 = jnp.int32

PARAMS = pltpu.CompilerParams(vmem_limit_bytes=58 * 1024 * 1024)


def vmem():
    return pl.BlockSpec(memory_space=pltpu.VMEM)


def smem():
    return pl.BlockSpec(memory_space=pltpu.SMEM)


def cols(k):
    return slice(k * C, (k + 1) * C)


def iota(shape, dim):
    return lax.broadcasted_iota(I32, shape, dim)


def as_bf16(mask):
    return jnp.where(mask, 1.0, 0.0).astype(BF16)


def dot(a, b):
    return jnp.dot(a, b, preferred_element_type=F32)


def mix_kernel(x_ref, mix_ref, mixed_ref):
    for k in range(K):
        mixed = dot(x_ref[:, cols(k)], mix_ref[degree_of[k], :C])
        mixed_ref[cols(k), :] = mixed.T.astype(BF16)


def pick_kernel(pick_ref, rows_ref, down_ref, up_ref):
    for t in range(rows_ref.shape[0]):
        for part, out_ref in ((0, down_ref), (1, up_ref)):
            picks = pick_ref[2 * t + part : 2 * t + part + 1, :]
            chosen = as_bf16(iota((ATOM_DEV, GHOST), 0) == picks)
            out_ref[t] = dot(rows_ref[t], chosen).astype(BF16)


def rank_kernel(count_ref, src_ref, label_ref, pos_ref, span_ref, oh_ref, cum_ref, *, slots):
    tiles = src_ref.shape[0]
    nb = span_ref.shape[0] // 2
    count = count_ref[0]
    label = label_ref[...]

    def mark(t, carry):
        bucket = src_ref[pl.ds(t, 1), :] >> CHUNK_BITS
        bucket = jnp.where(t < count, bucket, -1)
        oh_ref[pl.ds(pl.multiple_of(t * nb, nb), nb), :] = as_bf16(label == bucket)
        return carry

    lax.fori_loop(0, tiles, mark, 0, unroll=8)
    upto = as_bf16(iota((TE, TE), 0) <= iota((TE, TE), 1))
    both = jnp.concatenate([upto, jnp.ones((TE, TE), BF16)], axis=1)
    step = 256
    for r in range(0, tiles * nb, step):
        cum_ref[r : r + step, :] = dot(oh_ref[r : r + step, :], both)

    def add(t, total):
        return total + cum_ref[pl.ds(pl.multiple_of(t * nb, nb), nb), TE:]

    total = lax.fori_loop(0, tiles, add, jnp.zeros((nb, TE), F32), unroll=8)
    blocks = jnp.floor((total + (BE - 1)) * (1.0 / BE))
    below = as_bf16(iota((nb, nb), 1) < iota((nb, nb), 0))
    first = dot(below, blocks.astype(BF16))
    span_ref[:nb, :] = first.astype(I32)
    span_ref[nb:, :] = blocks.astype(I32)

    def place(t, run):
        rows = pl.ds(pl.multiple_of(t * nb, nb), nb)
        oh = oh_ref[rows, :].astype(F32)
        value = oh * (cum_ref[rows, :TE] + run)
        place_of = jnp.sum(value, axis=0, keepdims=True).astype(I32)
        pos_ref[pl.ds(t, 1), :] = jnp.where(t < count, place_of, slots)
        return run + cum_ref[rows, TE:]

    lax.fori_loop(0, tiles, place, first * BE - 1.0, unroll=8)


def sort_kernel(
    count_ref,
    pos_ref,
    span_ref,
    src_ref,
    tgt_ref,
    feat_ref,
    rin_ref,
    rad_ref,
    tgtb_ref,
    srcs_ref,
    rsum_ref,
    rad32,
    code32,
    even_r,
    even_c,
    odd_r,
    odd_c,
):
    tiles = src_ref.shape[0]
    nb = span_ref.shape[0] // 2
    count = count_ref[0]
    rsum_ref[...] = jnp.zeros_like(rsum_ref)

    def clear(b, carry):
        blocks = span_ref[nb + b, 0]

        @pl.when(blocks > 0)
        def _():
            last = pl.multiple_of((span_ref[b, 0] + blocks - 1) * BE, BE)
            rad32[pl.ds(last, BE), :] = jnp.zeros((BE, C), F32)
            code32[pl.ds(last, BE), :] = jnp.full((BE, C), -1.0, F32)

        return carry

    lax.fori_loop(0, nb, clear, 0)
    eye = iota((TE, TE), 0) == iota((TE, TE), 1)
    spread = jnp.concatenate(
        [jnp.ones((TE, C), BF16), jnp.full((TE, C), float(CHUNK), BF16)], axis=0
    )

    def compute(t, r_ref, c_ref):
        live = t < count
        t = jnp.minimum(t, tiles - 1)
        rows = pl.ds(pl.multiple_of(t * TE, TE), TE)
        hidden = dot(feat_ref[rows, :], rin_ref[...])
        radial = (hidden / (1.0 + jnp.exp(-hidden))).astype(BF16)
        r_ref[...] = radial.astype(F32)
        src = src_ref[pl.ds(t, 1), :] & (CHUNK - 1)
        tgt = tgt_ref[pl.ds(t, 1), :]
        diag_s = jnp.where(eye, src.astype(F32), 0.0).astype(BF16)
        diag_t = jnp.where(eye, tgt.astype(F32), 0.0).astype(BF16)
        c_ref[...] = dot(jnp.concatenate([diag_s, diag_t], axis=1), spread)
        tgt = jnp.where(live, tgt, -1)
        rsum_ref[...] += dot(as_bf16(iota((ATOM_DEV, TE), 0) == tgt), radial)

    def scatter(t, r_ref, c_ref):
        for e in range(TE):
            p = pos_ref[t, e]
            rad32[pl.ds(p, 1), :] = r_ref[e : e + 1, :]
            code32[pl.ds(p, 1), :] = c_ref[e : e + 1, :]

    compute(0, even_r, even_c)

    def pair(i, carry):
        compute(2 * i + 1, odd_r, odd_c)
        scatter(2 * i, even_r, even_c)
        compute(2 * i + 2, even_r, even_c)
        scatter(2 * i + 1, odd_r, odd_c)
        return carry

    lax.fori_loop(0, (count + 1) // 2, pair, 0)

    def finish(j, carry):
        rows = pl.ds(pl.multiple_of(j * BE, BE), BE)
        rad_ref[rows, :] = rad32[rows, :].astype(BF16)
        code = code32[rows, :].astype(I32)
        tgtb_ref[rows, :] = (code >> CHUNK_BITS).astype(F32).astype(BF16)
        src = (code & (CHUNK - 1)).astype(F32)
        for h in range(BE // TE):
            part = jnp.where(eye, src[h * TE : (h + 1) * TE, :], 0.0)
            row = pl.ds(j * (BE // TE) + h, 1)
            srcs_ref[row, :] = jnp.sum(part, axis=0, keepdims=True).astype(I32)
        return carry

    used = span_ref[nb - 1, 0] + span_ref[2 * nb - 1, 0]
    lax.fori_loop(0, used, finish, 0)


def main_kernel(*refs, low, count, split, final):
    span_ref, *refs = refs
    tables, refs = refs[: (2 if split else 1)], refs[(2 if split else 1) :]
    rad_hbm, tgt_hbm, src_ref, rout_ref, *refs = refs
    if final:
        part_ref, rsum_ref, x_ref, mix_ref, *refs = refs
    out_ref, rbuf, tbuf, sems, *refs = refs
    acc_ref = refs[0] if final else out_ref
    nb = span_ref.shape[0] // 2
    begin = span_ref[low, 0]
    end = span_ref[low + count - 1, 0] + span_ref[nb + low + count - 1, 0]

    def copies(j, slot):
        rows = pl.ds(pl.multiple_of(j * BE, BE), BE)
        return (
            pltpu.make_async_copy(rad_hbm.at[rows, :], rbuf.at[slot], sems.at[0, slot]),
            pltpu.make_async_copy(tgt_hbm.at[rows, :], tbuf.at[slot], sems.at[1, slot]),
        )

    @pl.when(begin < end)
    def _():
        for copy in copies(begin, begin & 1):
            copy.start()

    if final:
        acc_ref[...] = part_ref[...]
    else:
        acc_ref[...] = jnp.zeros_like(acc_ref)
    rout_t = rout_ref[...].astype(F32).T.astype(BF16)
    atom_id = iota((BE, TE), 1).astype(F32)
    row_id = iota((CHUNK, TE), 0)

    def chunk(c, carry):
        def block(j, inner):
            slot = j & 1
            for copy in copies(j, slot):
                copy.wait()

            @pl.when(j + 1 < end)
            def _():
                for copy in copies(j + 1, 1 - slot):
                    copy.start()

            tgt = tbuf[slot].astype(F32)
            land = jnp.concatenate(
                [as_bf16(tgt == atom_id), as_bf16(tgt == atom_id + float(TE))], axis=1
            )
            gate = lax.dot_general(
                rout_t, rbuf[slot], (((1,), (1,)), ((), ())), preferred_element_type=F32
            )
            pick = jnp.concatenate(
                [
                    as_bf16(row_id == src_ref[pl.ds(j * (BE // TE) + h, 1), :])
                    for h in range(BE // TE)
                ],
                axis=1,
            )
            if split:
                table = jnp.concatenate([tables[0][c], tables[1][c]], axis=1)
            else:
                table = tables[0][c]
            rows = dot(table, pick)
            message = jnp.concatenate(
                [(rows[cols(k), :] * gate[cols(degree_of[k]), :]).astype(BF16) for k in range(K)],
                axis=0,
            )
            acc_ref[...] += dot(message, land)
            return inner

        first = span_ref[low + c, 0]
        return lax.fori_loop(first, first + span_ref[nb + low + c, 0], block, carry)

    lax.fori_loop(0, count, chunk, 0)
    if not final:
        return
    gate_sum = jnp.dot(
        rsum_ref[...],
        rout_ref[...].astype(F32),
        preferred_element_type=F32,
        precision=lax.Precision.HIGHEST,
    )
    for k in range(K):
        own = dot(x_ref[:, cols(k)], mix_ref[degree_of[k], C:])
        full = acc_ref[cols(k), :].T + own * gate_sum[:, cols(degree_of[k])]
        out_ref[:, cols(k)] = (inv_scale * full).astype(BF16)


def shape(dims, kind):
    return jax.ShapeDtypeStruct(dims, kind)


def cost(flops, size):
    return pl.CostEstimate(flops=int(flops), bytes_accessed=int(size), transcendentals=0)


def body(
    embedding,
    ghost_index,
    tile_count,
    edge_source,
    edge_target,
    edge_features,
    radial_in,
    radial_out,
    mix_weight,
):
    n_dom, n_tile = lax.axis_size("dom"), lax.axis_size("tile")
    tiles = edge_source.shape[0] // TE
    nb = 2 * n_tile
    slots = (tiles * TE // BE + nb) * BE
    count = lax.dynamic_slice_in_dim(tile_count[0], lax.axis_index("tile"), 1)
    source = edge_source.reshape(tiles, TE)
    target = edge_target.reshape(tiles, TE)
    hbm = pl.BlockSpec(memory_space=pl.ANY)

    mixed = pl.pallas_call(
        mix_kernel,
        out_shape=shape((WIDTH, ATOM_DEV), BF16),
        in_specs=[vmem(), vmem()],
        out_specs=vmem(),
        compiler_params=PARAMS,
        cost_estimate=cost(256 * 256 * 1152, 2e6),
        name="mix",
    )(embedding, mix_weight)
    picks = lax.all_gather(ghost_index, "tile", axis=0, tiled=True).reshape(2 * n_tile, GHOST)
    blocks = lax.all_gather(mixed, "tile", axis=0, tiled=False)
    order = jnp.arange(nb, dtype=I32)
    label = jnp.where(order < n_tile, 2 * order, 2 * (order - n_tile) + 1)
    label = jnp.broadcast_to(label[:, None], (nb, TE))

    pos, span = pl.pallas_call(
        functools.partial(rank_kernel, slots=slots),
        out_shape=(shape((tiles, TE), I32), shape((2 * nb, TE), I32)),
        in_specs=[smem(), vmem(), vmem()],
        out_specs=(vmem(), vmem()),
        scratch_shapes=[
            pltpu.VMEM((tiles * nb, TE), BF16),
            pltpu.VMEM((tiles * nb, 2 * TE), F32),
        ],
        compiler_params=PARAMS,
        cost_estimate=cost(5e9, 1e6),
        name="rank",
    )(count, source, label)
    radial, target_sorted, source_sorted, radial_sum = pl.pallas_call(
        sort_kernel,
        out_shape=(
            shape((slots, C), BF16),
            shape((slots, C), BF16),
            shape((slots // TE, TE), I32),
            shape((ATOM_DEV, C), F32),
        ),
        in_specs=[smem(), smem(), smem(), vmem(), vmem(), vmem(), vmem()],
        out_specs=(vmem(), vmem(), vmem(), vmem()),
        scratch_shapes=[
            pltpu.VMEM((slots + 8, C), F32),
            pltpu.VMEM((slots + 8, C), F32),
        ]
        + [pltpu.VMEM((TE, C), F32)] * 4,
        compiler_params=PARAMS,
        cost_estimate=cost(20e9, 12e6),
        name="sort",
    )(count, pos, span, source, target, edge_features, radial_in)

    down_rows, up_rows = pl.pallas_call(
        pick_kernel,
        out_shape=(shape((n_tile, WIDTH, GHOST), BF16),) * 2,
        in_specs=[vmem(), vmem()],
        out_specs=(vmem(), vmem()),
        compiler_params=PARAMS,
        cost_estimate=cost(2e9, 10e6),
        name="pick",
    )(picks, blocks)
    up = [(i, i + 1) for i in range(n_dom - 1)]
    down = [(i + 1, i) for i in range(n_dom - 1)]
    lower = lax.ppermute(up_rows, "dom", up)
    upper = lax.ppermute(down_rows, "dom", down)

    def main(low, tables, final_args):
        final = len(final_args) > 0
        dims, kind = ((ATOM_DEV, WIDTH), BF16) if final else ((WIDTH, ATOM_DEV), F32)
        return pl.pallas_call(
            functools.partial(
                main_kernel, low=low, count=n_tile, split=len(tables) > 1, final=final
            ),
            out_shape=shape(dims, kind),
            in_specs=[smem()]
            + [vmem()] * len(tables)
            + [hbm, hbm, vmem(), vmem()]
            + [vmem()] * len(final_args),
            out_specs=vmem(),
            scratch_shapes=[
                pltpu.VMEM((2, BE, C), BF16),
                pltpu.VMEM((2, BE, C), BF16),
                pltpu.SemaphoreType.DMA((2, 2)),
            ]
            + ([pltpu.VMEM((WIDTH, ATOM_DEV), F32)] if final else []),
            compiler_params=PARAMS,
            cost_estimate=cost(12e9, 10e6),
            name="main_ghost" if final else "main_own",
        )(span, *tables, radial, target_sorted, source_sorted, radial_out, *final_args)

    part = main(0, (blocks,), ())
    return main(n_tile, (lower, upper), (part, radial_sum, embedding, mix_weight))


def solution(mesh):
    both = ("dom", "tile")
    return jax.shard_map(
        body,
        mesh=mesh,
        in_specs=(
            P(both, None),
            P(both),
            P("dom", None),
            P(both),
            P(both),
            P(both, None),
            P(),
            P(),
            P(),
        ),
        out_specs=P(both, None),
        check_vma=False,
    )
```

```python
import functools
import jax
import jax.numpy as jnp
from jax import lax
from jax.experimental import pallas as pl
from jax.experimental.pallas import tpu as pltpu
from jax.sharding import PartitionSpec as P

C = 128
K = 9
ATOM_DEV = 256
GHOST = 128
TE = 128
BE = 256
CHUNK = 256
CHUNK_BITS = 8
WIDTH = K * C
EXTRA = 16
degree_of = (0, 1, 1, 1, 2, 2, 2, 2, 2)
inv_scale = 0.125

F32 = jnp.float32
BF16 = jnp.bfloat16
I32 = jnp.int32

PARAMS = pltpu.CompilerParams(vmem_limit_bytes=58 * 1024 * 1024)


def vmem():
    return pl.BlockSpec(memory_space=pltpu.VMEM)


def smem():
    return pl.BlockSpec(memory_space=pltpu.SMEM)


def cols(k):
    return slice(k * C, (k + 1) * C)


def iota(shape, dim):
    return lax.broadcasted_iota(I32, shape, dim)


def as_bf16(mask):
    return jnp.where(mask, 1.0, 0.0).astype(BF16)


def dot(a, b):
    return jnp.dot(a, b, preferred_element_type=F32)


def mix_kernel(x_ref, mix_ref, pick_ref, mixed_ref):
    for k in range(K):
        mixed = dot(x_ref[:, cols(k)], mix_ref[degree_of[k], :C])
        mixed_ref[cols(k), :] = mixed.T.astype(BF16)
    picks = jnp.broadcast_to(pick_ref[...].astype(F32), (EXTRA, ATOM_DEV))
    mixed_ref[WIDTH:, :] = picks.astype(BF16)


def pick_kernel(rows_ref, down_ref, up_ref):
    for t in range(rows_ref.shape[0]):
        picks = rows_ref[t, WIDTH:, :].astype(F32)[:1, :].astype(I32)
        for part, out_ref in ((0, down_ref), (1, up_ref)):
            chosen = as_bf16(
                iota((ATOM_DEV, GHOST), 0) == picks[:, part * GHOST : (part + 1) * GHOST]
            )
            out_ref[t] = dot(rows_ref[t, :WIDTH, :], chosen).astype(BF16)


def rank_kernel(count_ref, src_ref, label_ref, pos_ref, span_ref, oh_ref, cum_ref, *, slots):
    tiles = src_ref.shape[0]
    nb = span_ref.shape[0] // 3
    count = count_ref[0]
    label = label_ref[...]

    def mark(t, carry):
        bucket = src_ref[pl.ds(t, 1), :] >> CHUNK_BITS
        bucket = jnp.where(t < count, bucket, -1)
        oh_ref[pl.ds(pl.multiple_of(t * nb, nb), nb), :] = as_bf16(label == bucket)
        return carry

    lax.fori_loop(0, tiles, mark, 0, unroll=8)
    upto = as_bf16(iota((TE, TE), 0) <= iota((TE, TE), 1))
    both = jnp.concatenate([upto, jnp.ones((TE, TE), BF16)], axis=1)
    step = 256
    for r in range(0, tiles * nb, step):
        cum_ref[r : r + step, :] = dot(oh_ref[r : r + step, :], both)

    def add(t, total):
        return total + cum_ref[pl.ds(pl.multiple_of(t * nb, nb), nb), TE:]

    total = lax.fori_loop(0, tiles, add, jnp.zeros((nb, TE), F32), unroll=8)
    blocks = jnp.floor((total + (BE - 1)) * (1.0 / BE))
    below = as_bf16(iota((nb, nb), 1) < iota((nb, nb), 0))
    first = dot(below, blocks.astype(BF16))
    span_ref[:nb, :] = first.astype(I32)
    span_ref[nb : 2 * nb, :] = blocks.astype(I32)
    passed = jnp.where(iota((nb, TE), 1).astype(F32) >= first + blocks, 1.0, 0.0)
    chunk_of = jnp.minimum(jnp.sum(passed, axis=0, keepdims=True), nb - 1.0)
    span_ref[2 * nb :, :] = jnp.broadcast_to(chunk_of, (nb, TE)).astype(I32)

    def place(t, run):
        rows = pl.ds(pl.multiple_of(t * nb, nb), nb)
        oh = oh_ref[rows, :].astype(F32)
        value = oh * (cum_ref[rows, :TE] + run)
        place_of = jnp.sum(value, axis=0, keepdims=True).astype(I32)
        pos_ref[pl.ds(t, 1), :] = jnp.where(t < count, 2 * place_of, 2 * slots)
        return run + cum_ref[rows, TE:]

    lax.fori_loop(0, tiles, place, first * BE - 1.0, unroll=8)


def sort_kernel(
    count_ref,
    pos_ref,
    span_ref,
    src_ref,
    tgt_ref,
    feat_ref,
    rin_ref,
    rad_ref,
    tgtb_ref,
    srcs_ref,
    rsum_ref,
    pairs,
    even,
    odd,
):
    tiles = src_ref.shape[0]
    nb = span_ref.shape[0] // 3
    count = count_ref[0]
    rsum_ref[...] = jnp.zeros_like(rsum_ref)
    blank = jnp.where((iota((2 * BE, C), 0) & 1) == 1, -1.0, 0.0)

    def clear(b, carry):
        blocks = span_ref[nb + b, 0]

        @pl.when(blocks > 0)
        def _():
            last = pl.multiple_of((span_ref[b, 0] + blocks - 1) * (2 * BE), 2 * BE)
            pairs[pl.ds(last, 2 * BE), :] = blank

        return carry

    lax.fori_loop(0, nb, clear, 0)
    eye = iota((TE, TE), 0) == iota((TE, TE), 1)
    spread = jnp.concatenate(
        [jnp.ones((TE, C), BF16), jnp.full((TE, C), float(CHUNK), BF16)], axis=0
    )

    def compute(t, out):
        live = t < count
        t = jnp.minimum(t, tiles - 1)
        rows = pl.ds(pl.multiple_of(t * TE, TE), TE)
        hidden = dot(feat_ref[rows, :], rin_ref[...])
        radial = (hidden / (1.0 + jnp.exp(-hidden))).astype(BF16)
        out[pl.ds(0, TE, stride=2), :] = radial.astype(F32)
        src = src_ref[pl.ds(t, 1), :] & (CHUNK - 1)
        tgt = tgt_ref[pl.ds(t, 1), :]
        diag_s = jnp.where(eye, src.astype(F32), 0.0).astype(BF16)
        diag_t = jnp.where(eye, tgt.astype(F32), 0.0).astype(BF16)
        code = dot(jnp.concatenate([diag_s, diag_t], axis=1), spread)
        out[pl.ds(1, TE, stride=2), :] = code
        tgt = jnp.where(live, tgt, -1)
        rsum_ref[...] += dot(as_bf16(iota((ATOM_DEV, TE), 0) == tgt), radial)

    def scatter(t, data):
        for e in range(TE):
            pairs[pl.ds(pos_ref[t, e], 2), :] = data[2 * e : 2 * e + 2, :]

    compute(0, even)

    def step(i, carry):
        compute(2 * i + 1, odd)
        scatter(2 * i, even)
        compute(2 * i + 2, even)
        scatter(2 * i + 1, odd)
        return carry

    lax.fori_loop(0, (count + 1) // 2, step, 0)

    def finish(j, carry):
        rows = pl.ds(pl.multiple_of(j * BE, BE), BE)
        base = pl.multiple_of(j * (2 * BE), 2 * BE)
        rad_ref[rows, :] = pairs[pl.ds(base, BE, stride=2), :].astype(BF16)
        code = pairs[pl.ds(base + 1, BE, stride=2), :].astype(I32)
        tgtb_ref[rows, :] = (code >> CHUNK_BITS).astype(F32).astype(BF16)
        src = (code & (CHUNK - 1)).astype(F32)
        for h in range(BE // TE):
            part = jnp.where(eye, src[h * TE : (h + 1) * TE, :], 0.0)
            row = pl.ds(j * (BE // TE) + h, 1)
            srcs_ref[row, :] = jnp.sum(part, axis=0, keepdims=True).astype(I32)
        return carry

    used = span_ref[nb - 1, 0] + span_ref[2 * nb - 1, 0]
    lax.fori_loop(0, used, finish, 0)


def main_kernel(*refs, low, count, split, final):
    span_ref, *refs = refs
    tables, refs = refs[: (2 if split else 1)], refs[(2 if split else 1) :]
    rad_hbm, tgt_hbm, src_ref, rout_ref, *refs = refs
    if final:
        part_ref, rsum_ref, x_ref, mix_ref, *refs = refs
    out_ref, rbuf, tbuf, land_ref, message_ref, sems, *refs = refs
    acc_ref = refs[0] if final else out_ref
    nb = span_ref.shape[0] // 3
    begin = span_ref[low, 0]
    end = span_ref[low + count - 1, 0] + span_ref[nb + low + count - 1, 0]
    pairs = (end - begin + 1) // 2

    def copies(p, slot):
        moves = []
        for h in range(2):
            j = jnp.minimum(begin + 2 * p + h, end - 1)
            rows = pl.ds(pl.multiple_of(j * BE, BE), BE)
            moves.append(
                pltpu.make_async_copy(rad_hbm.at[rows, :], rbuf.at[slot, h], sems.at[0, h, slot])
            )
            moves.append(
                pltpu.make_async_copy(tgt_hbm.at[rows, :], tbuf.at[slot, h], sems.at[1, h, slot])
            )
        return moves

    def fetch(p):
        @pl.when(p < pairs)
        def _():
            for copy in copies(p, p & 1):
                copy.start()

    def arrive(p):
        @pl.when(p < pairs)
        def _():
            for copy in copies(p, p & 1):
                copy.wait()

    fetch(0)
    if final:
        acc_ref[...] = part_ref[...]
    else:
        acc_ref[...] = jnp.zeros_like(acc_ref)
    rout_t = rout_ref[...].astype(F32).T.astype(BF16)
    atom_id = iota((BE, TE), 1).astype(F32)
    row_id = iota((CHUNK, TE), 0)

    def gather(p):
        for h in range(2):
            j = begin + 2 * p + h
            off = jnp.where(j < end, 0.0, 4096.0)
            j = jnp.maximum(jnp.minimum(j, end - 1), 0)
            c = jnp.clip(span_ref[2 * nb, j] - low, 0, count - 1)
            gate = lax.dot_general(
                rout_t, rbuf[p & 1, h], (((1,), (1,)), ((), ())), preferred_element_type=F32
            )
            pick = jnp.concatenate(
                [
                    as_bf16(row_id == src_ref[pl.ds(j * (BE // TE) + q, 1), :])
                    for q in range(BE // TE)
                ],
                axis=1,
            )
            if split:
                table = jnp.concatenate([tables[0][c], tables[1][c]], axis=1)
            else:
                table = tables[0][c, :WIDTH, :]
            rows = dot(table, pick)
            for k in range(K):
                message = rows[cols(k), :] * gate[cols(degree_of[k]), :]
                message_ref[cols(k), h * BE : (h + 1) * BE] = message.astype(BF16)
            tgt = tbuf[p & 1, h].astype(F32) + off
            for q in range(ATOM_DEV // TE):
                land_ref[h * BE : (h + 1) * BE, q * TE : (q + 1) * TE] = as_bf16(
                    tgt == atom_id + float(q * TE)
                )

    arrive(0)
    fetch(1)
    gather(0)

    def step(p, carry):
        arrive(p + 1)
        fetch(p + 2)
        acc_ref[...] += dot(message_ref[...], land_ref[...])
        gather(p + 1)
        return carry

    lax.fori_loop(0, pairs, step, 0)
    if not final:
        return
    gate_sum = jnp.dot(
        rsum_ref[...],
        rout_ref[...].astype(F32),
        preferred_element_type=F32,
        precision=lax.Precision.HIGHEST,
    )
    for k in range(K):
        own = dot(x_ref[:, cols(k)], mix_ref[degree_of[k], C:])
        full = acc_ref[cols(k), :].T + own * gate_sum[:, cols(degree_of[k])]
        out_ref[:, cols(k)] = (inv_scale * full).astype(BF16)


def shape(dims, kind):
    return jax.ShapeDtypeStruct(dims, kind)


def cost(flops, size):
    return pl.CostEstimate(flops=int(flops), bytes_accessed=int(size), transcendentals=0)


def body(
    embedding,
    ghost_index,
    tile_count,
    edge_source,
    edge_target,
    edge_features,
    radial_in,
    radial_out,
    mix_weight,
):
    n_dom, n_tile = lax.axis_size("dom"), lax.axis_size("tile")
    tiles = edge_source.shape[0] // TE
    nb = 2 * n_tile
    slots = (tiles * TE // BE + nb) * BE
    count = lax.dynamic_slice_in_dim(tile_count[0], lax.axis_index("tile"), 1)
    source = edge_source.reshape(tiles, TE)
    target = edge_target.reshape(tiles, TE)
    hbm = pl.BlockSpec(memory_space=pl.ANY)

    mixed = pl.pallas_call(
        mix_kernel,
        out_shape=shape((WIDTH + EXTRA, ATOM_DEV), BF16),
        in_specs=[vmem(), vmem(), vmem()],
        out_specs=vmem(),
        compiler_params=PARAMS,
        cost_estimate=cost(256 * 256 * 1152, 2e6),
        name="mix",
    )(embedding, mix_weight, ghost_index.reshape(1, ATOM_DEV))
    blocks = lax.all_gather(mixed, "tile", axis=0, tiled=False)
    order = jnp.arange(nb, dtype=I32)
    label = jnp.where(order < n_tile, 2 * order, 2 * (order - n_tile) + 1)
    label = jnp.broadcast_to(label[:, None], (nb, TE))

    pos, span = pl.pallas_call(
        functools.partial(rank_kernel, slots=slots),
        out_shape=(shape((tiles, TE), I32), shape((3 * nb, TE), I32)),
        in_specs=[smem(), vmem(), vmem()],
        out_specs=(vmem(), vmem()),
        scratch_shapes=[
            pltpu.VMEM((tiles * nb, TE), BF16),
            pltpu.VMEM((tiles * nb, 2 * TE), F32),
        ],
        compiler_params=PARAMS,
        cost_estimate=cost(5e9, 1e6),
        name="rank",
    )(count, source, label)
    radial, target_sorted, source_sorted, radial_sum = pl.pallas_call(
        sort_kernel,
        out_shape=(
            shape((slots, C), BF16),
            shape((slots, C), BF16),
            shape((slots // TE, TE), I32),
            shape((ATOM_DEV, C), F32),
        ),
        in_specs=[smem(), smem(), smem(), vmem(), vmem(), vmem(), vmem()],
        out_specs=(vmem(), vmem(), vmem(), vmem()),
        scratch_shapes=[
            pltpu.VMEM((2 * slots + 8, C), F32),
            pltpu.VMEM((2 * TE, C), F32),
            pltpu.VMEM((2 * TE, C), F32),
        ],
        compiler_params=PARAMS,
        cost_estimate=cost(20e9, 12e6),
        name="sort",
    )(count, pos, span, source, target, edge_features, radial_in)

    blocks, radial = lax.optimization_barrier((blocks, radial))
    down_rows, up_rows = pl.pallas_call(
        pick_kernel,
        out_shape=(shape((n_tile, WIDTH, GHOST), BF16),) * 2,
        in_specs=[vmem()],
        out_specs=(vmem(), vmem()),
        compiler_params=PARAMS,
        cost_estimate=cost(2e9, 10e6),
        name="pick",
    )(blocks)
    up = [(i, i + 1) for i in range(n_dom - 1)]
    down = [(i + 1, i) for i in range(n_dom - 1)]
    lower = lax.ppermute(up_rows, "dom", up)
    upper = lax.ppermute(down_rows, "dom", down)

    def main(low, tables, final_args):
        final = len(final_args) > 0
        dims, kind = ((ATOM_DEV, WIDTH), BF16) if final else ((WIDTH, ATOM_DEV), F32)
        return pl.pallas_call(
            functools.partial(
                main_kernel, low=low, count=n_tile, split=len(tables) > 1, final=final
            ),
            out_shape=shape(dims, kind),
            in_specs=[smem()]
            + [vmem()] * len(tables)
            + [hbm, hbm, vmem(), vmem()]
            + [vmem()] * len(final_args),
            out_specs=vmem(),
            scratch_shapes=[
                pltpu.VMEM((2, 2, BE, C), BF16),
                pltpu.VMEM((2, 2, BE, C), BF16),
                pltpu.VMEM((2 * BE, ATOM_DEV), BF16),
                pltpu.VMEM((WIDTH, 2 * BE), BF16),
                pltpu.SemaphoreType.DMA((2, 2, 2)),
            ]
            + ([pltpu.VMEM((WIDTH, ATOM_DEV), F32)] if final else []),
            compiler_params=PARAMS,
            cost_estimate=cost(12e9, 10e6),
            name="main_ghost" if final else "main_own",
        )(span, *tables, radial, target_sorted, source_sorted, radial_out, *final_args)

    part = main(0, (blocks,), ())
    return main(n_tile, (lower, upper), (part, radial_sum, embedding, mix_weight))


def solution(mesh):
    both = ("dom", "tile")
    return jax.shard_map(
        body,
        mesh=mesh,
        in_specs=(
            P(both, None),
            P(both),
            P("dom", None),
            P(both),
            P(both),
            P(both, None),
            P(),
            P(),
            P(),
        ),
        out_specs=P(both, None),
        check_vma=False,
    )
```

```python
import functools
import jax
import jax.numpy as jnp
from jax import lax
from jax.experimental import pallas as pl
from jax.experimental.pallas import tpu as pltpu
from jax.sharding import PartitionSpec as P

C = 128
K = 9
ATOM_DEV = 256
GHOST = 128
TE = 128
BE = 256
CHUNK = 256
CHUNK_BITS = 8
WIDTH = K * C
EXTRA = 16
PER = 4
degree_of = (0, 1, 1, 1, 2, 2, 2, 2, 2)
inv_scale = 0.125

F32 = jnp.float32
BF16 = jnp.bfloat16
I32 = jnp.int32

PARAMS = pltpu.CompilerParams(vmem_limit_bytes=58 * 1024 * 1024)


def vmem():
    return pl.BlockSpec(memory_space=pltpu.VMEM)


def smem():
    return pl.BlockSpec(memory_space=pltpu.SMEM)


def cols(k):
    return slice(k * C, (k + 1) * C)


def iota(shape, dim):
    return lax.broadcasted_iota(I32, shape, dim)


def as_bf16(mask):
    return jnp.where(mask, 1.0, 0.0).astype(BF16)


def dot(a, b):
    return jnp.dot(a, b, preferred_element_type=F32)


def mix_kernel(x_ref, mix_ref, pick_ref, mixed_ref):
    for k in range(K):
        mixed = dot(x_ref[:, cols(k)], mix_ref[degree_of[k], :C])
        mixed_ref[cols(k), :] = mixed.T.astype(BF16)
    picks = jnp.broadcast_to(pick_ref[...].astype(F32), (EXTRA, ATOM_DEV))
    mixed_ref[WIDTH:, :] = picks.astype(BF16)


def pick_kernel(*refs):
    *blocks, down_ref, up_ref = refs
    for i, rows_ref in enumerate(blocks):
        picks = rows_ref[WIDTH:, :].astype(F32)[:1, :].astype(I32)
        chosen = as_bf16(iota((ATOM_DEV, 2 * GHOST), 0) == picks)
        rows = dot(rows_ref[:WIDTH, :], chosen).astype(BF16)
        down_ref[i] = rows[:, :GHOST]
        up_ref[i] = rows[:, GHOST:]


def rank_kernel(count_ref, src_ref, label_ref, pos_ref, span_ref, oh_ref, cum_ref, *, slots):
    tiles = src_ref.shape[0]
    nb = span_ref.shape[0] // 3
    count = count_ref[0]
    label = label_ref[...]

    def mark(t, carry):
        bucket = src_ref[pl.ds(t, 1), :] >> CHUNK_BITS
        bucket = jnp.where(t < count, bucket, -1)
        oh_ref[pl.ds(pl.multiple_of(t * nb, nb), nb), :] = as_bf16(label == bucket)
        return carry

    lax.fori_loop(0, tiles, mark, 0, unroll=8)
    upto = as_bf16(iota((TE, TE), 0) <= iota((TE, TE), 1))
    both = jnp.concatenate([upto, jnp.ones((TE, TE), BF16)], axis=1)
    step = 256
    for r in range(0, tiles * nb, step):
        cum_ref[r : r + step, :] = dot(oh_ref[r : r + step, :], both)

    def add(t, total):
        return total + cum_ref[pl.ds(pl.multiple_of(t * nb, nb), nb), TE:]

    total = lax.fori_loop(0, tiles, add, jnp.zeros((nb, TE), F32), unroll=8)
    blocks = jnp.floor((total + (BE - 1)) * (1.0 / BE))
    below = as_bf16(iota((nb, nb), 1) < iota((nb, nb), 0))
    first = dot(below, blocks.astype(BF16))
    span_ref[:nb, :] = first.astype(I32)
    span_ref[nb : 2 * nb, :] = blocks.astype(I32)
    passed = jnp.where(iota((nb, TE), 1).astype(F32) >= first + blocks, 1.0, 0.0)
    chunk_of = jnp.minimum(jnp.sum(passed, axis=0, keepdims=True), nb - 1.0)
    span_ref[2 * nb :, :] = jnp.broadcast_to(chunk_of, (nb, TE)).astype(I32)

    def place(t, run):
        rows = pl.ds(pl.multiple_of(t * nb, nb), nb)
        oh = oh_ref[rows, :].astype(F32)
        value = oh * (cum_ref[rows, :TE] + run)
        place_of = jnp.sum(value, axis=0, keepdims=True).astype(I32)
        pos_ref[pl.ds(t, 1), :] = jnp.where(t < count, 2 * place_of, 2 * slots)
        return run + cum_ref[rows, TE:]

    lax.fori_loop(0, tiles, place, first * BE - 1.0, unroll=8)


def radial_kernel(count_ref, tgt_ref, feat_ref, rin_ref, rad_ref, rsum_ref):
    tiles = tgt_ref.shape[0]
    count = count_ref[0]
    rsum_ref[...] = jnp.zeros_like(rsum_ref)
    group = 4
    atom_id = iota((ATOM_DEV, TE), 0)

    def step(i, carry):
        rows = pl.ds(pl.multiple_of(i * (group * TE), group * TE), group * TE)
        hidden = dot(feat_ref[rows, :], rin_ref[...])
        radial = (hidden / (1.0 + jnp.exp(-hidden))).astype(BF16)
        rad_ref[rows, :] = radial
        land = []
        for q in range(group):
            t = i * group + q
            tgt = jnp.where(t < count, tgt_ref[pl.ds(t, 1), :], -1)
            land.append(as_bf16(atom_id == tgt))
        rsum_ref[...] += dot(jnp.concatenate(land, axis=1), radial)
        return carry

    lax.fori_loop(0, (count + group - 1) // group, step, 0)


def place_kernel(
    count_ref, pos_ref, span_ref, src_ref, tgt_ref, rin_ref, rad_ref, tgtb_ref, srcs_ref, pairs, even, odd
):
    tiles = src_ref.shape[0]
    nb = span_ref.shape[0] // 3
    count = count_ref[0]
    blank = jnp.where((iota((2 * BE, C), 0) & 1) == 1, -1.0, 0.0)

    def clear(b, carry):
        blocks = span_ref[nb + b, 0]

        @pl.when(blocks > 0)
        def _():
            last = pl.multiple_of((span_ref[b, 0] + blocks - 1) * (2 * BE), 2 * BE)
            pairs[pl.ds(last, 2 * BE), :] = blank

        return carry

    lax.fori_loop(0, nb, clear, 0)
    eye = iota((TE, TE), 0) == iota((TE, TE), 1)
    spread = jnp.concatenate(
        [jnp.ones((TE, C), BF16), jnp.full((TE, C), float(CHUNK), BF16)], axis=0
    )

    def compute(t, out):
        t = jnp.minimum(t, tiles - 1)
        rows = pl.ds(pl.multiple_of(t * TE, TE), TE)
        out[pl.ds(0, TE, stride=2), :] = rin_ref[rows, :].astype(F32)
        src = src_ref[pl.ds(t, 1), :] & (CHUNK - 1)
        tgt = tgt_ref[pl.ds(t, 1), :]
        diag_s = jnp.where(eye, src.astype(F32), 0.0).astype(BF16)
        diag_t = jnp.where(eye, tgt.astype(F32), 0.0).astype(BF16)
        code = dot(jnp.concatenate([diag_s, diag_t], axis=1), spread)
        out[pl.ds(1, TE, stride=2), :] = code

    def scatter(t, data):
        for e in range(TE):
            pairs[pl.ds(pos_ref[t, e], 2), :] = data[2 * e : 2 * e + 2, :]

    compute(0, even)

    def step(i, carry):
        compute(2 * i + 1, odd)
        scatter(2 * i, even)
        compute(2 * i + 2, even)
        scatter(2 * i + 1, odd)
        return carry

    lax.fori_loop(0, (count + 1) // 2, step, 0)

    def finish(j, carry):
        rows = pl.ds(pl.multiple_of(j * BE, BE), BE)
        base = pl.multiple_of(j * (2 * BE), 2 * BE)
        rad_ref[rows, :] = pairs[pl.ds(base, BE, stride=2), :].astype(BF16)
        code = pairs[pl.ds(base + 1, BE, stride=2), :].astype(I32)
        tgtb_ref[rows, :] = (code >> CHUNK_BITS).astype(F32).astype(BF16)
        src = (code & (CHUNK - 1)).astype(F32)
        for h in range(BE // TE):
            part = jnp.where(eye, src[h * TE : (h + 1) * TE, :], 0.0)
            row = pl.ds(j * (BE // TE) + h, 1)
            srcs_ref[row, :] = jnp.sum(part, axis=0, keepdims=True).astype(I32)
        return carry

    used = span_ref[nb - 1, 0] + span_ref[2 * nb - 1, 0]
    lax.fori_loop(0, used, finish, 0)


def main_kernel(*refs, low, n_ghost, n_own, first, final):
    span_ref, *refs = refs
    ghosts, refs = refs[: 2 * (n_ghost > 0)], refs[2 * (n_ghost > 0) :]
    owns, refs = refs[:n_own], refs[n_own:]
    rad_hbm, tgt_hbm, src_ref, rout_ref, *refs = refs
    if not first:
        part_ref, *refs = refs
    if final:
        rsum_ref, x_ref, mix_ref, *refs = refs
    out_ref, rbuf, tbuf, land_ref, message_ref, tables, sems, table_sems, *refs = refs
    acc_ref = refs[0] if final else out_ref
    count = n_ghost + n_own
    nb = span_ref.shape[0] // 3
    begin = span_ref[low, 0]
    end = span_ref[low + count - 1, 0] + span_ref[nb + low + count - 1, 0]
    groups = (end - begin + PER - 1) // PER

    loads = []
    for i, own in enumerate(owns):
        loads.append((own.at[:WIDTH, :], tables.at[n_ghost + i]))
    for i in range(n_ghost):
        for side in range(2):
            half = tables.at[i, :, side * GHOST : (side + 1) * GHOST]
            loads.append((ghosts[side].at[i], half))
    loads = [
        pltpu.make_async_copy(src, dst, table_sems.at[i]) for i, (src, dst) in enumerate(loads)
    ]
    for load in loads:
        load.start()

    def copies(p, slot):
        moves = []
        for h in range(PER):
            j = jnp.minimum(begin + PER * p + h, end - 1)
            rows = pl.ds(pl.multiple_of(j * BE, BE), BE)
            moves.append(
                pltpu.make_async_copy(rad_hbm.at[rows, :], rbuf.at[slot, h], sems.at[0, h, slot])
            )
            moves.append(
                pltpu.make_async_copy(tgt_hbm.at[rows, :], tbuf.at[slot, h], sems.at[1, h, slot])
            )
        return moves

    def fetch(p):
        @pl.when(p < groups)
        def _():
            for copy in copies(p, p & 1):
                copy.start()

    def arrive(p):
        @pl.when(p < groups)
        def _():
            for copy in copies(p, p & 1):
                copy.wait()

    fetch(0)
    if first:
        acc_ref[...] = jnp.zeros_like(acc_ref)
    else:
        acc_ref[...] = part_ref[...]
    rout_t = rout_ref[...].astype(F32).T.astype(BF16)
    atom_id = iota((BE, TE), 1).astype(F32)
    row_id = iota((CHUNK, TE), 0)

    def gather(p):
        for h in range(PER):
            j = begin + PER * p + h
            off = jnp.where(j < end, 0.0, 4096.0)
            j = jnp.maximum(jnp.minimum(j, end - 1), 0)
            c = jnp.clip(span_ref[2 * nb, j] - low, 0, count - 1)
            gate = lax.dot_general(
                rout_t, rbuf[p & 1, h], (((1,), (1,)), ((), ())), preferred_element_type=F32
            )
            pick = jnp.concatenate(
                [
                    as_bf16(row_id == src_ref[pl.ds(j * (BE // TE) + q, 1), :])
                    for q in range(BE // TE)
                ],
                axis=1,
            )
            rows = dot(tables[c], pick)
            for k in range(K):
                message = rows[cols(k), :] * gate[cols(degree_of[k]), :]
                message_ref[cols(k), h * BE : (h + 1) * BE] = message.astype(BF16)
            tgt = tbuf[p & 1, h].astype(F32) + off
            for q in range(ATOM_DEV // TE):
                land_ref[h * BE : (h + 1) * BE, q * TE : (q + 1) * TE] = as_bf16(
                    tgt == atom_id + float(q * TE)
                )

    for load in loads:
        load.wait()
    arrive(0)
    fetch(1)
    gather(0)

    def step(p, carry):
        arrive(p + 1)
        fetch(p + 2)
        acc_ref[...] += dot(message_ref[...], land_ref[...])
        gather(p + 1)
        return carry

    lax.fori_loop(0, groups, step, 0)
    if not final:
        return
    gate_sum = jnp.dot(
        rsum_ref[...],
        rout_ref[...].astype(F32),
        preferred_element_type=F32,
        precision=lax.Precision.HIGHEST,
    )
    for k in range(K):
        own = dot(x_ref[:, cols(k)], mix_ref[degree_of[k], C:])
        full = acc_ref[cols(k), :].T + own * gate_sum[:, cols(degree_of[k])]
        out_ref[:, cols(k)] = (inv_scale * full).astype(BF16)


def shape(dims, kind):
    return jax.ShapeDtypeStruct(dims, kind)


def cost(flops, size):
    return pl.CostEstimate(flops=int(flops), bytes_accessed=int(size), transcendentals=0)


def body(
    embedding,
    ghost_index,
    tile_count,
    edge_source,
    edge_target,
    edge_features,
    radial_in,
    radial_out,
    mix_weight,
):
    n_dom, n_tile = lax.axis_size("dom"), lax.axis_size("tile")
    tiles = edge_source.shape[0] // TE
    nb = 2 * n_tile
    slots = (tiles * TE // BE + nb) * BE
    count = lax.dynamic_slice_in_dim(tile_count[0], lax.axis_index("tile"), 1)
    source = edge_source.reshape(tiles, TE)
    target = edge_target.reshape(tiles, TE)
    hbm = pl.BlockSpec(memory_space=pl.ANY)

    mixed = pl.pallas_call(
        mix_kernel,
        out_shape=shape((WIDTH + EXTRA, ATOM_DEV), BF16),
        in_specs=[vmem(), vmem(), vmem()],
        out_specs=vmem(),
        compiler_params=PARAMS,
        cost_estimate=cost(256 * 256 * 1152, 2e6),
        name="mix",
    )(embedding, mix_weight, ghost_index.reshape(1, ATOM_DEV))
    ring = [(t, (t + 2) % n_tile) for t in range(n_tile)]
    flip = [(t, t ^ 1) for t in range(n_tile)]
    up = [(i, i + 1) for i in range(n_dom - 1)]
    down = [(i + 1, i) for i in range(n_dom - 1)]
    n_ring = n_tile // 2
    half = n_tile // 2

    tile_pos = lax.axis_index("tile")
    order = jnp.arange(nb, dtype=I32)
    quarter = order // half
    index = order - half * ((quarter + 1) // 2)
    steps, other = index // 2, index % 2
    origin = 2 * ((tile_pos // 2 - steps) % n_ring) + ((tile_pos % 2) ^ other)
    label = 2 * origin + quarter % 2
    label = jnp.broadcast_to(label[:, None], (nb, TE))

    pos, span = pl.pallas_call(
        functools.partial(rank_kernel, slots=slots),
        out_shape=(shape((tiles, TE), I32), shape((3 * nb, TE), I32)),
        in_specs=[smem(), vmem(), vmem()],
        out_specs=(vmem(), vmem()),
        scratch_shapes=[
            pltpu.VMEM((tiles * nb, TE), BF16),
            pltpu.VMEM((tiles * nb, 2 * TE), F32),
        ],
        compiler_params=PARAMS,
        cost_estimate=cost(4e9, 1e6),
        name="rank",
    )(count, source, label)
    radial, radial_sum = pl.pallas_call(
        radial_kernel,
        out_shape=(shape((tiles * TE, C), BF16), shape((ATOM_DEV, C), F32)),
        in_specs=[smem(), vmem(), vmem(), vmem()],
        out_specs=(vmem(), vmem()),
        compiler_params=PARAMS,
        cost_estimate=cost(10e9, 6e6),
        name="radial",
    )(count, target, edge_features, radial_in)

    def place(radial):
        return pl.pallas_call(
            place_kernel,
            out_shape=(
                shape((slots, C), BF16),
                shape((slots, C), BF16),
                shape((slots // TE, TE), I32),
            ),
            in_specs=[smem(), smem(), smem(), vmem(), vmem(), vmem()],
            out_specs=(vmem(), vmem(), vmem()),
            scratch_shapes=[
                pltpu.VMEM((2 * slots + 8, C), F32),
                pltpu.VMEM((2 * TE, C), F32),
                pltpu.VMEM((2 * TE, C), F32),
            ],
            compiler_params=PARAMS,
            cost_estimate=cost(20e9, 12e6),
            name="place",
        )(count, pos, span, source, target, radial)

    def pick(blocks):
        down_rows, up_rows = pl.pallas_call(
            pick_kernel,
            out_shape=(shape((len(blocks), WIDTH, GHOST), BF16),) * 2,
            in_specs=[vmem()] * len(blocks),
            out_specs=(vmem(), vmem()),
            compiler_params=PARAMS,
            cost_estimate=cost(3e9, 5e6),
            name="pick",
        )(*blocks)
        return [lax.ppermute(up_rows, "dom", up), lax.ppermute(down_rows, "dom", down)]

    def main(low, ghosts, owns, part, final_args, name):
        final = len(final_args) > 0
        dims, kind = ((ATOM_DEV, WIDTH), BF16) if final else ((WIDTH, ATOM_DEV), F32)
        n_ghost = half if ghosts else 0
        count_all = n_ghost + len(owns)
        extra = [*part, *final_args]
        return pl.pallas_call(
            functools.partial(
                main_kernel,
                low=low,
                n_ghost=n_ghost,
                n_own=len(owns),
                first=not part,
                final=final,
            ),
            out_shape=shape(dims, kind),
            in_specs=[smem()]
            + [hbm] * (len(ghosts) + len(owns) + 2)
            + [vmem()] * (2 + len(extra)),
            out_specs=vmem(),
            scratch_shapes=[
                pltpu.VMEM((2, PER, BE, C), BF16),
                pltpu.VMEM((2, PER, BE, C), BF16),
                pltpu.VMEM((PER * BE, ATOM_DEV), BF16),
                pltpu.VMEM((WIDTH, PER * BE), BF16),
                pltpu.VMEM((count_all, WIDTH, ATOM_DEV), BF16),
                pltpu.SemaphoreType.DMA((2, PER, 2)),
                pltpu.SemaphoreType.DMA((2 * n_ghost + len(owns),)),
            ]
            + ([pltpu.VMEM((WIDTH, ATOM_DEV), F32)] if final else []),
            compiler_params=PARAMS,
            cost_estimate=cost(3e9 * count_all, 2e6 * count_all),
            name=name,
        )(span, *ghosts, *owns, radial_sorted, target_sorted, source_sorted, radial_out, *extra)

    ring_rows, flip_rows = [mixed], []
    held = mixed
    for k in range(n_ring):
        flip_rows.append(lax.ppermute(held, "tile", flip))
        if k < n_ring - 1:
            held = lax.ppermute(held, "tile", ring)
            if k == 0:
                held, radial = lax.optimization_barrier((held, radial))
                radial_sorted, target_sorted, source_sorted = place(radial)
            if k == 1:
                held, radial_sorted = lax.optimization_barrier((held, radial_sorted))
            ring_rows.append(held)
    owns = [rows for pair in zip(ring_rows, flip_rows) for rows in pair]
    ghosts_a = pick(owns[:half])
    part = main(0, [], owns[:half], [], [], "main_own")
    owns_b = owns[half:]
    ghosts_b = pick(owns_b)
    part = main(half, ghosts_a, owns_b, [part], [], "main_mid")
    return main(
        n_tile + half, ghosts_b, [], [part], [radial_sum, embedding, mix_weight], "main_end"
    )


def solution(mesh):
    both = ("dom", "tile")
    return jax.shard_map(
        body,
        mesh=mesh,
        in_specs=(
            P(both, None),
            P(both),
            P("dom", None),
            P(both),
            P(both),
            P(both, None),
            P(),
            P(),
            P(),
        ),
        out_specs=P(both, None),
        check_vma=False,
    )
```

```python
import functools
import jax
import jax.numpy as jnp
from jax import lax
from jax.experimental import pallas as pl
from jax.experimental.pallas import tpu as pltpu
from jax.sharding import PartitionSpec as P

C = 128
K = 9
ATOM_DEV = 256
GHOST = 128
TE = 128
BE = 256
CHUNK = 256
CHUNK_BITS = 8
WIDTH = K * C
EXTRA = 16
PER = 4
FINISH = 2
degree_of = (0, 1, 1, 1, 2, 2, 2, 2, 2)
inv_scale = 0.125

F32 = jnp.float32
BF16 = jnp.bfloat16
I32 = jnp.int32

PARAMS = pltpu.CompilerParams(vmem_limit_bytes=64 * 1024 * 1024)


def vmem():
    return pl.BlockSpec(memory_space=pltpu.VMEM)


def smem():
    return pl.BlockSpec(memory_space=pltpu.SMEM)


def cols(k):
    return slice(k * C, (k + 1) * C)


def iota(shape, dim):
    return lax.broadcasted_iota(I32, shape, dim)


def as_bf16(mask):
    return jnp.where(mask, 1.0, 0.0).astype(BF16)


def dot(a, b):
    return jnp.dot(a, b, preferred_element_type=F32)


def mix_kernel(x_ref, mix_ref, pick_ref, mixed_ref):
    for k in range(K):
        mixed = dot(x_ref[:, cols(k)], mix_ref[degree_of[k], :C])
        mixed_ref[cols(k), :] = mixed.T.astype(BF16)
    picks = jnp.broadcast_to(pick_ref[...].astype(F32), (EXTRA, ATOM_DEV))
    mixed_ref[WIDTH:, :] = picks.astype(BF16)


def pick_kernel(*refs, n):
    blocks, refs = refs[:n], refs[n:]
    near_hbm, far_hbm, inside, near, far, sems = refs
    even = (lax.axis_index("dom") & 1) == 0
    loads = [
        pltpu.make_async_copy(block, inside.at[i], sems.at[0, i]) for i, block in enumerate(blocks)
    ]
    saves = []
    for load in loads:
        load.start()
    for i in range(n):
        loads[i].wait()
        picks = inside[i, WIDTH:, :].astype(F32)[:1, :].astype(I32)
        down, up = picks[:, :GHOST], picks[:, GHOST:]
        row_id = iota((ATOM_DEV, GHOST), 0)
        chosen = jnp.concatenate(
            [
                as_bf16(row_id == jnp.where(even, up, down)),
                as_bf16(row_id == jnp.where(even, down, up)),
            ],
            axis=1,
        )
        rows = dot(inside[i, :WIDTH, :], chosen).astype(BF16)
        near[i] = rows[:, :GHOST]
        far[i] = rows[:, GHOST:]
        for side, (src, dst) in enumerate(((near, near_hbm), (far, far_hbm))):
            save = pltpu.make_async_copy(src.at[i], dst.at[i], sems.at[1 + side, i])
            save.start()
            saves.append(save)
    for save in saves:
        save.wait()


def live_tiles(count_ref):
    return count_ref[0, lax.axis_index("tile")]


def rank_kernel(count_ref, src_ref, pos_ref, span_ref, oh_ref, cum_ref, *, slots):
    tiles = src_ref.shape[0]
    nb = span_ref.shape[0] // 3
    count = live_tiles(count_ref)
    half, half_bits = nb // 4, (nb // 4).bit_length() - 1
    order = iota((nb, TE), 0)
    quarter = order >> half_bits
    index = order - half * ((quarter + 1) >> 1)
    tile_pos = lax.axis_index("tile")
    ring_pos = (tile_pos >> 1) - (index >> 1)
    ring_pos = jnp.where(ring_pos < 0, ring_pos + nb // 4, ring_pos)
    label = 2 * (2 * ring_pos + ((tile_pos & 1) ^ (index & 1))) + (quarter & 1)

    def mark(t, carry):
        bucket = src_ref[pl.ds(t, 1), :] >> CHUNK_BITS
        bucket = jnp.where(t < count, bucket, -1)
        oh_ref[pl.ds(pl.multiple_of(t * nb, nb), nb), :] = as_bf16(label == bucket)
        return carry

    lax.fori_loop(0, tiles, mark, 0, unroll=8)
    upto = as_bf16(iota((TE, TE), 0) <= iota((TE, TE), 1))
    both = jnp.concatenate([upto, jnp.ones((TE, TE), BF16)], axis=1)
    step = 256
    for r in range(0, tiles * nb, step):
        cum_ref[r : r + step, :] = dot(oh_ref[r : r + step, :], both)

    def add(t, total):
        return total + cum_ref[pl.ds(pl.multiple_of(t * nb, nb), nb), TE:]

    total = lax.fori_loop(0, tiles, add, jnp.zeros((nb, TE), F32), unroll=8)
    blocks = jnp.floor((total + (BE - 1)) * (1.0 / BE))
    below = as_bf16(iota((nb, nb), 1) < iota((nb, nb), 0))
    first = dot(below, blocks.astype(BF16))
    span_ref[:nb, :] = first.astype(I32)
    span_ref[nb : 2 * nb, :] = blocks.astype(I32)
    passed = jnp.where(iota((nb, TE), 1).astype(F32) >= first + blocks, 1.0, 0.0)
    chunk_of = jnp.minimum(jnp.sum(passed, axis=0, keepdims=True), nb - 1.0)
    span_ref[2 * nb :, :] = jnp.broadcast_to(chunk_of, (nb, TE)).astype(I32)

    def place(t, run):
        rows = pl.ds(pl.multiple_of(t * nb, nb), nb)
        oh = oh_ref[rows, :].astype(F32)
        value = oh * (cum_ref[rows, :TE] + run)
        place_of = jnp.sum(value, axis=0, keepdims=True).astype(I32)
        pos_ref[pl.ds(t, 1), :] = jnp.where(t < count, 2 * place_of, 2 * slots)
        return run + cum_ref[rows, TE:]

    lax.fori_loop(0, tiles, place, first * BE - 1.0, unroll=8)


def radial_kernel(count_ref, tgt_ref, feat_ref, rin_ref, rad_ref, rsum_ref):
    tiles = tgt_ref.shape[0]
    count = live_tiles(count_ref)
    rsum_ref[...] = jnp.zeros_like(rsum_ref)
    group = 8
    atom_id = iota((ATOM_DEV, TE), 0)

    def rows_of(i):
        return pl.ds(pl.multiple_of(i * (group * TE), group * TE), group * TE)

    def hidden_layer(i):
        hidden = 0.5 * dot(feat_ref[rows_of(i), :], rin_ref[...])
        rad_ref[rows_of(i), :] = (hidden + hidden * jnp.tanh(hidden)).astype(BF16)

    def add_up(i):
        land = []
        for q in range(group):
            t = i * group + q
            tgt = jnp.where(t < count, tgt_ref[pl.ds(t, 1), :], -1)
            land.append(as_bf16(atom_id == tgt))
        rsum_ref[...] += dot(jnp.concatenate(land, axis=1), rad_ref[rows_of(i), :])

    hidden_layer(0)
    groups = (count + group - 1) // group

    def step(i, carry):
        add_up(i)
        hidden_layer(i + 1)
        return carry

    lax.fori_loop(0, groups - 1, step, 0)
    add_up(groups - 1)


def place_kernel(
    count_ref,
    pos_ref,
    span_ref,
    src_ref,
    tgt_ref,
    rin_ref,
    rad_hbm,
    tgt_hbm,
    srcs_ref,
    pairs,
    even,
    odd,
    rad_out,
    tgt_out,
    sems,
):
    tiles = src_ref.shape[0]
    nb = span_ref.shape[0] // 3
    count = live_tiles(count_ref)
    flip = jnp.where((lax.axis_index("dom") & 1) == 0, GHOST, 0)
    blank = jnp.where((iota((2 * BE, C), 0) & 1) == 1, -1.0, 0.0)

    def clear(b, carry):
        blocks = span_ref[nb + b, 0]

        @pl.when(blocks > 0)
        def _():
            last = pl.multiple_of((span_ref[b, 0] + blocks - 1) * (2 * BE), 2 * BE)
            pairs[pl.ds(last, 2 * BE), :] = blank

        return carry

    lax.fori_loop(0, nb, clear, 0)
    eye = iota((TE, TE), 0) == iota((TE, TE), 1)
    spread = jnp.concatenate(
        [jnp.ones((TE, C), BF16), jnp.full((TE, C), float(CHUNK), BF16)], axis=0
    )

    def compute(t, out):
        t = jnp.minimum(t, tiles - 1)
        rows = pl.ds(pl.multiple_of(t * TE, TE), TE)
        out[pl.ds(0, TE, stride=2), :] = rin_ref[rows, :].astype(F32)
        src = src_ref[pl.ds(t, 1), :]
        src = (src & (CHUNK - 1)) ^ jnp.where((src & CHUNK) != 0, flip, 0)
        tgt = tgt_ref[pl.ds(t, 1), :]
        diag_s = jnp.where(eye, src.astype(F32), 0.0).astype(BF16)
        diag_t = jnp.where(eye, tgt.astype(F32), 0.0).astype(BF16)
        code = dot(jnp.concatenate([diag_s, diag_t], axis=1), spread)
        out[pl.ds(1, TE, stride=2), :] = code

    def scatter(t, data):
        for e in range(TE):
            pairs[pl.ds(pos_ref[t, e], 2), :] = data[2 * e : 2 * e + 2, :]

    compute(0, even)

    def step(i, carry):
        compute(2 * i + 1, odd)
        scatter(2 * i, even)
        compute(2 * i + 2, even)
        scatter(2 * i + 1, odd)
        return carry

    lax.fori_loop(0, (count + 1) // 2, step, 0)
    many = FINISH * BE

    def saves(j, slot):
        rows = pl.ds(pl.multiple_of(j * many, many), many)
        return (
            pltpu.make_async_copy(rad_out.at[slot], rad_hbm.at[rows, :], sems.at[0, slot]),
            pltpu.make_async_copy(tgt_out.at[slot], tgt_hbm.at[rows, :], sems.at[1, slot]),
        )

    def finish(j, carry):
        slot = j & 1

        @pl.when(j >= 2)
        def _():
            for save in saves(j - 2, slot):
                save.wait()

        base = pl.multiple_of(j * (2 * many), 2 * many)
        rad_out[slot] = pairs[pl.ds(base, many, stride=2), :].astype(BF16)
        code = pairs[pl.ds(base + 1, many, stride=2), :].astype(I32)
        tgt_out[slot] = (code >> CHUNK_BITS).astype(F32).astype(BF16)
        src = (code & (CHUNK - 1)).astype(F32)
        for h in range(many // TE):
            part = jnp.where(eye, src[h * TE : (h + 1) * TE, :], 0.0)
            row = pl.ds(j * (many // TE) + h, 1)
            srcs_ref[row, :] = jnp.sum(part, axis=0, keepdims=True).astype(I32)
        for save in saves(j, slot):
            save.start()
        return carry

    used = span_ref[nb - 1, 0] + span_ref[2 * nb - 1, 0]
    steps = (used + FINISH - 1) // FINISH
    lax.fori_loop(0, steps, finish, 0)
    for back in (2, 1):

        @pl.when(steps >= back)
        def _():
            for save in saves(steps - back, (steps - back) & 1):
                save.wait()


def main_kernel(*refs, low, n_ghost, n_own, first, final):
    span_ref, *refs = refs
    ghosts, refs = refs[: 2 * (n_ghost > 0)], refs[2 * (n_ghost > 0) :]
    owns, refs = refs[:n_own], refs[n_own:]
    rad_hbm, tgt_hbm, src_ref, rout_ref, *refs = refs
    if not first:
        part_ref, *refs = refs
    if final:
        rsum_ref, x_ref, mix_ref, *refs = refs
    out_ref, rbuf, tbuf, land_ref, message_ref, tables, sems, table_sems, *refs = refs
    acc_ref = refs[0] if final else out_ref
    count = n_ghost + n_own
    nb = span_ref.shape[0] // 3
    begin = span_ref[low, 0]
    end = span_ref[low + count - 1, 0] + span_ref[nb + low + count - 1, 0]
    groups = (end - begin + PER - 1) // PER

    loads = []
    for i, own in enumerate(owns):
        loads.append((own.at[:WIDTH, :], tables.at[n_ghost + i]))
    for i in range(n_ghost):
        for side in range(2):
            half = tables.at[i, :, side * GHOST : (side + 1) * GHOST]
            loads.append((ghosts[side].at[i], half))
    loads = [
        pltpu.make_async_copy(src, dst, table_sems.at[i]) for i, (src, dst) in enumerate(loads)
    ]
    for load in loads:
        load.start()

    def copies(p, slot):
        moves = []
        for h in range(PER):
            j = jnp.minimum(begin + PER * p + h, end - 1)
            rows = pl.ds(pl.multiple_of(j * BE, BE), BE)
            moves.append(
                pltpu.make_async_copy(rad_hbm.at[rows, :], rbuf.at[slot, h], sems.at[0, h, slot])
            )
            moves.append(
                pltpu.make_async_copy(tgt_hbm.at[rows, :], tbuf.at[slot, h], sems.at[1, h, slot])
            )
        return moves

    def fetch(p):
        @pl.when(p < groups)
        def _():
            for copy in copies(p, p & 1):
                copy.start()

    def arrive(p):
        @pl.when(p < groups)
        def _():
            for copy in copies(p, p & 1):
                copy.wait()

    fetch(0)
    if first:
        acc_ref[...] = jnp.zeros_like(acc_ref)
    else:
        acc_ref[...] = part_ref[...]
    rout_t = rout_ref[...].astype(F32).T.astype(BF16)
    atom_id = iota((BE, TE), 1).astype(F32)
    row_id = iota((CHUNK, TE), 0)

    def gather(p):
        for h in range(PER):
            j = begin + PER * p + h
            off = jnp.where(j < end, 0.0, 4096.0)
            j = jnp.maximum(jnp.minimum(j, end - 1), 0)
            c = jnp.clip(span_ref[2 * nb, j] - low, 0, count - 1)
            gate = lax.dot_general(
                rout_t, rbuf[p & 1, h], (((1,), (1,)), ((), ())), preferred_element_type=F32
            )
            pick = jnp.concatenate(
                [
                    as_bf16(row_id == src_ref[pl.ds(j * (BE // TE) + q, 1), :])
                    for q in range(BE // TE)
                ],
                axis=1,
            )
            rows = dot(tables[c], pick)
            for k in range(K):
                message = rows[cols(k), :] * gate[cols(degree_of[k]), :]
                message_ref[cols(k), h * BE : (h + 1) * BE] = message.astype(BF16)
            tgt = tbuf[p & 1, h].astype(F32) + off
            for q in range(ATOM_DEV // TE):
                land_ref[h * BE : (h + 1) * BE, q * TE : (q + 1) * TE] = as_bf16(
                    tgt == atom_id + float(q * TE)
                )

    def add_up():
        acc_ref[...] += dot(message_ref[...], land_ref[...])

    for load in loads:
        load.wait()
    arrive(0)
    fetch(1)
    gather(0)

    def step(p, carry):
        arrive(p + 1)
        fetch(p + 2)
        add_up()
        gather(p + 1)
        return carry

    lax.fori_loop(0, groups - 1, step, 0)

    @pl.when(groups > 0)
    def _():
        add_up()

    if not final:
        return
    gate_sum = jnp.dot(
        rsum_ref[...],
        rout_ref[...].astype(F32),
        preferred_element_type=F32,
        precision=lax.Precision.HIGHEST,
    )
    for k in range(K):
        own = dot(x_ref[:, cols(k)], mix_ref[degree_of[k], C:])
        full = acc_ref[cols(k), :].T + own * gate_sum[:, cols(degree_of[k])]
        out_ref[:, cols(k)] = (inv_scale * full).astype(BF16)


def shape(dims, kind):
    return jax.ShapeDtypeStruct(dims, kind)


def cost(flops, size):
    return pl.CostEstimate(flops=int(flops), bytes_accessed=int(size), transcendentals=0)


def body(
    embedding,
    ghost_index,
    tile_count,
    edge_source,
    edge_target,
    edge_features,
    radial_in,
    radial_out,
    mix_weight,
):
    n_dom, n_tile = lax.axis_size("dom"), lax.axis_size("tile")
    tiles = edge_source.shape[0] // TE
    nb = 2 * n_tile
    slots = (tiles * TE // BE + nb) * BE
    count = tile_count
    source = edge_source.reshape(tiles, TE)
    target = edge_target.reshape(tiles, TE)
    hbm = pl.BlockSpec(memory_space=pl.ANY)

    mixed = pl.pallas_call(
        mix_kernel,
        out_shape=shape((WIDTH + EXTRA, ATOM_DEV), BF16),
        in_specs=[vmem(), vmem(), vmem()],
        out_specs=vmem(),
        compiler_params=PARAMS,
        cost_estimate=cost(256 * 256 * 1152, 2e6),
        name="mix",
    )(embedding, mix_weight, ghost_index.reshape(1, ATOM_DEV))
    ring = [(t, (t + 2) % n_tile) for t in range(n_tile)]
    flip = [(t, t ^ 1) for t in range(n_tile)]
    near = [(i, i ^ 1) for i in range(n_dom)]
    far = [(i, i + 1) for i in range(1, n_dom - 1, 2)]
    far += [(j, i) for i, j in far]
    n_ring = n_tile // 2
    half = n_tile // 2

    pos, span = pl.pallas_call(
        functools.partial(rank_kernel, slots=slots),
        out_shape=(shape((tiles, TE), I32), shape((3 * nb, TE), I32)),
        in_specs=[smem(), vmem()],
        out_specs=(vmem(), vmem()),
        scratch_shapes=[
            pltpu.VMEM((tiles * nb, TE), BF16),
            pltpu.VMEM((tiles * nb, 2 * TE), F32),
        ],
        compiler_params=PARAMS,
        cost_estimate=cost(4e9, 1e6),
        name="rank",
    )(count, source)
    radial, radial_sum = pl.pallas_call(
        radial_kernel,
        out_shape=(shape((tiles * TE, C), BF16), shape((ATOM_DEV, C), F32)),
        in_specs=[smem(), vmem(), vmem(), vmem()],
        out_specs=(vmem(), vmem()),
        compiler_params=PARAMS,
        cost_estimate=cost(10e9, 6e6),
        name="radial",
    )(count, target, edge_features, radial_in)

    def place(radial):
        return pl.pallas_call(
            place_kernel,
            out_shape=(
                shape((slots, C), BF16),
                shape((slots, C), BF16),
                shape((slots // TE, TE), I32),
            ),
            in_specs=[smem(), smem(), smem(), vmem(), vmem(), vmem()],
            out_specs=(hbm, hbm, vmem()),
            scratch_shapes=[
                pltpu.VMEM((2 * slots + 8, C), F32),
                pltpu.VMEM((2 * TE, C), F32),
                pltpu.VMEM((2 * TE, C), F32),
                pltpu.VMEM((2, FINISH * BE, C), BF16),
                pltpu.VMEM((2, FINISH * BE, C), BF16),
                pltpu.SemaphoreType.DMA((2, 2)),
            ],
            compiler_params=PARAMS,
            cost_estimate=cost(20e9, 12e6),
            name="place",
        )(count, pos, span, source, target, radial)

    def pick(blocks):
        n = len(blocks)
        near_rows, far_rows = pl.pallas_call(
            functools.partial(pick_kernel, n=n),
            out_shape=(shape((n, WIDTH, GHOST), BF16),) * 2,
            in_specs=[hbm] * n,
            out_specs=(hbm, hbm),
            scratch_shapes=[
                pltpu.VMEM((n, WIDTH + EXTRA, ATOM_DEV), BF16),
                pltpu.VMEM((n, WIDTH, GHOST), BF16),
                pltpu.VMEM((n, WIDTH, GHOST), BF16),
                pltpu.SemaphoreType.DMA((3, n)),
            ],
            compiler_params=PARAMS,
            cost_estimate=cost(3e9, 5e6),
            name="pick",
        )(*blocks)
        return [lax.ppermute(near_rows, "dom", near), lax.ppermute(far_rows, "dom", far)]

    def main(low, ghosts, owns, part, final_args, name):
        final = len(final_args) > 0
        dims, kind = ((ATOM_DEV, WIDTH), BF16) if final else ((WIDTH, ATOM_DEV), F32)
        n_ghost = half if ghosts else 0
        count_all = n_ghost + len(owns)
        extra = [*part, *final_args]
        return pl.pallas_call(
            functools.partial(
                main_kernel,
                low=low,
                n_ghost=n_ghost,
                n_own=len(owns),
                first=not part,
                final=final,
            ),
            out_shape=shape(dims, kind),
            in_specs=[smem()]
            + [hbm] * (len(ghosts) + len(owns) + 2)
            + [vmem()] * (2 + len(extra)),
            out_specs=vmem(),
            scratch_shapes=[
                pltpu.VMEM((2, PER, BE, C), BF16),
                pltpu.VMEM((2, PER, BE, C), BF16),
                pltpu.VMEM((PER * BE, ATOM_DEV), BF16),
                pltpu.VMEM((WIDTH, PER * BE), BF16),
                pltpu.VMEM((count_all, WIDTH, ATOM_DEV), BF16),
                pltpu.SemaphoreType.DMA((2, PER, 2)),
                pltpu.SemaphoreType.DMA((2 * n_ghost + len(owns),)),
            ]
            + ([pltpu.VMEM((WIDTH, ATOM_DEV), F32)] if final else []),
            compiler_params=PARAMS,
            cost_estimate=cost(3e9 * count_all, 2e6 * count_all),
            name=name,
        )(span, *ghosts, *owns, radial_sorted, target_sorted, source_sorted, radial_out, *extra)

    ring_rows, flip_rows = [mixed], []
    held = mixed
    for k in range(n_ring):
        flip_rows.append(lax.ppermute(held, "tile", flip))
        if k < n_ring - 1:
            held = lax.ppermute(held, "tile", ring)
            if k == 0:
                held, radial = lax.optimization_barrier((held, radial))
                radial_sorted, target_sorted, source_sorted = place(radial)
            if k == 1:
                held, radial_sorted = lax.optimization_barrier((held, radial_sorted))
            ring_rows.append(held)
    owns = [rows for pair in zip(ring_rows, flip_rows) for rows in pair]
    ghosts_a = pick(owns[:half])
    part = main(0, [], owns[:half], [], [], "main_own")
    owns_b = owns[half:]
    ghosts_b = pick(owns_b)
    part = main(half, ghosts_a, owns_b, [part], [], "main_mid")
    return main(
        n_tile + half, ghosts_b, [], [part], [radial_sum, embedding, mix_weight], "main_end"
    )


def solution(mesh):
    both = ("dom", "tile")
    return jax.shard_map(
        body,
        mesh=mesh,
        in_specs=(
            P(both, None),
            P(both),
            P("dom", None),
            P(both),
            P(both),
            P(both, None),
            P(),
            P(),
            P(),
        ),
        out_specs=P(both, None),
        check_vma=False,
    )
```

```python
import functools
import jax
import jax.numpy as jnp
from jax import lax
from jax.experimental import pallas as pl
from jax.experimental.pallas import tpu as pltpu
from jax.sharding import PartitionSpec as P

C = 128
K = 9
ATOM_DEV = 256
GHOST = 128
TE = 128
BE = 256
CHUNK = 256
CHUNK_BITS = 8
WIDTH = K * C
EXTRA = 16
PER = 4
degree_of = (0, 1, 1, 1, 2, 2, 2, 2, 2)
inv_scale = 0.125

F32 = jnp.float32
BF16 = jnp.bfloat16
I32 = jnp.int32

PARAMS = pltpu.CompilerParams(vmem_limit_bytes=64 * 1024 * 1024)


def vmem():
    return pl.BlockSpec(memory_space=pltpu.VMEM)


def smem():
    return pl.BlockSpec(memory_space=pltpu.SMEM)


def cols(k):
    return slice(k * C, (k + 1) * C)


def iota(shape, dim):
    return lax.broadcasted_iota(I32, shape, dim)


def as_bf16(mask):
    return jnp.where(mask, 1.0, 0.0).astype(BF16)


def dot(a, b):
    return jnp.dot(a, b, preferred_element_type=F32)


def mix_kernel(x_ref, mix_ref, pick_ref, mixed_ref):
    for k in range(K):
        mixed = dot(x_ref[:, cols(k)], mix_ref[degree_of[k], :C])
        mixed_ref[cols(k), :] = mixed.T.astype(BF16)
    picks = jnp.broadcast_to(pick_ref[...].astype(F32), (EXTRA, ATOM_DEV))
    mixed_ref[WIDTH:, :] = picks.astype(BF16)


def pick_kernel(*refs, n):
    blocks, refs = refs[:n], refs[n:]
    near_hbm, far_hbm, inside, near, far, sems = refs
    even = (lax.axis_index("dom") & 1) == 0
    loads = [
        pltpu.make_async_copy(block, inside.at[i], sems.at[0, i]) for i, block in enumerate(blocks)
    ]
    saves = []
    for load in loads:
        load.start()
    for i in range(n):
        loads[i].wait()
        picks = inside[i, WIDTH:, :].astype(F32)[:1, :].astype(I32)
        down, up = picks[:, :GHOST], picks[:, GHOST:]
        row_id = iota((ATOM_DEV, GHOST), 0)
        chosen = jnp.concatenate(
            [
                as_bf16(row_id == jnp.where(even, up, down)),
                as_bf16(row_id == jnp.where(even, down, up)),
            ],
            axis=1,
        )
        rows = dot(inside[i, :WIDTH, :], chosen).astype(BF16)
        near[i] = rows[:, :GHOST]
        far[i] = rows[:, GHOST:]
        for side, (src, dst) in enumerate(((near, near_hbm), (far, far_hbm))):
            save = pltpu.make_async_copy(src.at[i], dst.at[i], sems.at[1 + side, i])
            save.start()
            saves.append(save)
    for save in saves:
        save.wait()


def live_tiles(count_ref):
    return count_ref[0, lax.axis_index("tile")]


def rank_kernel(count_ref, src_ref, pos_ref, span_ref, oh_ref, cum_ref, *, slots):
    tiles = src_ref.shape[0]
    nb = span_ref.shape[0] // 3
    count = live_tiles(count_ref)
    owns, half = nb // 2, nb // 4
    order = iota((nb, TE), 0)
    ghost = ((order >= owns - 1) & (order < owns - 1 + half)) | (order >= owns + half)
    index = jnp.where(order >= owns - 1, order - (owns - 1), order)
    index = jnp.where(order == owns - 1 + half, owns - 1, index)
    index = jnp.where(order >= owns + half, order - owns, index)
    tile_pos = lax.axis_index("tile")
    ring_pos = (tile_pos >> 1) - (index >> 1)
    ring_pos = jnp.where(ring_pos < 0, ring_pos + half, ring_pos)
    label = 2 * (2 * ring_pos + ((tile_pos & 1) ^ (index & 1))) + jnp.where(ghost, 1, 0)

    def mark(t, carry):
        bucket = src_ref[pl.ds(t, 1), :] >> CHUNK_BITS
        bucket = jnp.where(t < count, bucket, -1)
        oh_ref[pl.ds(pl.multiple_of(t * nb, nb), nb), :] = as_bf16(label == bucket)
        return carry

    lax.fori_loop(0, tiles, mark, 0, unroll=8)
    upto = as_bf16(iota((TE, TE), 0) <= iota((TE, TE), 1))
    both = jnp.concatenate([upto, jnp.ones((TE, TE), BF16)], axis=1)
    step = 256
    for r in range(0, tiles * nb, step):
        cum_ref[r : r + step, :] = dot(oh_ref[r : r + step, :], both)

    def add(t, total):
        return total + cum_ref[pl.ds(pl.multiple_of(t * nb, nb), nb), TE:]

    total = lax.fori_loop(0, tiles, add, jnp.zeros((nb, TE), F32), unroll=8)
    blocks = jnp.floor((total + (BE - 1)) * (1.0 / BE))
    below = as_bf16(iota((nb, nb), 1) < iota((nb, nb), 0))
    first = dot(below, blocks.astype(BF16))
    span_ref[:nb, :] = first.astype(I32)
    span_ref[nb : 2 * nb, :] = blocks.astype(I32)
    passed = jnp.where(iota((nb, TE), 1).astype(F32) >= first + blocks, 1.0, 0.0)
    chunk_of = jnp.minimum(jnp.sum(passed, axis=0, keepdims=True), nb - 1.0)
    span_ref[2 * nb :, :] = jnp.broadcast_to(chunk_of, (nb, TE)).astype(I32)

    def place(t, run):
        rows = pl.ds(pl.multiple_of(t * nb, nb), nb)
        oh = oh_ref[rows, :].astype(F32)
        value = oh * (cum_ref[rows, :TE] + run)
        place_of = jnp.sum(value, axis=0, keepdims=True).astype(I32)
        pos_ref[pl.ds(t, 1), :] = jnp.where(t < count, 2 * place_of, 2 * slots)
        return run + cum_ref[rows, TE:]

    lax.fori_loop(0, tiles, place, first * BE - 1.0, unroll=8)


def radial_kernel(count_ref, tgt_ref, feat_ref, rin_ref, rad_ref, rsum_ref):
    tiles = tgt_ref.shape[0]
    count = live_tiles(count_ref)
    rsum_ref[...] = jnp.zeros_like(rsum_ref)
    group = 8
    atom_id = iota((ATOM_DEV, TE), 0)

    def rows_of(i):
        return pl.ds(pl.multiple_of(i * (group * TE), group * TE), group * TE)

    def hidden_layer(i):
        hidden = 0.5 * dot(feat_ref[rows_of(i), :], rin_ref[...])
        rad_ref[rows_of(i), :] = (hidden + hidden * jnp.tanh(hidden)).astype(BF16)

    def add_up(i):
        land = []
        for q in range(group):
            t = i * group + q
            tgt = jnp.where(t < count, tgt_ref[pl.ds(t, 1), :], -1)
            land.append(as_bf16(atom_id == tgt))
        rsum_ref[...] += dot(jnp.concatenate(land, axis=1), rad_ref[rows_of(i), :])

    hidden_layer(0)
    groups = (count + group - 1) // group

    def step(i, carry):
        add_up(i)
        hidden_layer(i + 1)
        return carry

    lax.fori_loop(0, groups - 1, step, 0)
    add_up(groups - 1)


def place_kernel(
    count_ref,
    pos_ref,
    span_ref,
    src_ref,
    tgt_ref,
    rin_ref,
    rad_hbm,
    tgt_hbm,
    srcs_ref,
    pairs,
    even,
    odd,
    rad_out,
    tgt_out,
    sems,
):
    tiles = src_ref.shape[0]
    nb = span_ref.shape[0] // 3
    count = live_tiles(count_ref)
    flip = jnp.where((lax.axis_index("dom") & 1) == 0, GHOST, 0)
    blank = jnp.where((iota((2 * BE, C), 0) & 1) == 1, -1.0, 0.0)

    def clear(b, carry):
        blocks = span_ref[nb + b, 0]

        @pl.when(blocks > 0)
        def _():
            last = pl.multiple_of((span_ref[b, 0] + blocks - 1) * (2 * BE), 2 * BE)
            pairs[pl.ds(last, 2 * BE), :] = blank

        return carry

    lax.fori_loop(0, nb, clear, 0)
    eye = iota((TE, TE), 0) == iota((TE, TE), 1)
    spread = jnp.concatenate(
        [jnp.ones((TE, C), BF16), jnp.full((TE, C), float(CHUNK), BF16)], axis=0
    )

    def compute(t, out):
        t = jnp.minimum(t, tiles - 1)
        rows = pl.ds(pl.multiple_of(t * TE, TE), TE)
        out[pl.ds(0, TE, stride=2), :] = rin_ref[rows, :].astype(F32)
        src = src_ref[pl.ds(t, 1), :]
        src = (src & (CHUNK - 1)) ^ jnp.where((src & CHUNK) != 0, flip, 0)
        tgt = tgt_ref[pl.ds(t, 1), :]
        diag_s = jnp.where(eye, src.astype(F32), 0.0).astype(BF16)
        diag_t = jnp.where(eye, tgt.astype(F32), 0.0).astype(BF16)
        code = dot(jnp.concatenate([diag_s, diag_t], axis=1), spread)
        out[pl.ds(1, TE, stride=2), :] = code

    def scatter(t, data):
        for e in range(TE):
            pairs[pl.ds(pos_ref[t, e], 2), :] = data[2 * e : 2 * e + 2, :]

    compute(0, even)

    def step(i, carry):
        compute(2 * i + 1, odd)
        scatter(2 * i, even)
        compute(2 * i + 2, even)
        scatter(2 * i + 1, odd)
        return carry

    lax.fori_loop(0, (count + 1) // 2, step, 0)

    def saves(j):
        rows = pl.ds(pl.multiple_of(j * BE, BE), BE)
        return (
            pltpu.make_async_copy(rad_out.at[rows, :], rad_hbm.at[rows, :], sems.at[0, j]),
            pltpu.make_async_copy(tgt_out.at[rows, :], tgt_hbm.at[rows, :], sems.at[1, j]),
        )

    def finish(j, carry):
        for h in range(BE // TE):
            row = j * (BE // TE) + h
            rows = pl.ds(pl.multiple_of(row * TE, TE), TE)
            base = pl.multiple_of(row * (2 * TE), 2 * TE)
            rad_out[rows, :] = pairs[pl.ds(base, TE, stride=2), :].astype(BF16)
            code = pairs[pl.ds(base + 1, TE, stride=2), :]
            tgt = jnp.floor(code * (1.0 / CHUNK))
            tgt_out[rows, :] = tgt.astype(BF16)
            src = jnp.where(eye, code - CHUNK * tgt, 0.0)
            srcs_ref[pl.ds(row, 1), :] = jnp.sum(src, axis=0, keepdims=True).astype(I32)
        for save in saves(j):
            save.start()
        return carry

    used = span_ref[nb - 1, 0] + span_ref[2 * nb - 1, 0]
    lax.fori_loop(0, used, finish, 0)

    def drain(j, carry):
        for save in saves(j):
            save.wait()
        return carry

    lax.fori_loop(0, used, drain, 0)


def main_kernel(*refs, low, n_ghost, n_own, first, final):
    span_ref, *refs = refs
    ghosts, refs = refs[: 2 * (n_ghost > 0)], refs[2 * (n_ghost > 0) :]
    owns, refs = refs[:n_own], refs[n_own:]
    rad_hbm, tgt_hbm, src_ref, rout_ref, *refs = refs
    if not first:
        part_ref, *refs = refs
    if final:
        rsum_ref, x_ref, mix_ref, *refs = refs
    out_ref, rbuf, tbuf, land_ref, message_ref, tables, sems, table_sems, *refs = refs
    acc_ref = refs[0] if final else out_ref
    count = n_ghost + n_own
    nb = span_ref.shape[0] // 3
    begin = span_ref[low, 0]
    end = span_ref[low + count - 1, 0] + span_ref[nb + low + count - 1, 0]
    groups = (end - begin + PER - 1) // PER

    loads = []
    for i, own in enumerate(owns):
        loads.append((own.at[:WIDTH, :], tables.at[n_ghost + i]))
    for i in range(n_ghost):
        for side in range(2):
            half = tables.at[i, :, side * GHOST : (side + 1) * GHOST]
            loads.append((ghosts[side].at[i], half))
    loads = [
        pltpu.make_async_copy(src, dst, table_sems.at[i]) for i, (src, dst) in enumerate(loads)
    ]
    for load in loads:
        load.start()

    def copies(p, slot):
        moves = []
        for h in range(PER):
            j = jnp.minimum(begin + PER * p + h, end - 1)
            rows = pl.ds(pl.multiple_of(j * BE, BE), BE)
            moves.append(
                pltpu.make_async_copy(rad_hbm.at[rows, :], rbuf.at[slot, h], sems.at[0, h, slot])
            )
            moves.append(
                pltpu.make_async_copy(tgt_hbm.at[rows, :], tbuf.at[slot, h], sems.at[1, h, slot])
            )
        return moves

    def fetch(p):
        @pl.when(p < groups)
        def _():
            for copy in copies(p, p & 1):
                copy.start()

    def arrive(p):
        @pl.when(p < groups)
        def _():
            for copy in copies(p, p & 1):
                copy.wait()

    fetch(0)
    if first:
        acc_ref[...] = jnp.zeros_like(acc_ref)
    else:
        acc_ref[...] = part_ref[...]
    rout_t = rout_ref[...].astype(F32).T.astype(BF16)
    atom_id = iota((BE, TE), 1).astype(F32)
    row_id = iota((CHUNK, TE), 0)

    def gather(p):
        for h in range(PER):
            j = begin + PER * p + h
            off = jnp.where(j < end, 0.0, 4096.0)
            j = jnp.maximum(jnp.minimum(j, end - 1), 0)
            c = jnp.clip(span_ref[2 * nb, j] - low, 0, count - 1)
            gate = lax.dot_general(
                rout_t, rbuf[p & 1, h], (((1,), (1,)), ((), ())), preferred_element_type=F32
            )
            pick = jnp.concatenate(
                [
                    as_bf16(row_id == src_ref[pl.ds(j * (BE // TE) + q, 1), :])
                    for q in range(BE // TE)
                ],
                axis=1,
            )
            rows = dot(tables[c], pick)
            for k in range(K):
                message = rows[cols(k), :] * gate[cols(degree_of[k]), :]
                message_ref[cols(k), h * BE : (h + 1) * BE] = message.astype(BF16)
            tgt = tbuf[p & 1, h].astype(F32) + off
            for q in range(ATOM_DEV // TE):
                land_ref[h * BE : (h + 1) * BE, q * TE : (q + 1) * TE] = as_bf16(
                    tgt == atom_id + float(q * TE)
                )

    def add_up():
        acc_ref[...] += dot(message_ref[...], land_ref[...])

    for load in loads:
        load.wait()
    arrive(0)
    fetch(1)
    gather(0)

    def step(p, carry):
        arrive(p + 1)
        fetch(p + 2)
        add_up()
        gather(p + 1)
        return carry

    lax.fori_loop(0, groups - 1, step, 0)

    @pl.when(groups > 0)
    def _():
        add_up()

    if not final:
        return
    gate_sum = jnp.dot(
        rsum_ref[...],
        rout_ref[...].astype(F32),
        preferred_element_type=F32,
        precision=lax.Precision.HIGHEST,
    )
    for k in range(K):
        own = dot(x_ref[:, cols(k)], mix_ref[degree_of[k], C:])
        full = acc_ref[cols(k), :].T + own * gate_sum[:, cols(degree_of[k])]
        out_ref[:, cols(k)] = (inv_scale * full).astype(BF16)


def shape(dims, kind):
    return jax.ShapeDtypeStruct(dims, kind)


def cost(flops, size):
    return pl.CostEstimate(flops=int(flops), bytes_accessed=int(size), transcendentals=0)


def body(
    embedding,
    ghost_index,
    tile_count,
    edge_source,
    edge_target,
    edge_features,
    radial_in,
    radial_out,
    mix_weight,
):
    n_dom, n_tile = lax.axis_size("dom"), lax.axis_size("tile")
    tiles = edge_source.shape[0] // TE
    nb = 2 * n_tile
    slots = (tiles * TE // BE + nb) * BE
    count = tile_count
    source = edge_source.reshape(tiles, TE)
    target = edge_target.reshape(tiles, TE)
    hbm = pl.BlockSpec(memory_space=pl.ANY)

    mixed = pl.pallas_call(
        mix_kernel,
        out_shape=shape((WIDTH + EXTRA, ATOM_DEV), BF16),
        in_specs=[vmem(), vmem(), vmem()],
        out_specs=vmem(),
        compiler_params=PARAMS,
        cost_estimate=cost(256 * 256 * 1152, 2e6),
        name="mix",
    )(embedding, mix_weight, ghost_index.reshape(1, ATOM_DEV))
    ring = [(t, (t + 2) % n_tile) for t in range(n_tile)]
    flip = [(t, t ^ 1) for t in range(n_tile)]
    near = [(i, i ^ 1) for i in range(n_dom)]
    far = [(i, i + 1) for i in range(1, n_dom - 1, 2)]
    far += [(j, i) for i, j in far]
    n_ring = n_tile // 2
    half = n_tile // 2

    pos, span = pl.pallas_call(
        functools.partial(rank_kernel, slots=slots),
        out_shape=(shape((tiles, TE), I32), shape((3 * nb, TE), I32)),
        in_specs=[smem(), vmem()],
        out_specs=(vmem(), vmem()),
        scratch_shapes=[
            pltpu.VMEM((tiles * nb, TE), BF16),
            pltpu.VMEM((tiles * nb, 2 * TE), F32),
        ],
        compiler_params=PARAMS,
        cost_estimate=cost(4e9, 1e6),
        name="rank",
    )(count, source)
    radial, radial_sum = pl.pallas_call(
        radial_kernel,
        out_shape=(shape((tiles * TE, C), BF16), shape((ATOM_DEV, C), F32)),
        in_specs=[smem(), vmem(), vmem(), vmem()],
        out_specs=(vmem(), vmem()),
        compiler_params=PARAMS,
        cost_estimate=cost(10e9, 6e6),
        name="radial",
    )(count, target, edge_features, radial_in)

    def place(radial):
        return pl.pallas_call(
            place_kernel,
            out_shape=(
                shape((slots, C), BF16),
                shape((slots, C), BF16),
                shape((slots // TE, TE), I32),
            ),
            in_specs=[smem(), smem(), smem(), vmem(), vmem(), vmem()],
            out_specs=(hbm, hbm, vmem()),
            scratch_shapes=[
                pltpu.VMEM((2 * slots + 8, C), F32),
                pltpu.VMEM((2 * TE, C), F32),
                pltpu.VMEM((2 * TE, C), F32),
                pltpu.VMEM((slots, C), BF16),
                pltpu.VMEM((slots, C), BF16),
                pltpu.SemaphoreType.DMA((2, slots // BE)),
            ],
            compiler_params=PARAMS,
            cost_estimate=cost(20e9, 12e6),
            name="place",
        )(count, pos, span, source, target, radial)

    def pick(blocks):
        n = len(blocks)
        near_rows, far_rows = pl.pallas_call(
            functools.partial(pick_kernel, n=n),
            out_shape=(shape((n, WIDTH, GHOST), BF16),) * 2,
            in_specs=[hbm] * n,
            out_specs=(hbm, hbm),
            scratch_shapes=[
                pltpu.VMEM((n, WIDTH + EXTRA, ATOM_DEV), BF16),
                pltpu.VMEM((n, WIDTH, GHOST), BF16),
                pltpu.VMEM((n, WIDTH, GHOST), BF16),
                pltpu.SemaphoreType.DMA((3, n)),
            ],
            compiler_params=PARAMS,
            cost_estimate=cost(2e8, 4e5),
            name="pick",
        )(*blocks)
        return near_rows, far_rows

    def main(low, ghosts, owns, part, final_args, name):
        final = len(final_args) > 0
        dims, kind = ((ATOM_DEV, WIDTH), BF16) if final else ((WIDTH, ATOM_DEV), F32)
        n_ghost = half if ghosts else 0
        count_all = n_ghost + len(owns)
        extra = [*part, *final_args]
        return pl.pallas_call(
            functools.partial(
                main_kernel,
                low=low,
                n_ghost=n_ghost,
                n_own=len(owns),
                first=not part,
                final=final,
            ),
            out_shape=shape(dims, kind),
            in_specs=[smem()]
            + [hbm] * (len(ghosts) + len(owns) + 2)
            + [vmem()] * (2 + len(extra)),
            out_specs=vmem(),
            scratch_shapes=[
                pltpu.VMEM((2, PER, BE, C), BF16),
                pltpu.VMEM((2, PER, BE, C), BF16),
                pltpu.VMEM((PER * BE, ATOM_DEV), BF16),
                pltpu.VMEM((WIDTH, PER * BE), BF16),
                pltpu.VMEM((count_all, WIDTH, ATOM_DEV), BF16),
                pltpu.SemaphoreType.DMA((2, PER, 2)),
                pltpu.SemaphoreType.DMA((2 * n_ghost + len(owns),)),
            ]
            + ([pltpu.VMEM((WIDTH, ATOM_DEV), F32)] if final else []),
            compiler_params=PARAMS,
            cost_estimate=cost(1e8 * count_all, 1e5 * count_all),
            name=name,
        )(span, *ghosts, *owns, radial_sorted, target_sorted, source_sorted, radial_out, *extra)

    together = lax.optimization_barrier
    ring_rows, flip_rows = [mixed], []
    held = mixed
    part = None
    for k in range(n_ring):
        if k == n_ring - 1:
            early = [rows for pair in zip(ring_rows, flip_rows) for rows in pair]
            early.append(ring_rows[half // 2])
            part = main(0, [], early[: half + 1], [], [], "main_one")
            held, part = together((held, part))
            ring_rows[-1] = held
        flip_rows.append(lax.ppermute(held, "tile", flip))
        if k < n_ring - 1:
            held = lax.ppermute(held, "tile", ring)
            if k == 0:
                held, radial = together((held, radial))
                radial_sorted, target_sorted, source_sorted = place(radial)
            if k == 1:
                held, radial_sorted = together((held, radial_sorted))
            ring_rows.append(held)
    owns = [rows for pair in zip(ring_rows, flip_rows) for rows in pair]

    def pick_after(blocks, part):
        first, part = together((blocks[0], part))
        near_rows, far_rows = pick([first, *blocks[1:]])
        near_rows, part = together((near_rows, part))
        return [lax.ppermute(near_rows, "dom", near), lax.ppermute(far_rows, "dom", far)], part

    ghosts_a, part = pick_after(owns[:half], part)
    part = main(half + 1, [], owns[half + 1 : -1], [part], [], "main_two")
    ghosts_b, part = pick_after(owns[half:], part)
    part = main(n_tile - 1, ghosts_a, owns[-1:], [part], [], "main_three")
    return main(
        n_tile + half, ghosts_b, [], [part], [radial_sum, embedding, mix_weight], "main_four"
    )


def solution(mesh):
    both = ("dom", "tile")
    return jax.shard_map(
        body,
        mesh=mesh,
        in_specs=(
            P(both, None),
            P(both),
            P("dom", None),
            P(both),
            P(both),
            P(both, None),
            P(),
            P(),
            P(),
        ),
        out_specs=P(both, None),
        check_vma=False,
    )
```

```python
import functools
import jax
import jax.numpy as jnp
from jax import lax
from jax.experimental import pallas as pl
from jax.experimental.pallas import tpu as pltpu
from jax.sharding import PartitionSpec as P

C = 128
K = 9
ATOM_DEV = 256
GHOST = 128
TE = 128
BE = 256
CHUNK = 256
CHUNK_BITS = 8
WIDTH = K * C
EXTRA = 16
PER = 4
degree_of = (0, 1, 1, 1, 2, 2, 2, 2, 2)
inv_scale = 0.125

F32 = jnp.float32
BF16 = jnp.bfloat16
I32 = jnp.int32

PARAMS = pltpu.CompilerParams(vmem_limit_bytes=64 * 1024 * 1024)


def vmem():
    return pl.BlockSpec(memory_space=pltpu.VMEM)


def smem():
    return pl.BlockSpec(memory_space=pltpu.SMEM)


def cols(k):
    return slice(k * C, (k + 1) * C)


def iota(shape, dim):
    return lax.broadcasted_iota(I32, shape, dim)


def as_bf16(mask):
    return jnp.where(mask, 1.0, 0.0).astype(BF16)


def dot(a, b):
    return jnp.dot(a, b, preferred_element_type=F32)


def mix_kernel(x_ref, mix_ref, pick_ref, mixed_ref):
    for k in range(K):
        mixed = dot(x_ref[:, cols(k)], mix_ref[degree_of[k], :C])
        mixed_ref[cols(k), :] = mixed.T.astype(BF16)
    picks = jnp.broadcast_to(pick_ref[...].astype(F32), (EXTRA, ATOM_DEV))
    mixed_ref[WIDTH:, :] = picks.astype(BF16)


def pick_kernel(*refs, n):
    blocks, refs = refs[:n], refs[n:]
    near_hbm, far_hbm, inside, near, far, sems = refs
    even = (lax.axis_index("dom") & 1) == 0
    loads = [
        pltpu.make_async_copy(block, inside.at[i], sems.at[0, i]) for i, block in enumerate(blocks)
    ]
    saves = []
    for load in loads:
        load.start()
    for load in loads:
        load.wait()
    for i in range(n):
        picks = inside[i, WIDTH:, :].astype(F32)[:1, :].astype(I32)
        down, up = picks[:, :GHOST], picks[:, GHOST:]
        row_id = iota((ATOM_DEV, GHOST), 0)
        chosen = jnp.concatenate(
            [
                as_bf16(row_id == jnp.where(even, up, down)),
                as_bf16(row_id == jnp.where(even, down, up)),
            ],
            axis=1,
        )
        rows = dot(inside[i, :WIDTH, :], chosen).astype(BF16)
        near[i] = rows[:, :GHOST]
        far[i] = rows[:, GHOST:]
    for i in range(n):
        for side, (src, dst) in enumerate(((near, near_hbm), (far, far_hbm))):
            save = pltpu.make_async_copy(src.at[i], dst.at[i], sems.at[1 + side, i])
            save.start()
            saves.append(save)
    for save in saves:
        save.wait()


def base_kernel(rsum_ref, rout_ref, x_ref, mix_ref, base_ref, rout_t_ref):
    rout = rout_ref[...].astype(F32)
    rout_t_ref[...] = rout.T.astype(BF16)
    gate_sum = jnp.dot(
        rsum_ref[...], rout, preferred_element_type=F32, precision=lax.Precision.HIGHEST
    )
    for k in range(K):
        own = dot(x_ref[:, cols(k)], mix_ref[degree_of[k], C:])
        base_ref[cols(k), :] = (own * gate_sum[:, cols(degree_of[k])]).T


def live_tiles(count_ref):
    return count_ref[0, lax.axis_index("tile")]


def rank_kernel(count_ref, src_ref, pos_ref, span_ref, oh_ref, cum_ref, *, slots):
    tiles = src_ref.shape[0]
    nb = span_ref.shape[0] // 3
    count = live_tiles(count_ref)
    owns, half = nb // 2, nb // 4
    order = iota((nb, TE), 0)
    ghost = ((order >= owns - 1) & (order < owns - 1 + half)) | (order >= owns + half)
    index = jnp.where(order >= owns - 1, order - (owns - 1), order)
    index = jnp.where(order == owns - 1 + half, owns - 1, index)
    index = jnp.where(order >= owns + half, order - owns, index)
    tile_pos = lax.axis_index("tile")
    ring_pos = (tile_pos >> 1) - (index >> 1)
    ring_pos = jnp.where(ring_pos < 0, ring_pos + half, ring_pos)
    label = 2 * (2 * ring_pos + ((tile_pos & 1) ^ (index & 1))) + jnp.where(ghost, 1, 0)

    def mark(t, carry):
        bucket = src_ref[pl.ds(t, 1), :] >> CHUNK_BITS
        bucket = jnp.where(t < count, bucket, -1)
        oh_ref[pl.ds(pl.multiple_of(t * nb, nb), nb), :] = as_bf16(label == bucket)
        return carry

    lax.fori_loop(0, tiles, mark, 0, unroll=8)
    upto = as_bf16(iota((TE, TE), 0) <= iota((TE, TE), 1))
    both = jnp.concatenate([upto, jnp.ones((TE, TE), BF16)], axis=1)
    step = 256
    for r in range(0, tiles * nb, step):
        cum_ref[r : r + step, :] = dot(oh_ref[r : r + step, :], both)

    def add(t, total):
        return total + cum_ref[pl.ds(pl.multiple_of(t * nb, nb), nb), TE:]

    total = lax.fori_loop(0, tiles, add, jnp.zeros((nb, TE), F32), unroll=8)
    blocks = jnp.floor((total + (BE - 1)) * (1.0 / BE))
    below = as_bf16(iota((nb, nb), 1) < iota((nb, nb), 0))
    first = dot(below, blocks.astype(BF16))
    span_ref[:nb, :] = first.astype(I32)
    span_ref[nb : 2 * nb, :] = blocks.astype(I32)
    passed = jnp.where(iota((nb, TE), 1).astype(F32) >= first + blocks, 1.0, 0.0)
    chunk_of = jnp.minimum(jnp.sum(passed, axis=0, keepdims=True), nb - 1.0)
    span_ref[2 * nb :, :] = jnp.broadcast_to(chunk_of, (nb, TE)).astype(I32)

    def place(t, run):
        rows = pl.ds(pl.multiple_of(t * nb, nb), nb)
        oh = oh_ref[rows, :].astype(F32)
        value = oh * (cum_ref[rows, :TE] + run)
        place_of = jnp.sum(value, axis=0, keepdims=True).astype(I32)
        pos_ref[pl.ds(t, 1), :] = jnp.where(t < count, 2 * place_of, 2 * slots)
        return run + cum_ref[rows, TE:]

    lax.fori_loop(0, tiles, place, first * BE - 1.0, unroll=8)


def radial_kernel(count_ref, tgt_ref, feat_ref, rin_ref, rad_ref, rsum_ref):
    tiles = tgt_ref.shape[0]
    count = live_tiles(count_ref)
    rsum_ref[...] = jnp.zeros_like(rsum_ref)
    group = 8
    atom_id = iota((ATOM_DEV, TE), 0)

    def rows_of(i):
        return pl.ds(pl.multiple_of(i * (group * TE), group * TE), group * TE)

    def hidden_layer(i):
        hidden = 0.5 * dot(feat_ref[rows_of(i), :], rin_ref[...])
        rad_ref[rows_of(i), :] = (hidden + hidden * jnp.tanh(hidden)).astype(BF16)

    def add_up(i):
        land = []
        for q in range(group):
            t = i * group + q
            tgt = jnp.where(t < count, tgt_ref[pl.ds(t, 1), :], -1)
            land.append(as_bf16(atom_id == tgt))
        rsum_ref[...] += dot(jnp.concatenate(land, axis=1), rad_ref[rows_of(i), :])

    hidden_layer(0)
    groups = (count + group - 1) // group

    def step(i, carry):
        add_up(i)
        hidden_layer(i + 1)
        return carry

    lax.fori_loop(0, groups - 1, step, 0)
    add_up(groups - 1)


def place_kernel(
    count_ref,
    pos_ref,
    span_ref,
    src_ref,
    tgt_ref,
    rin_hbm,
    rad_hbm,
    tgt_hbm,
    srcs_ref,
    pairs,
    even,
    odd,
    rad_out,
    tgt_out,
    rin_ref,
    rin_sems,
    sems,
):
    tiles = src_ref.shape[0]
    head = min(16, tiles) * TE
    loads = [
        pltpu.make_async_copy(rin_hbm.at[rows, :], rin_ref.at[rows, :], rin_sems.at[i])
        for i, rows in enumerate((pl.ds(0, head), pl.ds(head, tiles * TE - head)))
    ]
    for load in loads:
        load.start()
    nb = span_ref.shape[0] // 3
    count = live_tiles(count_ref)
    flip = jnp.where((lax.axis_index("dom") & 1) == 0, GHOST, 0)
    blank = jnp.where((iota((2 * BE, C), 0) & 1) == 1, -1.0, 0.0)

    def clear(b, carry):
        blocks = span_ref[nb + b, 0]

        @pl.when(blocks > 0)
        def _():
            last = pl.multiple_of((span_ref[b, 0] + blocks - 1) * (2 * BE), 2 * BE)
            pairs[pl.ds(last, 2 * BE), :] = blank

        return carry

    lax.fori_loop(0, nb, clear, 0)
    eye = iota((TE, TE), 0) == iota((TE, TE), 1)
    spread = jnp.concatenate(
        [jnp.ones((TE, C), BF16), jnp.full((TE, C), float(CHUNK), BF16)], axis=0
    )

    def compute(t, out):
        t = jnp.minimum(t, tiles - 1)
        rows = pl.ds(pl.multiple_of(t * TE, TE), TE)
        out[pl.ds(0, TE, stride=2), :] = rin_ref[rows, :].astype(F32)
        src = src_ref[pl.ds(t, 1), :]
        src = (src & (CHUNK - 1)) ^ jnp.where((src & CHUNK) != 0, flip, 0)
        tgt = tgt_ref[pl.ds(t, 1), :]
        diag_s = jnp.where(eye, src.astype(F32), 0.0).astype(BF16)
        diag_t = jnp.where(eye, tgt.astype(F32), 0.0).astype(BF16)
        code = dot(jnp.concatenate([diag_s, diag_t], axis=1), spread)
        out[pl.ds(1, TE, stride=2), :] = code

    def scatter(t, data):
        for e in range(TE):
            pairs[pl.ds(pos_ref[t, e], 2), :] = data[2 * e : 2 * e + 2, :]

    loads[0].wait()
    compute(0, even)

    def step(i, carry):
        compute(2 * i + 1, odd)
        scatter(2 * i, even)
        compute(2 * i + 2, even)
        scatter(2 * i + 1, odd)
        return carry

    steps = (count + 1) // 2
    split = jnp.minimum(steps, head // (2 * TE) - 1)
    lax.fori_loop(0, split, step, 0)
    loads[1].wait()
    lax.fori_loop(split, steps, step, 0)

    def saves(j):
        rows = pl.ds(pl.multiple_of(j * BE, BE), BE)
        return (
            pltpu.make_async_copy(rad_out.at[rows, :], rad_hbm.at[rows, :], sems.at[0, j]),
            pltpu.make_async_copy(tgt_out.at[rows, :], tgt_hbm.at[rows, :], sems.at[1, j]),
        )

    def finish(j, carry):
        for h in range(BE // TE):
            row = j * (BE // TE) + h
            rows = pl.ds(pl.multiple_of(row * TE, TE), TE)
            base = pl.multiple_of(row * (2 * TE), 2 * TE)
            rad_out[rows, :] = pairs[pl.ds(base, TE, stride=2), :].astype(BF16)
            code = pairs[pl.ds(base + 1, TE, stride=2), :]
            tgt = jnp.floor(code * (1.0 / CHUNK))
            tgt_out[rows, :] = tgt.astype(BF16)
            src = jnp.where(eye, code - CHUNK * tgt, 0.0)
            srcs_ref[pl.ds(row, 1), :] = jnp.sum(src, axis=0, keepdims=True).astype(I32)
        for save in saves(j):
            save.start()
        return carry

    used = span_ref[nb - 1, 0] + span_ref[2 * nb - 1, 0]
    lax.fori_loop(0, used, finish, 0)

    def drain(j, carry):
        for save in saves(j):
            save.wait()
        return carry

    lax.fori_loop(0, used, drain, 0)


def main_kernel(*refs, low, n_ghost, n_own, final):
    span_ref, *refs = refs
    ghosts, refs = refs[: 2 * (n_ghost > 0)], refs[2 * (n_ghost > 0) :]
    owns, refs = refs[:n_own], refs[n_own:]
    rad_hbm, tgt_hbm, part_hbm, src_ref, rout_ref, *refs = refs
    out_ref, rbuf, tbuf, land_ref, message_ref, tables, sems, table_sems, part_sem, *refs = refs
    acc_ref = refs[0] if final else out_ref
    count = n_ghost + n_own
    nb = span_ref.shape[0] // 3
    begin = span_ref[low, 0]
    end = span_ref[low + count - 1, 0] + span_ref[nb + low + count - 1, 0]
    groups = (end - begin + PER - 1) // PER

    loads = []
    for i, own in enumerate(owns):
        loads.append((own.at[:WIDTH, :], tables.at[n_ghost + i]))
    for i in range(n_ghost):
        for side in range(2):
            half = tables.at[i, :, side * GHOST : (side + 1) * GHOST]
            loads.append((ghosts[side].at[i], half))
    loads = [
        pltpu.make_async_copy(src, dst, table_sems.at[i]) for i, (src, dst) in enumerate(loads)
    ]
    def copies(p, slot):
        moves = []
        for h in range(PER):
            j = jnp.minimum(begin + PER * p + h, end - 1)
            rows = pl.ds(pl.multiple_of(j * BE, BE), BE)
            moves.append(
                pltpu.make_async_copy(rad_hbm.at[rows, :], rbuf.at[slot, h], sems.at[0, h, slot])
            )
            moves.append(
                pltpu.make_async_copy(tgt_hbm.at[rows, :], tbuf.at[slot, h], sems.at[1, h, slot])
            )
        return moves

    def fetch(p):
        @pl.when(p < groups)
        def _():
            for copy in copies(p, p & 1):
                copy.start()

    def arrive(p):
        @pl.when(p < groups)
        def _():
            for copy in copies(p, p & 1):
                copy.wait()

    fetch(0)
    for load in loads:
        load.start()
    part_load = pltpu.make_async_copy(part_hbm, acc_ref, part_sem)
    part_load.start()
    rout_t = rout_ref[...]
    atom_id = iota((BE, TE), 1).astype(F32)
    row_id = iota((CHUNK, TE), 0)

    def gather(p):
        for h in range(PER):
            j = begin + PER * p + h
            off = jnp.where(j < end, 0.0, 4096.0)
            j = jnp.maximum(jnp.minimum(j, end - 1), 0)
            c = jnp.clip(span_ref[2 * nb, j] - low, 0, count - 1)
            gate = lax.dot_general(
                rout_t, rbuf[p & 1, h], (((1,), (1,)), ((), ())), preferred_element_type=F32
            )
            pick = jnp.concatenate(
                [
                    as_bf16(row_id == src_ref[pl.ds(j * (BE // TE) + q, 1), :])
                    for q in range(BE // TE)
                ],
                axis=1,
            )
            rows = dot(tables[c], pick)
            for k in range(K):
                message = rows[cols(k), :] * gate[cols(degree_of[k]), :]
                message_ref[cols(k), h * BE : (h + 1) * BE] = message.astype(BF16)
            tgt = tbuf[p & 1, h].astype(F32) + off
            for q in range(ATOM_DEV // TE):
                land_ref[h * BE : (h + 1) * BE, q * TE : (q + 1) * TE] = as_bf16(
                    tgt == atom_id + float(q * TE)
                )

    def add_up():
        acc_ref[...] += dot(message_ref[...], land_ref[...])

    for load in loads:
        load.wait()
    arrive(0)
    fetch(1)
    gather(0)
    part_load.wait()

    def step(p, carry):
        arrive(p + 1)
        fetch(p + 2)
        add_up()
        gather(p + 1)
        return carry

    lax.fori_loop(0, groups - 1, step, 0)

    @pl.when(groups > 0)
    def _():
        add_up()

    if final:
        for k in range(K):
            out_ref[:, cols(k)] = (inv_scale * acc_ref[cols(k), :]).T.astype(BF16)


def shape(dims, kind):
    return jax.ShapeDtypeStruct(dims, kind)


def cost(flops, size):
    return pl.CostEstimate(flops=int(flops), bytes_accessed=int(size), transcendentals=0)


def body(
    embedding,
    ghost_index,
    tile_count,
    edge_source,
    edge_target,
    edge_features,
    radial_in,
    radial_out,
    mix_weight,
):
    n_dom, n_tile = lax.axis_size("dom"), lax.axis_size("tile")
    tiles = edge_source.shape[0] // TE
    nb = 2 * n_tile
    slots = (tiles * TE // BE + nb) * BE
    count = tile_count
    source = edge_source.reshape(tiles, TE)
    target = edge_target.reshape(tiles, TE)
    hbm = pl.BlockSpec(memory_space=pl.ANY)

    mixed = pl.pallas_call(
        mix_kernel,
        out_shape=shape((WIDTH + EXTRA, ATOM_DEV), BF16),
        in_specs=[vmem(), vmem(), vmem()],
        out_specs=vmem(),
        compiler_params=PARAMS,
        cost_estimate=cost(256 * 256 * 1152, 2e6),
        name="mix",
    )(embedding, mix_weight, ghost_index.reshape(1, ATOM_DEV))
    ring = [(t, (t + 2) % n_tile) for t in range(n_tile)]
    flip = [(t, t ^ 1) for t in range(n_tile)]
    near = [(i, i ^ 1) for i in range(n_dom)]
    far = [(i, i + 1) for i in range(1, n_dom - 1, 2)]
    far += [(j, i) for i, j in far]
    n_ring = n_tile // 2
    half = n_tile // 2

    pos, span = pl.pallas_call(
        functools.partial(rank_kernel, slots=slots),
        out_shape=(shape((tiles, TE), I32), shape((3 * nb, TE), I32)),
        in_specs=[smem(), vmem()],
        out_specs=(vmem(), vmem()),
        scratch_shapes=[
            pltpu.VMEM((tiles * nb, TE), BF16),
            pltpu.VMEM((tiles * nb, 2 * TE), F32),
        ],
        compiler_params=PARAMS,
        cost_estimate=cost(4e9, 1e6),
        name="rank",
    )(count, source)
    radial, radial_sum = pl.pallas_call(
        radial_kernel,
        out_shape=(shape((tiles * TE, C), BF16), shape((ATOM_DEV, C), F32)),
        in_specs=[smem(), vmem(), vmem(), vmem()],
        out_specs=(vmem(), vmem()),
        compiler_params=PARAMS,
        cost_estimate=cost(10e9, 6e6),
        name="radial",
    )(count, target, edge_features, radial_in)

    def place(radial):
        return pl.pallas_call(
            place_kernel,
            out_shape=(
                shape((slots, C), BF16),
                shape((slots, C), BF16),
                shape((slots // TE, TE), I32),
            ),
            in_specs=[smem(), smem(), smem(), vmem(), vmem(), hbm],
            out_specs=(hbm, hbm, vmem()),
            scratch_shapes=[
                pltpu.VMEM((2 * slots + 8, C), F32),
                pltpu.VMEM((2 * TE, C), F32),
                pltpu.VMEM((2 * TE, C), F32),
                pltpu.VMEM((slots, C), BF16),
                pltpu.VMEM((slots, C), BF16),
                pltpu.VMEM((tiles * TE, C), BF16),
                pltpu.SemaphoreType.DMA((2,)),
                pltpu.SemaphoreType.DMA((2, slots // BE)),
            ],
            compiler_params=PARAMS,
            cost_estimate=cost(20e9, 12e6),
            name="place",
        )(count, pos, span, source, target, radial)

    def pick(blocks):
        n = len(blocks)
        near_rows, far_rows = pl.pallas_call(
            functools.partial(pick_kernel, n=n),
            out_shape=(shape((n, WIDTH, GHOST), BF16),) * 2,
            in_specs=[hbm] * n,
            out_specs=(hbm, hbm),
            scratch_shapes=[
                pltpu.VMEM((n, WIDTH + EXTRA, ATOM_DEV), BF16),
                pltpu.VMEM((n, WIDTH, GHOST), BF16),
                pltpu.VMEM((n, WIDTH, GHOST), BF16),
                pltpu.SemaphoreType.DMA((3, n)),
            ],
            compiler_params=PARAMS,
            cost_estimate=cost(2e8, 4e5),
            name="pick",
        )(*blocks)
        return near_rows, far_rows

    base, rout_t = pl.pallas_call(
        base_kernel,
        out_shape=(shape((WIDTH, ATOM_DEV), F32), shape((3 * C, C), BF16)),
        in_specs=[vmem()] * 4,
        out_specs=(vmem(), vmem()),
        compiler_params=PARAMS,
        cost_estimate=cost(1e9, 2e6),
        name="base",
    )(radial_sum, radial_out, embedding, mix_weight)

    def main(low, ghosts, owns, part, name, final=False):
        dims, kind = ((ATOM_DEV, WIDTH), BF16) if final else ((WIDTH, ATOM_DEV), F32)
        n_ghost = half if ghosts else 0
        count_all = n_ghost + len(owns)
        return pl.pallas_call(
            functools.partial(
                main_kernel, low=low, n_ghost=n_ghost, n_own=len(owns), final=final
            ),
            out_shape=shape(dims, kind),
            in_specs=[smem()] + [hbm] * (len(ghosts) + len(owns) + 3) + [vmem()] * 2,
            out_specs=vmem(),
            scratch_shapes=[
                pltpu.VMEM((2, PER, BE, C), BF16),
                pltpu.VMEM((2, PER, BE, C), BF16),
                pltpu.VMEM((PER * BE, ATOM_DEV), BF16),
                pltpu.VMEM((WIDTH, PER * BE), BF16),
                pltpu.VMEM((count_all, WIDTH, ATOM_DEV), BF16),
                pltpu.SemaphoreType.DMA((2, PER, 2)),
                pltpu.SemaphoreType.DMA((2 * n_ghost + len(owns),)),
                pltpu.SemaphoreType.DMA,
            ]
            + ([pltpu.VMEM((WIDTH, ATOM_DEV), F32)] if final else []),
            compiler_params=PARAMS,
            cost_estimate=cost(1e8 * count_all, 1e5 * count_all),
            name=name,
        )(span, *ghosts, *owns, radial_sorted, target_sorted, part, source_sorted, rout_t)

    together = lax.optimization_barrier
    ring_rows, flip_rows = [mixed], []
    held = mixed
    part = None
    for k in range(n_ring):
        if k == n_ring - 1:
            early = [rows for pair in zip(ring_rows, flip_rows) for rows in pair]
            early.append(ring_rows[half // 2])
            part = main(0, [], early[: half + 1], base, "main_one")
            held, part = together((held, part))
            ring_rows[-1] = held
        swap = together((held, span))[0] if k == 0 else held
        flip_rows.append(lax.ppermute(swap, "tile", flip))
        if k < n_ring - 1:
            held = lax.ppermute(held, "tile", ring)
            if k == 0:
                held, radial, base = together((held, radial, base))
                radial_sorted, target_sorted, source_sorted = place(radial)
            if k == 1:
                held, radial_sorted = together((held, radial_sorted))
            ring_rows.append(held)
    owns = [rows for pair in zip(ring_rows, flip_rows) for rows in pair]

    def pick_after(blocks, part):
        first, part = together((blocks[0], part))
        near_rows, far_rows = pick([first, *blocks[1:]])
        near_rows, part = together((near_rows, part))
        return [lax.ppermute(near_rows, "dom", near), lax.ppermute(far_rows, "dom", far)], part

    ghosts_a, part = pick_after(owns[:half], part)
    part = main(half + 1, [], owns[half + 1 : -1], part, "main_two")
    ghosts_b, part = pick_after(owns[half:], part)
    part = main(n_tile - 1, ghosts_a, owns[-1:], part, "main_three")
    return main(n_tile + half, ghosts_b, [], part, "main_four", final=True)


def solution(mesh):
    both = ("dom", "tile")
    return jax.shard_map(
        body,
        mesh=mesh,
        in_specs=(
            P(both, None),
            P(both),
            P("dom", None),
            P(both),
            P(both),
            P(both, None),
            P(),
            P(),
            P(),
        ),
        out_specs=P(both, None),
        check_vma=False,
    )
```

```python
import functools
import jax
import jax.numpy as jnp
from jax import lax
from jax.experimental import pallas as pl
from jax.experimental.pallas import tpu as pltpu
from jax.sharding import PartitionSpec as P

C = 128
K = 9
ATOM_DEV = 256
GHOST = 128
TE = 128
BE = 256
CHUNK = 256
CHUNK_BITS = 8
WIDTH = K * C
EXTRA = 16
PER = 4
degree_of = (0, 1, 1, 1, 2, 2, 2, 2, 2)
inv_scale = 0.125

F32 = jnp.float32
BF16 = jnp.bfloat16
I32 = jnp.int32

PARAMS = pltpu.CompilerParams(vmem_limit_bytes=64 * 1024 * 1024)


def vmem():
    return pl.BlockSpec(memory_space=pltpu.VMEM)


def smem():
    return pl.BlockSpec(memory_space=pltpu.SMEM)


def cols(k):
    return slice(k * C, (k + 1) * C)


def iota(shape, dim):
    return lax.broadcasted_iota(I32, shape, dim)


def as_bf16(mask):
    return jnp.where(mask, 1.0, 0.0).astype(BF16)


def dot(a, b):
    return jnp.dot(a, b, preferred_element_type=F32)


def mix_kernel(x_ref, mix_ref, pick_ref, mixed_ref):
    for k in range(K):
        mixed = dot(x_ref[:, cols(k)], mix_ref[degree_of[k], :C])
        mixed_ref[cols(k), :] = mixed.T.astype(BF16)
    picks = jnp.broadcast_to(pick_ref[...].astype(F32), (EXTRA, ATOM_DEV))
    mixed_ref[WIDTH:, :] = picks.astype(BF16)


def pick_rows(table, picks, near_ref, far_ref):
    even = (lax.axis_index("dom") & 1) == 0
    picks = picks.astype(F32)[:1, :].astype(I32)
    down, up = picks[:, :GHOST], picks[:, GHOST:]
    row_id = iota((ATOM_DEV, GHOST), 0)
    chosen = jnp.concatenate(
        [
            as_bf16(row_id == jnp.where(even, up, down)),
            as_bf16(row_id == jnp.where(even, down, up)),
        ],
        axis=1,
    )
    rows = dot(table, chosen).astype(BF16)
    near_ref[...] = rows[:, :GHOST]
    far_ref[...] = rows[:, GHOST:]


def pick_kernel(*refs, n):
    blocks, refs = refs[:n], refs[n:]
    near_hbm, far_hbm, inside, near, far, sems = refs
    loads = [
        pltpu.make_async_copy(block, inside.at[i], sems.at[0, i]) for i, block in enumerate(blocks)
    ]
    saves = []
    for load in loads:
        load.start()
    for load in loads:
        load.wait()
    for i in range(n):
        pick_rows(inside[i, :WIDTH, :], inside[i, WIDTH:, :], near.at[i], far.at[i])
    for i in range(n):
        for side, (src, dst) in enumerate(((near, near_hbm), (far, far_hbm))):
            save = pltpu.make_async_copy(src.at[i], dst.at[i], sems.at[1 + side, i])
            save.start()
            saves.append(save)
    for save in saves:
        save.wait()


def base_kernel(rsum_ref, rout_ref, x_ref, mix_ref, base_ref, rout_t_ref):
    rout = rout_ref[...].astype(F32)
    rout_t_ref[...] = rout.T.astype(BF16)
    gate_sum = jnp.dot(
        rsum_ref[...], rout, preferred_element_type=F32, precision=lax.Precision.HIGHEST
    )
    for k in range(K):
        own = dot(x_ref[:, cols(k)], mix_ref[degree_of[k], C:])
        base_ref[cols(k), :] = (own * gate_sum[:, cols(degree_of[k])]).T


def live_tiles(count_ref):
    return count_ref[0, lax.axis_index("tile")]


def rank_kernel(count_ref, src_ref, pos_ref, span_ref, oh_ref, cum_ref, *, slots):
    tiles = src_ref.shape[0]
    nb = span_ref.shape[0] // 3
    count = live_tiles(count_ref)
    half, few = nb // 4, nb // 8
    order = iota((nb, TE), 0)
    ghost = ((order >= half + few) & (order < 2 * half + few)) | (order >= 3 * half)
    index = order
    index = jnp.where(order >= half, half + 2 * (order - half), index)
    index = jnp.where(order >= half + few, order - (half + few), index)
    index = jnp.where(order >= 2 * half + few, half + 2 * (order - (2 * half + few)) + 1, index)
    index = jnp.where(order >= 3 * half, order - 2 * half, index)
    tile_pos = lax.axis_index("tile")
    step = index >> 1
    ahead = half // 2
    ring_pos = (tile_pos >> 1) + jnp.where(step <= ahead, -step, step - ahead)
    ring_pos = jnp.where(ring_pos < 0, ring_pos + half, ring_pos)
    ring_pos = jnp.where(ring_pos >= half, ring_pos - half, ring_pos)
    label = 2 * (2 * ring_pos + ((tile_pos & 1) ^ (index & 1))) + jnp.where(ghost, 1, 0)

    def mark(t, carry):
        bucket = src_ref[pl.ds(t, 1), :] >> CHUNK_BITS
        bucket = jnp.where(t < count, bucket, -1)
        oh_ref[pl.ds(pl.multiple_of(t * nb, nb), nb), :] = as_bf16(label == bucket)
        return carry

    lax.fori_loop(0, tiles, mark, 0, unroll=8)
    upto = as_bf16(iota((TE, TE), 0) <= iota((TE, TE), 1))
    both = jnp.concatenate([upto, jnp.ones((TE, TE), BF16)], axis=1)
    step = 256
    for r in range(0, tiles * nb, step):
        cum_ref[r : r + step, :] = dot(oh_ref[r : r + step, :], both)

    def add(t, total):
        return total + cum_ref[pl.ds(pl.multiple_of(t * nb, nb), nb), TE:]

    total = lax.fori_loop(0, tiles, add, jnp.zeros((nb, TE), F32), unroll=8)
    blocks = jnp.floor((total + (BE - 1)) * (1.0 / BE))
    below = as_bf16(iota((nb, nb), 1) < iota((nb, nb), 0))
    first = dot(below, blocks.astype(BF16))
    span_ref[:nb, :] = first.astype(I32)
    span_ref[nb : 2 * nb, :] = blocks.astype(I32)
    passed = jnp.where(iota((nb, TE), 1).astype(F32) >= first + blocks, 1.0, 0.0)
    chunk_of = jnp.minimum(jnp.sum(passed, axis=0, keepdims=True), nb - 1.0)
    span_ref[2 * nb :, :] = jnp.broadcast_to(chunk_of, (nb, TE)).astype(I32)

    def place(t, run):
        rows = pl.ds(pl.multiple_of(t * nb, nb), nb)
        oh = oh_ref[rows, :].astype(F32)
        value = oh * (cum_ref[rows, :TE] + run)
        place_of = jnp.sum(value, axis=0, keepdims=True).astype(I32)
        pos_ref[pl.ds(t, 1), :] = jnp.where(t < count, 2 * place_of, 2 * slots)
        return run + cum_ref[rows, TE:]

    lax.fori_loop(0, tiles, place, first * BE - 1.0, unroll=8)


def radial_kernel(count_ref, tgt_ref, feat_ref, rin_ref, rad_ref, rsum_ref):
    tiles = tgt_ref.shape[0]
    count = live_tiles(count_ref)
    rsum_ref[...] = jnp.zeros_like(rsum_ref)
    group = 8
    atom_id = iota((ATOM_DEV, TE), 0)

    def rows_of(i):
        return pl.ds(pl.multiple_of(i * (group * TE), group * TE), group * TE)

    def hidden_layer(i):
        hidden = 0.5 * dot(feat_ref[rows_of(i), :], rin_ref[...])
        rad_ref[rows_of(i), :] = (hidden + hidden * jnp.tanh(hidden)).astype(BF16)

    def add_up(i):
        land = []
        for q in range(group):
            t = i * group + q
            tgt = jnp.where(t < count, tgt_ref[pl.ds(t, 1), :], -1)
            land.append(as_bf16(atom_id == tgt))
        rsum_ref[...] += dot(jnp.concatenate(land, axis=1), rad_ref[rows_of(i), :])

    hidden_layer(0)
    groups = (count + group - 1) // group

    def step(i, carry):
        add_up(i)
        hidden_layer(i + 1)
        return carry

    lax.fori_loop(0, groups - 1, step, 0)
    add_up(groups - 1)


def place_kernel(
    count_ref,
    pos_ref,
    span_ref,
    src_ref,
    tgt_ref,
    rin_hbm,
    rad_hbm,
    tgt_hbm,
    srcs_ref,
    pairs,
    even,
    odd,
    rad_out,
    tgt_out,
    rin_ref,
    rin_sems,
    sems,
):
    tiles = src_ref.shape[0]
    head = min(16, tiles) * TE
    loads = [
        pltpu.make_async_copy(rin_hbm.at[rows, :], rin_ref.at[rows, :], rin_sems.at[i])
        for i, rows in enumerate((pl.ds(0, head), pl.ds(head, tiles * TE - head)))
    ]
    for load in loads:
        load.start()
    nb = span_ref.shape[0] // 3
    count = live_tiles(count_ref)
    flip = jnp.where((lax.axis_index("dom") & 1) == 0, GHOST, 0)
    blank = jnp.where((iota((2 * BE, C), 0) & 1) == 1, -1.0, 0.0)

    def clear(b, carry):
        blocks = span_ref[nb + b, 0]

        @pl.when(blocks > 0)
        def _():
            last = pl.multiple_of((span_ref[b, 0] + blocks - 1) * (2 * BE), 2 * BE)
            pairs[pl.ds(last, 2 * BE), :] = blank

        return carry

    lax.fori_loop(0, nb, clear, 0)
    eye = iota((TE, TE), 0) == iota((TE, TE), 1)
    spread = jnp.concatenate(
        [jnp.ones((TE, C), BF16), jnp.full((TE, C), float(CHUNK), BF16)], axis=0
    )

    def compute(t, out):
        t = jnp.minimum(t, tiles - 1)
        rows = pl.ds(pl.multiple_of(t * TE, TE), TE)
        out[pl.ds(0, TE, stride=2), :] = rin_ref[rows, :].astype(F32)
        src = src_ref[pl.ds(t, 1), :]
        src = (src & (CHUNK - 1)) ^ jnp.where((src & CHUNK) != 0, flip, 0)
        tgt = tgt_ref[pl.ds(t, 1), :]
        diag_s = jnp.where(eye, src.astype(F32), 0.0).astype(BF16)
        diag_t = jnp.where(eye, tgt.astype(F32), 0.0).astype(BF16)
        code = dot(jnp.concatenate([diag_s, diag_t], axis=1), spread)
        out[pl.ds(1, TE, stride=2), :] = code

    def scatter(t, data):
        for e in range(TE):
            pairs[pl.ds(pos_ref[t, e], 2), :] = data[2 * e : 2 * e + 2, :]

    loads[0].wait()
    compute(0, even)

    def step(i, carry):
        compute(2 * i + 1, odd)
        scatter(2 * i, even)
        compute(2 * i + 2, even)
        scatter(2 * i + 1, odd)
        return carry

    steps = (count + 1) // 2
    split = jnp.minimum(steps, head // (2 * TE) - 1)
    lax.fori_loop(0, split, step, 0)
    loads[1].wait()
    lax.fori_loop(split, steps, step, 0)

    def saves(j):
        rows = pl.ds(pl.multiple_of(j * BE, BE), BE)
        return (
            pltpu.make_async_copy(rad_out.at[rows, :], rad_hbm.at[rows, :], sems.at[0, j]),
            pltpu.make_async_copy(tgt_out.at[rows, :], tgt_hbm.at[rows, :], sems.at[1, j]),
        )

    def finish(j, carry):
        for h in range(BE // TE):
            row = j * (BE // TE) + h
            rows = pl.ds(pl.multiple_of(row * TE, TE), TE)
            base = pl.multiple_of(row * (2 * TE), 2 * TE)
            rad_out[rows, :] = pairs[pl.ds(base, TE, stride=2), :].astype(BF16)
            code = pairs[pl.ds(base + 1, TE, stride=2), :]
            tgt = jnp.floor(code * (1.0 / CHUNK))
            tgt_out[rows, :] = tgt.astype(BF16)
            src = jnp.where(eye, code - CHUNK * tgt, 0.0)
            srcs_ref[pl.ds(row, 1), :] = jnp.sum(src, axis=0, keepdims=True).astype(I32)
        for save in saves(j):
            save.start()
        return carry

    used = span_ref[nb - 1, 0] + span_ref[2 * nb - 1, 0]
    lax.fori_loop(0, used, finish, 0)

    def drain(j, carry):
        for save in saves(j):
            save.wait()
        return carry

    lax.fori_loop(0, used, drain, 0)


def main_kernel(*refs, low, n_ghost, n_own, n_pick, final):
    span_ref, *refs = refs
    ghosts, refs = refs[: 2 * (n_ghost > 0)], refs[2 * (n_ghost > 0) :]
    owns, refs = refs[:n_own], refs[n_own:]
    rad_hbm, tgt_hbm, part_hbm, src_ref, rout_ref, *refs = refs
    out_ref, *refs = refs
    if n_pick:
        near_hbm, far_hbm, *refs = refs
    rbuf, tbuf, land_ref, message_ref, tables, sems, table_sems, part_sem, *refs = refs
    acc_ref = refs[0] if final else out_ref
    if n_pick:
        picks, near, far, pick_sems = refs
    count = n_ghost + n_own
    nb = span_ref.shape[0] // 3
    begin = span_ref[low, 0]
    end = span_ref[low + count - 1, 0] + span_ref[nb + low + count - 1, 0]
    groups = (end - begin + PER - 1) // PER

    loads = []
    for i, own in enumerate(owns):
        loads.append((own.at[:WIDTH, :], tables.at[n_ghost + i]))
    for i in range(n_ghost):
        for side in range(2):
            half = tables.at[i, :, side * GHOST : (side + 1) * GHOST]
            loads.append((ghosts[side].at[i], half))
    loads = [
        pltpu.make_async_copy(src, dst, table_sems.at[i]) for i, (src, dst) in enumerate(loads)
    ]
    for i in range(n_pick):
        load = pltpu.make_async_copy(owns[i].at[WIDTH:, :], picks.at[i], pick_sems.at[0, i])
        loads.append(load)
    def copies(p, slot):
        moves = []
        for h in range(PER):
            j = jnp.minimum(begin + PER * p + h, end - 1)
            rows = pl.ds(pl.multiple_of(j * BE, BE), BE)
            moves.append(
                pltpu.make_async_copy(rad_hbm.at[rows, :], rbuf.at[slot, h], sems.at[0, h, slot])
            )
            moves.append(
                pltpu.make_async_copy(tgt_hbm.at[rows, :], tbuf.at[slot, h], sems.at[1, h, slot])
            )
        return moves

    def fetch(p):
        @pl.when(p < groups)
        def _():
            for copy in copies(p, p & 1):
                copy.start()

    def arrive(p):
        @pl.when(p < groups)
        def _():
            for copy in copies(p, p & 1):
                copy.wait()

    fetch(0)
    for load in loads:
        load.start()
    part_load = pltpu.make_async_copy(part_hbm, acc_ref, part_sem)
    part_load.start()
    rout_t = rout_ref[...]
    atom_id = iota((BE, TE), 1).astype(F32)
    row_id = iota((CHUNK, TE), 0)

    def gather(p):
        for h in range(PER):
            j = begin + PER * p + h
            off = jnp.where(j < end, 0.0, 4096.0)
            j = jnp.maximum(jnp.minimum(j, end - 1), 0)
            c = jnp.clip(span_ref[2 * nb, j] - low, 0, count - 1)
            gate = lax.dot_general(
                rout_t, rbuf[p & 1, h], (((1,), (1,)), ((), ())), preferred_element_type=F32
            )
            pick = jnp.concatenate(
                [
                    as_bf16(row_id == src_ref[pl.ds(j * (BE // TE) + q, 1), :])
                    for q in range(BE // TE)
                ],
                axis=1,
            )
            rows = dot(tables[c], pick)
            for k in range(K):
                message = rows[cols(k), :] * gate[cols(degree_of[k]), :]
                message_ref[cols(k), h * BE : (h + 1) * BE] = message.astype(BF16)
            tgt = tbuf[p & 1, h].astype(F32) + off
            for q in range(ATOM_DEV // TE):
                land_ref[h * BE : (h + 1) * BE, q * TE : (q + 1) * TE] = as_bf16(
                    tgt == atom_id + float(q * TE)
                )

    def add_up():
        acc_ref[...] += dot(message_ref[...], land_ref[...])

    for load in loads:
        load.wait()
    saves = []
    for i in range(n_pick):
        pick_rows(tables[i], picks[i], near.at[i], far.at[i])
    for i in range(n_pick):
        for side, (src, dst) in enumerate(((near, near_hbm), (far, far_hbm))):
            save = pltpu.make_async_copy(src.at[i], dst.at[i], pick_sems.at[1 + side, i])
            save.start()
            saves.append(save)
    arrive(0)
    fetch(1)
    gather(0)
    part_load.wait()

    def step(p, carry):
        arrive(p + 1)
        fetch(p + 2)
        add_up()
        gather(p + 1)
        return carry

    lax.fori_loop(0, groups - 1, step, 0)

    @pl.when(groups > 0)
    def _():
        add_up()

    for save in saves:
        save.wait()
    if final:
        for k in range(K):
            out_ref[:, cols(k)] = (inv_scale * acc_ref[cols(k), :]).T.astype(BF16)


def shape(dims, kind):
    return jax.ShapeDtypeStruct(dims, kind)


def cost(flops, size):
    return pl.CostEstimate(flops=int(flops), bytes_accessed=int(size), transcendentals=0)


def body(
    embedding,
    ghost_index,
    tile_count,
    edge_source,
    edge_target,
    edge_features,
    radial_in,
    radial_out,
    mix_weight,
):
    n_dom, n_tile = lax.axis_size("dom"), lax.axis_size("tile")
    tiles = edge_source.shape[0] // TE
    nb = 2 * n_tile
    slots = (tiles * TE // BE + nb) * BE
    count = tile_count
    source = edge_source.reshape(tiles, TE)
    target = edge_target.reshape(tiles, TE)
    hbm = pl.BlockSpec(memory_space=pl.ANY)

    mixed = pl.pallas_call(
        mix_kernel,
        out_shape=shape((WIDTH + EXTRA, ATOM_DEV), BF16),
        in_specs=[vmem(), vmem(), vmem()],
        out_specs=vmem(),
        compiler_params=PARAMS,
        cost_estimate=cost(256 * 256 * 1152, 2e6),
        name="mix",
    )(embedding, mix_weight, ghost_index.reshape(1, ATOM_DEV))
    ring = [(t, (t + 2) % n_tile) for t in range(n_tile)]
    back = [(target, source) for source, target in ring]
    flip = [(t, t ^ 1) for t in range(n_tile)]
    near = [(i, i ^ 1) for i in range(n_dom)]
    far = [(i, i + 1) for i in range(1, n_dom - 1, 2)]
    far += [(j, i) for i, j in far]
    n_ring = n_tile // 2
    half = n_tile // 2

    pos, span = pl.pallas_call(
        functools.partial(rank_kernel, slots=slots),
        out_shape=(shape((tiles, TE), I32), shape((3 * nb, TE), I32)),
        in_specs=[smem(), vmem()],
        out_specs=(vmem(), vmem()),
        scratch_shapes=[
            pltpu.VMEM((tiles * nb, TE), BF16),
            pltpu.VMEM((tiles * nb, 2 * TE), F32),
        ],
        compiler_params=PARAMS,
        cost_estimate=cost(4e9, 1e6),
        name="rank",
    )(count, source)
    radial, radial_sum = pl.pallas_call(
        radial_kernel,
        out_shape=(shape((tiles * TE, C), BF16), shape((ATOM_DEV, C), F32)),
        in_specs=[smem(), vmem(), vmem(), vmem()],
        out_specs=(vmem(), vmem()),
        compiler_params=PARAMS,
        cost_estimate=cost(10e9, 6e6),
        name="radial",
    )(count, target, edge_features, radial_in)

    def place(radial):
        return pl.pallas_call(
            place_kernel,
            out_shape=(
                shape((slots, C), BF16),
                shape((slots, C), BF16),
                shape((slots // TE, TE), I32),
            ),
            in_specs=[smem(), smem(), smem(), vmem(), vmem(), hbm],
            out_specs=(hbm, hbm, vmem()),
            scratch_shapes=[
                pltpu.VMEM((2 * slots + 8, C), F32),
                pltpu.VMEM((2 * TE, C), F32),
                pltpu.VMEM((2 * TE, C), F32),
                pltpu.VMEM((slots, C), BF16),
                pltpu.VMEM((slots, C), BF16),
                pltpu.VMEM((tiles * TE, C), BF16),
                pltpu.SemaphoreType.DMA((2,)),
                pltpu.SemaphoreType.DMA((2, slots // BE)),
            ],
            compiler_params=PARAMS,
            cost_estimate=cost(20e9, 12e6),
            name="place",
        )(count, pos, span, source, target, radial)

    def pick(blocks):
        n = len(blocks)
        near_rows, far_rows = pl.pallas_call(
            functools.partial(pick_kernel, n=n),
            out_shape=(shape((n, WIDTH, GHOST), BF16),) * 2,
            in_specs=[hbm] * n,
            out_specs=(hbm, hbm),
            scratch_shapes=[
                pltpu.VMEM((n, WIDTH + EXTRA, ATOM_DEV), BF16),
                pltpu.VMEM((n, WIDTH, GHOST), BF16),
                pltpu.VMEM((n, WIDTH, GHOST), BF16),
                pltpu.SemaphoreType.DMA((3, n)),
            ],
            compiler_params=PARAMS,
            cost_estimate=cost(2e8, 4e5),
            name="pick",
        )(*blocks)
        return near_rows, far_rows

    base, rout_t = pl.pallas_call(
        base_kernel,
        out_shape=(shape((WIDTH, ATOM_DEV), F32), shape((3 * C, C), BF16)),
        in_specs=[vmem()] * 4,
        out_specs=(vmem(), vmem()),
        compiler_params=PARAMS,
        cost_estimate=cost(1e9, 2e6),
        name="base",
    )(radial_sum, radial_out, embedding, mix_weight)

    def main(low, ghosts, owns, part, name, n_pick=0, final=False):
        dims, kind = ((ATOM_DEV, WIDTH), BF16) if final else ((WIDTH, ATOM_DEV), F32)
        n_ghost = half if ghosts else 0
        count_all = n_ghost + len(owns)
        return pl.pallas_call(
            functools.partial(
                main_kernel,
                low=low,
                n_ghost=n_ghost,
                n_own=len(owns),
                n_pick=n_pick,
                final=final,
            ),
            out_shape=(shape(dims, kind),)
            + ((shape((n_pick, WIDTH, GHOST), BF16),) * 2 if n_pick else ()),
            in_specs=[smem()] + [hbm] * (len(ghosts) + len(owns) + 3) + [vmem()] * 2,
            out_specs=(vmem(),) + ((hbm, hbm) if n_pick else ()),
            scratch_shapes=[
                pltpu.VMEM((2, PER, BE, C), BF16),
                pltpu.VMEM((2, PER, BE, C), BF16),
                pltpu.VMEM((PER * BE, ATOM_DEV), BF16),
                pltpu.VMEM((WIDTH, PER * BE), BF16),
                pltpu.VMEM((count_all, WIDTH, ATOM_DEV), BF16),
                pltpu.SemaphoreType.DMA((2, PER, 2)),
                pltpu.SemaphoreType.DMA((2 * n_ghost + len(owns),)),
                pltpu.SemaphoreType.DMA,
            ]
            + ([pltpu.VMEM((WIDTH, ATOM_DEV), F32)] if final else [])
            + (
                [
                    pltpu.VMEM((n_pick, EXTRA, ATOM_DEV), BF16),
                    pltpu.VMEM((n_pick, WIDTH, GHOST), BF16),
                    pltpu.VMEM((n_pick, WIDTH, GHOST), BF16),
                    pltpu.SemaphoreType.DMA((3, n_pick)),
                ]
                if n_pick
                else []
            ),
            compiler_params=PARAMS,
            cost_estimate=cost(1e8 * count_all, 1e5 * count_all),
            name=name,
        )(span, *ghosts, *owns, radial_sorted, target_sorted, part, source_sorted, rout_t)

    together = lax.optimization_barrier

    def to_ring(rows):
        return lax.ppermute(rows, "tile", ring)

    def to_flip(rows):
        return lax.ppermute(rows, "tile", flip)

    def exchange(near_rows, far_rows):
        return [lax.ppermute(near_rows, "dom", near), lax.ppermute(far_rows, "dom", far)]

    few = half // 2
    ahead = [mixed, to_ring(mixed)]
    behind = [lax.ppermute(together((mixed, radial))[0], "tile", back)]
    ahead[1], radial, base = together((ahead[1], radial, base))
    flips = [to_flip(together((mixed, span))[0]), to_flip(ahead[1])]
    while len(ahead) <= few:
        ahead.append(to_ring(ahead[-1]))
    while len(behind) < n_ring - 1 - few:
        behind.append(lax.ppermute(behind[-1], "tile", back))
    radial_sorted, target_sorted, source_sorted = place(radial)
    ahead[2], behind[0], radial_sorted = together((ahead[2], behind[0], radial_sorted))
    rings = ahead + behind
    flips += [to_flip(rows) for rows in rings[2:]]
    owns = [rows for pair in zip(rings, flips) for rows in pair]
    part, near_rows, far_rows = main(
        0, [], owns[:half] + rings[few:], base, "main_one", n_pick=half
    )
    ghosts_a = exchange(near_rows, far_rows)
    last = owns[half:]
    last[0], part = together((last[0], part))
    near_rows, far_rows = pick(last)
    near_rows, part = together((near_rows, part))
    ghosts_b = exchange(near_rows, far_rows)
    (part,) = main(half + few, ghosts_a, flips[few:], part, "main_two")
    return main(n_tile + half, ghosts_b, [], part, "main_three", final=True)[0]


def solution(mesh):
    both = ("dom", "tile")
    return jax.shard_map(
        body,
        mesh=mesh,
        in_specs=(
            P(both, None),
            P(both),
            P("dom", None),
            P(both),
            P(both),
            P(both, None),
            P(),
            P(),
            P(),
        ),
        out_specs=P(both, None),
        check_vma=False,
    )
```

```python
import functools
import jax
import jax.numpy as jnp
from jax import lax
from jax.experimental import pallas as pl
from jax.experimental.pallas import tpu as pltpu
from jax.sharding import PartitionSpec as P

C = 128
K = 9
ATOM_DEV = 256
GHOST = 128
TE = 128
BE = 256
CHUNK = 256
CHUNK_BITS = 8
WIDTH = K * C
EXTRA = 16
PER = 4
degree_of = (0, 1, 1, 1, 2, 2, 2, 2, 2)
inv_scale = 0.125

F32 = jnp.float32
BF16 = jnp.bfloat16
I32 = jnp.int32

PARAMS = pltpu.CompilerParams(vmem_limit_bytes=64 * 1024 * 1024)


def vmem():
    return pl.BlockSpec(memory_space=pltpu.VMEM)


def smem():
    return pl.BlockSpec(memory_space=pltpu.SMEM)


def cols(k):
    return slice(k * C, (k + 1) * C)


def iota(shape, dim):
    return lax.broadcasted_iota(I32, shape, dim)


def as_bf16(mask):
    return jnp.where(mask, 1.0, 0.0).astype(BF16)


def dot(a, b):
    return jnp.dot(a, b, preferred_element_type=F32)


def mix_kernel(x_ref, mix_ref, pick_ref, mixed_ref):
    for k in range(K):
        mixed = dot(x_ref[:, cols(k)], mix_ref[degree_of[k], :C])
        mixed_ref[cols(k), :] = mixed.T.astype(BF16)
    picks = jnp.broadcast_to(pick_ref[...].astype(F32), (EXTRA, ATOM_DEV))
    mixed_ref[WIDTH:, :] = picks.astype(BF16)


def pick_rows(table, picks, near_ref, far_ref):
    even = (lax.axis_index("dom") & 1) == 0
    picks = picks.astype(F32)[:1, :].astype(I32)
    down, up = picks[:, :GHOST], picks[:, GHOST:]
    row_id = iota((ATOM_DEV, GHOST), 0)
    chosen = jnp.concatenate(
        [
            as_bf16(row_id == jnp.where(even, up, down)),
            as_bf16(row_id == jnp.where(even, down, up)),
        ],
        axis=1,
    )
    rows = dot(table, chosen).astype(BF16)
    near_ref[...] = rows[:, :GHOST]
    far_ref[...] = rows[:, GHOST:]


def pick_kernel(*refs, n):
    blocks, refs = refs[:n], refs[n:]
    near_hbm, far_hbm, inside, near, far, sems = refs
    loads = [
        pltpu.make_async_copy(block, inside.at[i], sems.at[0, i]) for i, block in enumerate(blocks)
    ]
    saves = []
    for load in loads:
        load.start()
    for load in loads:
        load.wait()
    for i in range(n):
        pick_rows(inside[i, :WIDTH, :], inside[i, WIDTH:, :], near.at[i], far.at[i])
    for i in range(n):
        for side, (src, dst) in enumerate(((near, near_hbm), (far, far_hbm))):
            save = pltpu.make_async_copy(src.at[i], dst.at[i], sems.at[1 + side, i])
            save.start()
            saves.append(save)
    for save in saves:
        save.wait()


def base_kernel(rsum_ref, rout_ref, x_ref, mix_ref, base_ref, rout_t_ref):
    rout = rout_ref[...].astype(F32)
    rout_t_ref[...] = rout.T.astype(BF16)
    gate_sum = jnp.dot(
        rsum_ref[...], rout, preferred_element_type=F32, precision=lax.Precision.HIGHEST
    )
    for k in range(K):
        own = dot(x_ref[:, cols(k)], mix_ref[degree_of[k], C:])
        base_ref[cols(k), :] = (own * gate_sum[:, cols(degree_of[k])]).T


def live_tiles(count_ref):
    return count_ref[0, lax.axis_index("tile")]


def rank_kernel(count_ref, src_ref, pos_ref, span_ref, oh_ref, cum_ref, *, slots):
    tiles = src_ref.shape[0]
    nb = span_ref.shape[0] // 3
    count = live_tiles(count_ref)
    half, few = nb // 4, nb // 8
    order = iota((nb, TE), 0)
    ghost = ((order >= half + few) & (order < 2 * half + few)) | (order >= 3 * half)
    index = order
    index = jnp.where(order >= half, half + 2 * (order - half), index)
    index = jnp.where(order >= half + few, order - (half + few), index)
    index = jnp.where(order >= 2 * half + few, half + 2 * (order - (2 * half + few)) + 1, index)
    index = jnp.where(order >= 3 * half, order - 2 * half, index)
    tile_pos = lax.axis_index("tile")
    step = index >> 1
    ahead = half // 2
    ring_pos = (tile_pos >> 1) + jnp.where(step <= ahead, -step, step - ahead)
    ring_pos = jnp.where(ring_pos < 0, ring_pos + half, ring_pos)
    ring_pos = jnp.where(ring_pos >= half, ring_pos - half, ring_pos)
    label = 2 * (2 * ring_pos + ((tile_pos & 1) ^ (index & 1))) + jnp.where(ghost, 1, 0)

    def mark(t, carry):
        bucket = src_ref[pl.ds(t, 1), :] >> CHUNK_BITS
        bucket = jnp.where(t < count, bucket, -1)
        oh_ref[pl.ds(pl.multiple_of(t * nb, nb), nb), :] = as_bf16(label == bucket)
        return carry

    lax.fori_loop(0, tiles, mark, 0, unroll=8)
    upto = as_bf16(iota((TE, TE), 0) <= iota((TE, TE), 1))
    both = jnp.concatenate([upto, jnp.ones((TE, TE), BF16)], axis=1)
    step = 256
    for r in range(0, tiles * nb, step):
        cum_ref[r : r + step, :] = dot(oh_ref[r : r + step, :], both)

    def add(t, total):
        return total + cum_ref[pl.ds(pl.multiple_of(t * nb, nb), nb), TE:]

    total = lax.fori_loop(0, tiles, add, jnp.zeros((nb, TE), F32), unroll=8)
    blocks = jnp.floor((total + (BE - 1)) * (1.0 / BE))
    below = as_bf16(iota((nb, nb), 1) < iota((nb, nb), 0))
    first = dot(below, blocks.astype(BF16))
    span_ref[:nb, :] = first.astype(I32)
    span_ref[nb : 2 * nb, :] = blocks.astype(I32)
    passed = jnp.where(iota((nb, TE), 1).astype(F32) >= first + blocks, 1.0, 0.0)
    chunk_of = jnp.minimum(jnp.sum(passed, axis=0, keepdims=True), nb - 1.0)
    span_ref[2 * nb :, :] = jnp.broadcast_to(chunk_of, (nb, TE)).astype(I32)

    def place(t, run):
        rows = pl.ds(pl.multiple_of(t * nb, nb), nb)
        oh = oh_ref[rows, :].astype(F32)
        value = oh * (cum_ref[rows, :TE] + run)
        place_of = jnp.sum(value, axis=0, keepdims=True).astype(I32)
        pos_ref[pl.ds(t, 1), :] = jnp.where(t < count, 2 * place_of, 2 * slots)
        return run + cum_ref[rows, TE:]

    lax.fori_loop(0, tiles, place, first * BE - 1.0, unroll=8)


def radial_kernel(count_ref, tgt_ref, feat_ref, rin_ref, rad_ref, rsum_ref):
    tiles = tgt_ref.shape[0]
    count = live_tiles(count_ref)
    rsum_ref[...] = jnp.zeros_like(rsum_ref)
    group = 8
    atom_id = iota((ATOM_DEV, TE), 0)

    def rows_of(i):
        return pl.ds(pl.multiple_of(i * (group * TE), group * TE), group * TE)

    def hidden_layer(i):
        hidden = 0.5 * dot(feat_ref[rows_of(i), :], rin_ref[...])
        rad_ref[rows_of(i), :] = (hidden + hidden * jnp.tanh(hidden)).astype(BF16)

    def add_up(i):
        land = []
        for q in range(group):
            t = i * group + q
            tgt = jnp.where(t < count, tgt_ref[pl.ds(t, 1), :], -1)
            land.append(as_bf16(atom_id == tgt))
        rsum_ref[...] += dot(jnp.concatenate(land, axis=1), rad_ref[rows_of(i), :])

    hidden_layer(0)
    groups = (count + group - 1) // group

    def step(i, carry):
        add_up(i)
        hidden_layer(i + 1)
        return carry

    lax.fori_loop(0, groups - 1, step, 0)
    add_up(groups - 1)


def place_kernel(
    count_ref,
    pos_ref,
    span_ref,
    src_ref,
    tgt_ref,
    rin_hbm,
    rad_hbm,
    tgt_hbm,
    srcs_ref,
    pairs,
    even,
    odd,
    rad_out,
    tgt_out,
    rin_ref,
    rin_sems,
    sems,
):
    tiles = src_ref.shape[0]
    head = min(16, tiles) * TE
    loads = [
        pltpu.make_async_copy(rin_hbm.at[rows, :], rin_ref.at[rows, :], rin_sems.at[i])
        for i, rows in enumerate((pl.ds(0, head), pl.ds(head, tiles * TE - head)))
    ]
    for load in loads:
        load.start()
    nb = span_ref.shape[0] // 3
    count = live_tiles(count_ref)
    flip = jnp.where((lax.axis_index("dom") & 1) == 0, GHOST, 0)
    blank = jnp.where((iota((2 * BE, C), 0) & 1) == 1, -1.0, 0.0)

    def clear(b, carry):
        blocks = span_ref[nb + b, 0]

        @pl.when(blocks > 0)
        def _():
            last = pl.multiple_of((span_ref[b, 0] + blocks - 1) * (2 * BE), 2 * BE)
            pairs[pl.ds(last, 2 * BE), :] = blank

        return carry

    lax.fori_loop(0, nb, clear, 0)
    eye = iota((TE, TE), 0) == iota((TE, TE), 1)
    spread = jnp.concatenate(
        [jnp.ones((TE, C), BF16), jnp.full((TE, C), float(CHUNK), BF16)], axis=0
    )

    def compute(t, out):
        t = jnp.minimum(t, tiles - 1)
        rows = pl.ds(pl.multiple_of(t * TE, TE), TE)
        out[pl.ds(0, TE, stride=2), :] = rin_ref[rows, :].astype(F32)
        src = src_ref[pl.ds(t, 1), :]
        src = (src & (CHUNK - 1)) ^ jnp.where((src & CHUNK) != 0, flip, 0)
        tgt = tgt_ref[pl.ds(t, 1), :]
        diag_s = jnp.where(eye, src.astype(F32), 0.0).astype(BF16)
        diag_t = jnp.where(eye, tgt.astype(F32), 0.0).astype(BF16)
        code = dot(jnp.concatenate([diag_s, diag_t], axis=1), spread)
        out[pl.ds(1, TE, stride=2), :] = code

    def scatter(t, data):
        for e in range(TE):
            pairs[pl.ds(pos_ref[t, e], 2), :] = data[2 * e : 2 * e + 2, :]

    loads[0].wait()
    compute(0, even)

    def step(i, carry):
        compute(2 * i + 1, odd)
        scatter(2 * i, even)
        compute(2 * i + 2, even)
        scatter(2 * i + 1, odd)
        return carry

    steps = (count + 1) // 2
    split = jnp.minimum(steps, head // (2 * TE) - 1)
    lax.fori_loop(0, split, step, 0)
    loads[1].wait()
    lax.fori_loop(split, steps, step, 0)

    def saves(j):
        rows = pl.ds(pl.multiple_of(j * BE, BE), BE)
        return (
            pltpu.make_async_copy(rad_out.at[rows, :], rad_hbm.at[rows, :], sems.at[0, j]),
            pltpu.make_async_copy(tgt_out.at[rows, :], tgt_hbm.at[rows, :], sems.at[1, j]),
        )

    def finish(j, carry):
        for h in range(BE // TE):
            row = j * (BE // TE) + h
            rows = pl.ds(pl.multiple_of(row * TE, TE), TE)
            base = pl.multiple_of(row * (2 * TE), 2 * TE)
            rad_out[rows, :] = pairs[pl.ds(base, TE, stride=2), :].astype(BF16)
            code = pairs[pl.ds(base + 1, TE, stride=2), :]
            tgt = jnp.floor(code * (1.0 / CHUNK))
            tgt_out[rows, :] = tgt.astype(BF16)
            src = jnp.where(eye, code - CHUNK * tgt, 0.0)
            srcs_ref[pl.ds(row, 1), :] = jnp.sum(src, axis=0, keepdims=True).astype(I32)
        for save in saves(j):
            save.start()
        return carry

    used = span_ref[nb - 1, 0] + span_ref[2 * nb - 1, 0]
    lax.fori_loop(0, used, finish, 0)

    def drain(j, carry):
        for save in saves(j):
            save.wait()
        return carry

    lax.fori_loop(0, used, drain, 0)


def main_kernel(*refs, low, n_ghost, n_own, n_pick, final):
    span_ref, *refs = refs
    ghosts, refs = refs[: 2 * (n_ghost > 0)], refs[2 * (n_ghost > 0) :]
    owns, refs = refs[:n_own], refs[n_own:]
    rad_hbm, tgt_hbm, part_hbm, src_ref, rout_ref, *refs = refs
    out_ref, *refs = refs
    if n_pick:
        near_hbm, far_hbm, *refs = refs
    rbuf, tbuf, land_ref, message_ref, tables, sems, table_sems, part_sem, *refs = refs
    acc_ref = refs[0] if final else out_ref
    if n_pick:
        picks, near, far, pick_sems = refs
    count = n_ghost + n_own
    nb = span_ref.shape[0] // 3
    begin = span_ref[low, 0]
    end = span_ref[low + count - 1, 0] + span_ref[nb + low + count - 1, 0]
    groups = (end - begin + PER - 1) // PER

    loads = []
    for i, own in enumerate(owns):
        loads.append((own.at[:WIDTH, :], tables.at[n_ghost + i]))
    for i in range(n_ghost):
        for side in range(2):
            half = tables.at[i, :, side * GHOST : (side + 1) * GHOST]
            loads.append((ghosts[side].at[i], half))
    loads = [
        pltpu.make_async_copy(src, dst, table_sems.at[i]) for i, (src, dst) in enumerate(loads)
    ]
    for i in range(n_pick):
        load = pltpu.make_async_copy(owns[i].at[WIDTH:, :], picks.at[i], pick_sems.at[0, i])
        loads.append(load)
    def copies(p, slot):
        moves = []
        for h in range(PER):
            j = jnp.minimum(begin + PER * p + h, end - 1)
            rows = pl.ds(pl.multiple_of(j * BE, BE), BE)
            moves.append(
                pltpu.make_async_copy(rad_hbm.at[rows, :], rbuf.at[slot, h], sems.at[0, h, slot])
            )
            moves.append(
                pltpu.make_async_copy(tgt_hbm.at[rows, :], tbuf.at[slot, h], sems.at[1, h, slot])
            )
        return moves

    def fetch(p):
        @pl.when(p < groups)
        def _():
            for copy in copies(p, p & 1):
                copy.start()

    def arrive(p):
        @pl.when(p < groups)
        def _():
            for copy in copies(p, p & 1):
                copy.wait()

    fetch(0)
    for load in loads:
        load.start()
    part_load = pltpu.make_async_copy(part_hbm, acc_ref, part_sem)
    part_load.start()
    rout_t = rout_ref[...]
    atom_id = iota((BE, TE), 1).astype(F32)
    row_id = iota((CHUNK, TE), 0)

    def gather(p):
        for h in range(PER):
            j = begin + PER * p + h
            off = jnp.where(j < end, 0.0, 4096.0)
            j = jnp.maximum(jnp.minimum(j, end - 1), 0)
            c = jnp.clip(span_ref[2 * nb, j] - low, 0, count - 1)
            gate = lax.dot_general(
                rout_t, rbuf[p & 1, h], (((1,), (1,)), ((), ())), preferred_element_type=F32
            )
            pick = jnp.concatenate(
                [
                    as_bf16(row_id == src_ref[pl.ds(j * (BE // TE) + q, 1), :])
                    for q in range(BE // TE)
                ],
                axis=1,
            )
            rows = dot(tables[c], pick)
            for k in range(K):
                message = rows[cols(k), :] * gate[cols(degree_of[k]), :]
                message_ref[cols(k), h * BE : (h + 1) * BE] = message.astype(BF16)
            tgt = tbuf[p & 1, h].astype(F32) + off
            for q in range(ATOM_DEV // TE):
                land_ref[h * BE : (h + 1) * BE, q * TE : (q + 1) * TE] = as_bf16(
                    tgt == atom_id + float(q * TE)
                )

    def add_up():
        acc_ref[...] += dot(message_ref[...], land_ref[...])

    for load in loads:
        load.wait()
    saves = []
    for i in range(n_pick):
        pick_rows(tables[i], picks[i], near.at[i], far.at[i])
    for i in range(n_pick):
        for side, (src, dst) in enumerate(((near, near_hbm), (far, far_hbm))):
            save = pltpu.make_async_copy(src.at[i], dst.at[i], pick_sems.at[1 + side, i])
            save.start()
            saves.append(save)
    arrive(0)
    fetch(1)
    gather(0)
    part_load.wait()

    def step(p, carry):
        arrive(p + 1)
        fetch(p + 2)
        add_up()
        gather(p + 1)
        return carry

    lax.fori_loop(0, groups - 1, step, 0)

    @pl.when(groups > 0)
    def _():
        add_up()

    for save in saves:
        save.wait()
    if final:
        for k in range(K):
            out_ref[:, cols(k)] = (inv_scale * acc_ref[cols(k), :]).T.astype(BF16)


def shape(dims, kind):
    return jax.ShapeDtypeStruct(dims, kind)


def cost(flops, size):
    return pl.CostEstimate(flops=int(flops), bytes_accessed=int(size), transcendentals=0)


def body(
    embedding,
    ghost_index,
    tile_count,
    edge_source,
    edge_target,
    edge_features,
    radial_in,
    radial_out,
    mix_weight,
):
    n_dom, n_tile = lax.axis_size("dom"), lax.axis_size("tile")
    tiles = edge_source.shape[0] // TE
    nb = 2 * n_tile
    slots = (tiles * TE // BE + nb) * BE
    count = tile_count
    source = edge_source.reshape(tiles, TE)
    target = edge_target.reshape(tiles, TE)
    hbm = pl.BlockSpec(memory_space=pl.ANY)

    mixed = pl.pallas_call(
        mix_kernel,
        out_shape=shape((WIDTH + EXTRA, ATOM_DEV), BF16),
        in_specs=[vmem(), vmem(), vmem()],
        out_specs=vmem(),
        compiler_params=PARAMS,
        cost_estimate=cost(256 * 256 * 1152, 2e6),
        name="mix",
    )(embedding, mix_weight, ghost_index.reshape(1, ATOM_DEV))
    ring = [(t, (t + 2) % n_tile) for t in range(n_tile)]
    back = [(target, source) for source, target in ring]
    flip = [(t, t ^ 1) for t in range(n_tile)]
    near = [(i, i ^ 1) for i in range(n_dom)]
    far = [(i, i + 1) for i in range(1, n_dom - 1, 2)]
    far += [(j, i) for i, j in far]
    n_ring = n_tile // 2
    half = n_tile // 2

    pos, span = pl.pallas_call(
        functools.partial(rank_kernel, slots=slots),
        out_shape=(shape((tiles, TE), I32), shape((3 * nb, TE), I32)),
        in_specs=[smem(), vmem()],
        out_specs=(vmem(), vmem()),
        scratch_shapes=[
            pltpu.VMEM((tiles * nb, TE), BF16),
            pltpu.VMEM((tiles * nb, 2 * TE), F32),
        ],
        compiler_params=PARAMS,
        cost_estimate=cost(4e9, 1e6),
        name="rank",
    )(count, source)
    radial, radial_sum = pl.pallas_call(
        radial_kernel,
        out_shape=(shape((tiles * TE, C), BF16), shape((ATOM_DEV, C), F32)),
        in_specs=[smem(), vmem(), vmem(), vmem()],
        out_specs=(vmem(), vmem()),
        compiler_params=PARAMS,
        cost_estimate=cost(10e9, 6e6),
        name="radial",
    )(count, target, edge_features, radial_in)

    def place(radial):
        return pl.pallas_call(
            place_kernel,
            out_shape=(
                shape((slots, C), BF16),
                shape((slots, C), BF16),
                shape((slots // TE, TE), I32),
            ),
            in_specs=[smem(), smem(), smem(), vmem(), vmem(), hbm],
            out_specs=(hbm, hbm, vmem()),
            scratch_shapes=[
                pltpu.VMEM((2 * slots + 8, C), F32),
                pltpu.VMEM((2 * TE, C), F32),
                pltpu.VMEM((2 * TE, C), F32),
                pltpu.VMEM((slots, C), BF16),
                pltpu.VMEM((slots, C), BF16),
                pltpu.VMEM((tiles * TE, C), BF16),
                pltpu.SemaphoreType.DMA((2,)),
                pltpu.SemaphoreType.DMA((2, slots // BE)),
            ],
            compiler_params=PARAMS,
            cost_estimate=cost(20e9, 12e6),
            name="place",
        )(count, pos, span, source, target, radial)

    def pick(blocks):
        n = len(blocks)
        near_rows, far_rows = pl.pallas_call(
            functools.partial(pick_kernel, n=n),
            out_shape=(shape((n, WIDTH, GHOST), BF16),) * 2,
            in_specs=[hbm] * n,
            out_specs=(hbm, hbm),
            scratch_shapes=[
                pltpu.VMEM((n, WIDTH + EXTRA, ATOM_DEV), BF16),
                pltpu.VMEM((n, WIDTH, GHOST), BF16),
                pltpu.VMEM((n, WIDTH, GHOST), BF16),
                pltpu.SemaphoreType.DMA((3, n)),
            ],
            compiler_params=PARAMS,
            cost_estimate=cost(2e8, 4e5),
            name="pick",
        )(*blocks)
        return near_rows, far_rows

    base, rout_t = pl.pallas_call(
        base_kernel,
        out_shape=(shape((WIDTH, ATOM_DEV), F32), shape((3 * C, C), BF16)),
        in_specs=[vmem()] * 4,
        out_specs=(vmem(), vmem()),
        compiler_params=PARAMS,
        cost_estimate=cost(1e9, 2e6),
        name="base",
    )(radial_sum, radial_out, embedding, mix_weight)

    def main(low, ghosts, owns, part, name, n_pick=0, final=False):
        dims, kind = ((ATOM_DEV, WIDTH), BF16) if final else ((WIDTH, ATOM_DEV), F32)
        n_ghost = half if ghosts else 0
        count_all = n_ghost + len(owns)
        return pl.pallas_call(
            functools.partial(
                main_kernel,
                low=low,
                n_ghost=n_ghost,
                n_own=len(owns),
                n_pick=n_pick,
                final=final,
            ),
            out_shape=(shape(dims, kind),)
            + ((shape((n_pick, WIDTH, GHOST), BF16),) * 2 if n_pick else ()),
            in_specs=[smem()] + [hbm] * (len(ghosts) + len(owns) + 3) + [vmem()] * 2,
            out_specs=(vmem(),) + ((hbm, hbm) if n_pick else ()),
            scratch_shapes=[
                pltpu.VMEM((2, PER, BE, C), BF16),
                pltpu.VMEM((2, PER, BE, C), BF16),
                pltpu.VMEM((PER * BE, ATOM_DEV), BF16),
                pltpu.VMEM((WIDTH, PER * BE), BF16),
                pltpu.VMEM((count_all, WIDTH, ATOM_DEV), BF16),
                pltpu.SemaphoreType.DMA((2, PER, 2)),
                pltpu.SemaphoreType.DMA((2 * n_ghost + len(owns),)),
                pltpu.SemaphoreType.DMA,
            ]
            + ([pltpu.VMEM((WIDTH, ATOM_DEV), F32)] if final else [])
            + (
                [
                    pltpu.VMEM((n_pick, EXTRA, ATOM_DEV), BF16),
                    pltpu.VMEM((n_pick, WIDTH, GHOST), BF16),
                    pltpu.VMEM((n_pick, WIDTH, GHOST), BF16),
                    pltpu.SemaphoreType.DMA((3, n_pick)),
                ]
                if n_pick
                else []
            ),
            compiler_params=PARAMS,
            cost_estimate=cost(1e8 * count_all, 1e5 * count_all),
            name=name,
        )(span, *ghosts, *owns, radial_sorted, target_sorted, part, source_sorted, rout_t)

    together = lax.optimization_barrier

    def to_ring(rows):
        return lax.ppermute(rows, "tile", ring)

    def to_flip(rows):
        return lax.ppermute(rows, "tile", flip)

    def to_back(rows):
        return lax.ppermute(rows, "tile", back)

    few = half // 2
    ahead = [mixed, to_ring(mixed)]
    flips = [to_flip(together((mixed, span))[0])]
    ahead[1], radial, base, own = together((ahead[1], radial, base, mixed))
    while len(ahead) <= few:
        ahead.append(to_ring(ahead[-1]))
    flips.append(to_flip(ahead[1]))
    behind = [to_back(own)]
    while len(behind) < n_ring - 1 - few:
        behind.append(to_back(behind[-1]))
    radial_sorted, target_sorted, source_sorted = place(radial)
    ahead[2], flips[0], radial_sorted = together((ahead[2], flips[0], radial_sorted))
    rings = ahead + behind
    flips += [to_flip(rows) for rows in ahead[2:]]
    other = flips[0]
    for _ in behind:
        other = to_back(other)
        flips.append(other)
    owns = [rows for pair in zip(rings, flips) for rows in pair]

    def exchange_after(blocks, part):
        near_rows, far_rows = pick(blocks)
        near_rows, part = together((near_rows, part))
        return [lax.ppermute(near_rows, "dom", near), lax.ppermute(far_rows, "dom", far)], part

    ghosts_a, base = exchange_after(owns[:half], base)
    (part,) = main(0, [], owns[:half] + rings[few:], base, "main_one")
    last = owns[half:]
    last[0], part = together((last[0], part))
    ghosts_b, part = exchange_after(last, part)
    (part,) = main(half + few, ghosts_a, flips[few:], part, "main_two")
    return main(n_tile + half, ghosts_b, [], part, "main_three", final=True)[0]


def solution(mesh):
    both = ("dom", "tile")
    return jax.shard_map(
        body,
        mesh=mesh,
        in_specs=(
            P(both, None),
            P(both),
            P("dom", None),
            P(both),
            P(both),
            P(both, None),
            P(),
            P(),
            P(),
        ),
        out_specs=P(both, None),
        check_vma=False,
    )
```

```python
import functools
import jax
import jax.numpy as jnp
from jax import lax
from jax.experimental import pallas as pl
from jax.experimental.pallas import tpu as pltpu
from jax.sharding import PartitionSpec as P

C = 128
K = 9
ATOM_DEV = 256
GHOST = 128
TE = 128
BE = 256
CHUNK = 256
CHUNK_BITS = 8
WIDTH = K * C
EXTRA = 16
PER = 4
degree_of = (0, 1, 1, 1, 2, 2, 2, 2, 2)
inv_scale = 0.125

F32 = jnp.float32
BF16 = jnp.bfloat16
I32 = jnp.int32

PARAMS = pltpu.CompilerParams(vmem_limit_bytes=64 * 1024 * 1024)


def vmem():
    return pl.BlockSpec(memory_space=pltpu.VMEM)


def smem():
    return pl.BlockSpec(memory_space=pltpu.SMEM)


def cols(k):
    return slice(k * C, (k + 1) * C)


def iota(shape, dim):
    return lax.broadcasted_iota(I32, shape, dim)


def as_bf16(mask):
    return jnp.where(mask, 1.0, 0.0).astype(BF16)


def dot(a, b):
    return jnp.dot(a, b, preferred_element_type=F32)


def mix_kernel(x_ref, mix_ref, pick_ref, mixed_ref):
    for k in range(K):
        mixed = dot(x_ref[:, cols(k)], mix_ref[degree_of[k], :C])
        mixed_ref[cols(k), :] = mixed.T.astype(BF16)
    picks = jnp.broadcast_to(pick_ref[...].astype(F32), (EXTRA, ATOM_DEV))
    mixed_ref[WIDTH:, :] = picks.astype(BF16)


def pick_rows(table, picks, near_ref, far_ref):
    even = (lax.axis_index("dom") & 1) == 0
    picks = picks.astype(F32)[:1, :].astype(I32)
    down, up = picks[:, :GHOST], picks[:, GHOST:]
    row_id = iota((ATOM_DEV, GHOST), 0)
    chosen = jnp.concatenate(
        [
            as_bf16(row_id == jnp.where(even, up, down)),
            as_bf16(row_id == jnp.where(even, down, up)),
        ],
        axis=1,
    )
    rows = dot(table, chosen).astype(BF16)
    near_ref[...] = rows[:, :GHOST]
    far_ref[...] = rows[:, GHOST:]


def pick_kernel(*refs, n):
    blocks, refs = refs[:n], refs[n:]
    near_hbm, far_hbm, inside, near, far, sems = refs
    loads = [
        pltpu.make_async_copy(block, inside.at[i], sems.at[0, i]) for i, block in enumerate(blocks)
    ]
    saves = []
    for load in loads:
        load.start()
    for load in loads:
        load.wait()
    for i in range(n):
        pick_rows(inside[i, :WIDTH, :], inside[i, WIDTH:, :], near.at[i], far.at[i])
    for i in range(n):
        for side, (src, dst) in enumerate(((near, near_hbm), (far, far_hbm))):
            save = pltpu.make_async_copy(src.at[i], dst.at[i], sems.at[1 + side, i])
            save.start()
            saves.append(save)
    for save in saves:
        save.wait()


def base_kernel(rsum_ref, rout_ref, x_ref, mix_ref, base_ref, rout_t_ref):
    rout = rout_ref[...].astype(F32)
    rout_t_ref[...] = rout.T.astype(BF16)
    gate_sum = jnp.dot(
        rsum_ref[...], rout, preferred_element_type=F32, precision=lax.Precision.HIGHEST
    )
    for k in range(K):
        own = dot(x_ref[:, cols(k)], mix_ref[degree_of[k], C:])
        base_ref[cols(k), :] = (own * gate_sum[:, cols(degree_of[k])]).T


def live_tiles(count_ref):
    return count_ref[0, lax.axis_index("tile")]


def rank_kernel(count_ref, src_ref, pos_ref, span_ref, oh_ref, cum_ref, *, slots):
    tiles = src_ref.shape[0]
    nb = span_ref.shape[0] // 3
    count = live_tiles(count_ref)
    half, few = nb // 4, nb // 8
    order = iota((nb, TE), 0)
    ghost = ((order >= half + few) & (order < 2 * half + few)) | (order >= 3 * half)
    index = order
    index = jnp.where(order >= half, half + 2 * (order - half), index)
    index = jnp.where(order >= half + few, order - (half + few), index)
    index = jnp.where(order >= 2 * half + few, half + 2 * (order - (2 * half + few)) + 1, index)
    index = jnp.where(order >= 3 * half, order - 2 * half, index)
    tile_pos = lax.axis_index("tile")
    step = index >> 1
    ahead = half // 2
    ring_pos = (tile_pos >> 1) + jnp.where(step <= ahead, -step, step - ahead)
    ring_pos = jnp.where(ring_pos < 0, ring_pos + half, ring_pos)
    ring_pos = jnp.where(ring_pos >= half, ring_pos - half, ring_pos)
    label = 2 * (2 * ring_pos + ((tile_pos & 1) ^ (index & 1))) + jnp.where(ghost, 1, 0)

    def mark(t, carry):
        bucket = src_ref[pl.ds(t, 1), :] >> CHUNK_BITS
        bucket = jnp.where(t < count, bucket, -1)
        oh_ref[pl.ds(pl.multiple_of(t * nb, nb), nb), :] = as_bf16(label == bucket)
        return carry

    lax.fori_loop(0, tiles, mark, 0, unroll=8)
    upto = as_bf16(iota((TE, TE), 0) <= iota((TE, TE), 1))
    both = jnp.concatenate([upto, jnp.ones((TE, TE), BF16)], axis=1)
    step = 256
    for r in range(0, tiles * nb, step):
        cum_ref[r : r + step, :] = dot(oh_ref[r : r + step, :], both)

    def add(t, total):
        return total + cum_ref[pl.ds(pl.multiple_of(t * nb, nb), nb), TE:]

    total = lax.fori_loop(0, tiles, add, jnp.zeros((nb, TE), F32), unroll=8)
    blocks = jnp.floor((total + (BE - 1)) * (1.0 / BE))
    below = as_bf16(iota((nb, nb), 1) < iota((nb, nb), 0))
    first = dot(below, blocks.astype(BF16))
    span_ref[:nb, :] = first.astype(I32)
    span_ref[nb : 2 * nb, :] = blocks.astype(I32)
    passed = jnp.where(iota((nb, TE), 1).astype(F32) >= first + blocks, 1.0, 0.0)
    chunk_of = jnp.minimum(jnp.sum(passed, axis=0, keepdims=True), nb - 1.0)
    span_ref[2 * nb :, :] = jnp.broadcast_to(chunk_of, (nb, TE)).astype(I32)

    def place(t, run):
        rows = pl.ds(pl.multiple_of(t * nb, nb), nb)
        oh = oh_ref[rows, :].astype(F32)
        value = oh * (cum_ref[rows, :TE] + run)
        place_of = jnp.sum(value, axis=0, keepdims=True).astype(I32)
        pos_ref[pl.ds(t, 1), :] = jnp.where(t < count, 2 * place_of, 2 * slots)
        return run + cum_ref[rows, TE:]

    lax.fori_loop(0, tiles, place, first * BE - 1.0, unroll=8)


def radial_kernel(count_ref, tgt_ref, feat_hbm, rin_ref, rad_hbm, rsum_ref, feat_ref, rad_ref, sems):
    tiles = tgt_ref.shape[0]
    count = live_tiles(count_ref)
    rsum_ref[...] = jnp.zeros_like(rsum_ref)
    group = 8
    atom_id = iota((ATOM_DEV, TE), 0)

    def rows_of(i):
        return pl.ds(pl.multiple_of(i * (group * TE), group * TE), group * TE)

    def load(i):
        rows = rows_of(i)
        return pltpu.make_async_copy(feat_hbm.at[rows, :], feat_ref.at[rows, :], sems.at[0, i])

    def save(i):
        rows = rows_of(i)
        return pltpu.make_async_copy(rad_ref.at[rows, :], rad_hbm.at[rows, :], sems.at[1, i])

    def begin(i, carry):
        load(i).start()
        return carry

    def end(i, carry):
        save(i).wait()
        return carry

    def hidden_layer(i):
        load(i).wait()
        hidden = 0.5 * dot(feat_ref[rows_of(i), :], rin_ref[...])
        rad_ref[rows_of(i), :] = (hidden + hidden * jnp.tanh(hidden)).astype(BF16)
        save(i).start()

    def add_up(i):
        land = []
        for q in range(group):
            t = i * group + q
            tgt = jnp.where(t < count, tgt_ref[pl.ds(t, 1), :], -1)
            land.append(as_bf16(atom_id == tgt))
        rsum_ref[...] += dot(jnp.concatenate(land, axis=1), rad_ref[rows_of(i), :])

    groups = (count + group - 1) // group
    lax.fori_loop(0, groups, begin, 0)
    hidden_layer(0)

    def step(i, carry):
        add_up(i)
        hidden_layer(i + 1)
        return carry

    lax.fori_loop(0, groups - 1, step, 0)
    add_up(groups - 1)
    lax.fori_loop(0, groups, end, 0)


def place_kernel(
    count_ref,
    pos_ref,
    span_ref,
    src_ref,
    tgt_ref,
    rin_hbm,
    rad_hbm,
    tgt_hbm,
    srcs_ref,
    pairs,
    even,
    odd,
    rad_out,
    tgt_out,
    rin_ref,
    rin_sems,
    sems,
):
    tiles = src_ref.shape[0]
    head = min(16, tiles) * TE
    loads = [
        pltpu.make_async_copy(rin_hbm.at[rows, :], rin_ref.at[rows, :], rin_sems.at[i])
        for i, rows in enumerate((pl.ds(0, head), pl.ds(head, tiles * TE - head)))
    ]
    for load in loads:
        load.start()
    nb = span_ref.shape[0] // 3
    count = live_tiles(count_ref)
    flip = jnp.where((lax.axis_index("dom") & 1) == 0, GHOST, 0)
    blank = jnp.where((iota((2 * BE, C), 0) & 1) == 1, -1.0, 0.0)

    def clear(b, carry):
        blocks = span_ref[nb + b, 0]

        @pl.when(blocks > 0)
        def _():
            last = pl.multiple_of((span_ref[b, 0] + blocks - 1) * (2 * BE), 2 * BE)
            pairs[pl.ds(last, 2 * BE), :] = blank

        return carry

    lax.fori_loop(0, nb, clear, 0)
    eye = iota((TE, TE), 0) == iota((TE, TE), 1)
    spread = jnp.concatenate(
        [jnp.ones((TE, C), BF16), jnp.full((TE, C), float(CHUNK), BF16)], axis=0
    )

    def compute(t, out):
        t = jnp.minimum(t, tiles - 1)
        rows = pl.ds(pl.multiple_of(t * TE, TE), TE)
        out[pl.ds(0, TE, stride=2), :] = rin_ref[rows, :].astype(F32)
        src = src_ref[pl.ds(t, 1), :]
        src = (src & (CHUNK - 1)) ^ jnp.where((src & CHUNK) != 0, flip, 0)
        tgt = tgt_ref[pl.ds(t, 1), :]
        diag_s = jnp.where(eye, src.astype(F32), 0.0).astype(BF16)
        diag_t = jnp.where(eye, tgt.astype(F32), 0.0).astype(BF16)
        code = dot(jnp.concatenate([diag_s, diag_t], axis=1), spread)
        out[pl.ds(1, TE, stride=2), :] = code

    def scatter(t, data):
        for e in range(TE):
            pairs[pl.ds(pos_ref[t, e], 2), :] = data[2 * e : 2 * e + 2, :]

    loads[0].wait()
    compute(0, even)

    def step(i, carry):
        compute(2 * i + 1, odd)
        scatter(2 * i, even)
        compute(2 * i + 2, even)
        scatter(2 * i + 1, odd)
        return carry

    steps = (count + 1) // 2
    split = jnp.minimum(steps, head // (2 * TE) - 1)
    lax.fori_loop(0, split, step, 0)
    loads[1].wait()
    lax.fori_loop(split, steps, step, 0)

    def saves(j):
        rows = pl.ds(pl.multiple_of(j * BE, BE), BE)
        return (
            pltpu.make_async_copy(rad_out.at[rows, :], rad_hbm.at[rows, :], sems.at[0, j]),
            pltpu.make_async_copy(tgt_out.at[rows, :], tgt_hbm.at[rows, :], sems.at[1, j]),
        )

    def finish(j, carry):
        for h in range(BE // TE):
            row = j * (BE // TE) + h
            rows = pl.ds(pl.multiple_of(row * TE, TE), TE)
            base = pl.multiple_of(row * (2 * TE), 2 * TE)
            rad_out[rows, :] = pairs[pl.ds(base, TE, stride=2), :].astype(BF16)
            code = pairs[pl.ds(base + 1, TE, stride=2), :]
            tgt = jnp.floor(code * (1.0 / CHUNK))
            tgt_out[rows, :] = tgt.astype(BF16)
            src = jnp.where(eye, code - CHUNK * tgt, 0.0)
            srcs_ref[pl.ds(row, 1), :] = jnp.sum(src, axis=0, keepdims=True).astype(I32)
        for save in saves(j):
            save.start()
        return carry

    used = span_ref[nb - 1, 0] + span_ref[2 * nb - 1, 0]
    lax.fori_loop(0, used, finish, 0)

    def drain(j, carry):
        for save in saves(j):
            save.wait()
        return carry

    lax.fori_loop(0, used, drain, 0)


def main_kernel(*refs, low, n_ghost, n_own, n_pick, final):
    span_ref, *refs = refs
    ghosts, refs = refs[: 2 * (n_ghost > 0)], refs[2 * (n_ghost > 0) :]
    owns, refs = refs[:n_own], refs[n_own:]
    rad_hbm, tgt_hbm, part_hbm, src_ref, rout_ref, *refs = refs
    out_ref, *refs = refs
    if n_pick:
        near_hbm, far_hbm, *refs = refs
    rbuf, tbuf, land_ref, message_ref, tables, sems, table_sems, part_sem, *refs = refs
    acc_ref = refs[0] if final else out_ref
    if n_pick:
        picks, near, far, pick_sems = refs
    count = n_ghost + n_own
    nb = span_ref.shape[0] // 3
    begin = span_ref[low, 0]
    end = span_ref[low + count - 1, 0] + span_ref[nb + low + count - 1, 0]
    groups = (end - begin + PER - 1) // PER

    loads = []
    for i, own in enumerate(owns):
        loads.append((own.at[:WIDTH, :], tables.at[n_ghost + i]))
    for i in range(n_ghost):
        for side in range(2):
            half = tables.at[i, :, side * GHOST : (side + 1) * GHOST]
            loads.append((ghosts[side].at[i], half))
    loads = [
        pltpu.make_async_copy(src, dst, table_sems.at[i]) for i, (src, dst) in enumerate(loads)
    ]
    for i in range(n_pick):
        load = pltpu.make_async_copy(owns[i].at[WIDTH:, :], picks.at[i], pick_sems.at[0, i])
        loads.append(load)
    def copies(p, slot):
        moves = []
        for h in range(PER):
            j = jnp.minimum(begin + PER * p + h, end - 1)
            rows = pl.ds(pl.multiple_of(j * BE, BE), BE)
            moves.append(
                pltpu.make_async_copy(rad_hbm.at[rows, :], rbuf.at[slot, h], sems.at[0, h, slot])
            )
            moves.append(
                pltpu.make_async_copy(tgt_hbm.at[rows, :], tbuf.at[slot, h], sems.at[1, h, slot])
            )
        return moves

    def fetch(p):
        @pl.when(p < groups)
        def _():
            for copy in copies(p, p & 1):
                copy.start()

    def arrive(p):
        @pl.when(p < groups)
        def _():
            for copy in copies(p, p & 1):
                copy.wait()

    fetch(0)
    for load in loads:
        load.start()
    part_load = pltpu.make_async_copy(part_hbm, acc_ref, part_sem)
    part_load.start()
    rout_t = rout_ref[...]
    atom_id = iota((BE, TE), 1).astype(F32)
    row_id = iota((CHUNK, TE), 0)

    def gather(p):
        for h in range(PER):
            j = begin + PER * p + h
            off = jnp.where(j < end, 0.0, 4096.0)
            j = jnp.maximum(jnp.minimum(j, end - 1), 0)
            c = jnp.clip(span_ref[2 * nb, j] - low, 0, count - 1)
            gate = lax.dot_general(
                rout_t, rbuf[p & 1, h], (((1,), (1,)), ((), ())), preferred_element_type=F32
            )
            pick = jnp.concatenate(
                [
                    as_bf16(row_id == src_ref[pl.ds(j * (BE // TE) + q, 1), :])
                    for q in range(BE // TE)
                ],
                axis=1,
            )
            rows = dot(tables[c], pick)
            for k in range(K):
                message = rows[cols(k), :] * gate[cols(degree_of[k]), :]
                message_ref[cols(k), h * BE : (h + 1) * BE] = message.astype(BF16)
            tgt = tbuf[p & 1, h].astype(F32) + off
            for q in range(ATOM_DEV // TE):
                land_ref[h * BE : (h + 1) * BE, q * TE : (q + 1) * TE] = as_bf16(
                    tgt == atom_id + float(q * TE)
                )

    def add_up():
        acc_ref[...] += dot(message_ref[...], land_ref[...])

    for load in loads:
        load.wait()
    saves = []
    for i in range(n_pick):
        pick_rows(tables[i], picks[i], near.at[i], far.at[i])
    for i in range(n_pick):
        for side, (src, dst) in enumerate(((near, near_hbm), (far, far_hbm))):
            save = pltpu.make_async_copy(src.at[i], dst.at[i], pick_sems.at[1 + side, i])
            save.start()
            saves.append(save)
    arrive(0)
    fetch(1)
    gather(0)
    part_load.wait()

    def step(p, carry):
        arrive(p + 1)
        fetch(p + 2)
        add_up()
        gather(p + 1)
        return carry

    lax.fori_loop(0, groups - 1, step, 0)

    @pl.when(groups > 0)
    def _():
        add_up()

    for save in saves:
        save.wait()
    if final:
        for k in range(K):
            out_ref[:, cols(k)] = (inv_scale * acc_ref[cols(k), :]).T.astype(BF16)


def shape(dims, kind):
    return jax.ShapeDtypeStruct(dims, kind)


def cost(flops, size):
    return pl.CostEstimate(flops=int(flops), bytes_accessed=int(size), transcendentals=0)


def body(
    embedding,
    ghost_index,
    tile_count,
    edge_source,
    edge_target,
    edge_features,
    radial_in,
    radial_out,
    mix_weight,
):
    n_dom, n_tile = lax.axis_size("dom"), lax.axis_size("tile")
    tiles = edge_source.shape[0] // TE
    nb = 2 * n_tile
    slots = (tiles * TE // BE + nb) * BE
    count = tile_count
    source = edge_source.reshape(tiles, TE)
    target = edge_target.reshape(tiles, TE)
    hbm = pl.BlockSpec(memory_space=pl.ANY)

    mixed = pl.pallas_call(
        mix_kernel,
        out_shape=shape((WIDTH + EXTRA, ATOM_DEV), BF16),
        in_specs=[vmem(), vmem(), vmem()],
        out_specs=vmem(),
        compiler_params=PARAMS,
        cost_estimate=cost(256 * 256 * 1152, 2e6),
        name="mix",
    )(embedding, mix_weight, ghost_index.reshape(1, ATOM_DEV))
    ring = [(t, (t + 2) % n_tile) for t in range(n_tile)]
    back = [(target, source) for source, target in ring]
    flip = [(t, t ^ 1) for t in range(n_tile)]
    near = [(i, i ^ 1) for i in range(n_dom)]
    far = [(i, i + 1) for i in range(1, n_dom - 1, 2)]
    far += [(j, i) for i, j in far]
    n_ring = n_tile // 2
    half = n_tile // 2

    pos, span = pl.pallas_call(
        functools.partial(rank_kernel, slots=slots),
        out_shape=(shape((tiles, TE), I32), shape((3 * nb, TE), I32)),
        in_specs=[smem(), vmem()],
        out_specs=(vmem(), vmem()),
        scratch_shapes=[
            pltpu.VMEM((tiles * nb, TE), BF16),
            pltpu.VMEM((tiles * nb, 2 * TE), F32),
        ],
        compiler_params=PARAMS,
        cost_estimate=cost(4e9, 1e6),
        name="rank",
    )(count, source)
    radial, radial_sum = pl.pallas_call(
        radial_kernel,
        out_shape=(shape((tiles * TE, C), BF16), shape((ATOM_DEV, C), F32)),
        in_specs=[smem(), vmem(), hbm, vmem()],
        out_specs=(hbm, vmem()),
        scratch_shapes=[
            pltpu.VMEM((tiles * TE, C), BF16),
            pltpu.VMEM((tiles * TE, C), BF16),
            pltpu.SemaphoreType.DMA((2, tiles // 8)),
        ],
        compiler_params=PARAMS,
        cost_estimate=cost(10e9, 6e6),
        name="radial",
    )(count, target, edge_features, radial_in)

    def place(radial):
        return pl.pallas_call(
            place_kernel,
            out_shape=(
                shape((slots, C), BF16),
                shape((slots, C), BF16),
                shape((slots // TE, TE), I32),
            ),
            in_specs=[smem(), smem(), smem(), vmem(), vmem(), hbm],
            out_specs=(hbm, hbm, vmem()),
            scratch_shapes=[
                pltpu.VMEM((2 * slots + 8, C), F32),
                pltpu.VMEM((2 * TE, C), F32),
                pltpu.VMEM((2 * TE, C), F32),
                pltpu.VMEM((slots, C), BF16),
                pltpu.VMEM((slots, C), BF16),
                pltpu.VMEM((tiles * TE, C), BF16),
                pltpu.SemaphoreType.DMA((2,)),
                pltpu.SemaphoreType.DMA((2, slots // BE)),
            ],
            compiler_params=PARAMS,
            cost_estimate=cost(20e9, 12e6),
            name="place",
        )(count, pos, span, source, target, radial)

    def pick(blocks):
        n = len(blocks)
        near_rows, far_rows = pl.pallas_call(
            functools.partial(pick_kernel, n=n),
            out_shape=(shape((n, WIDTH, GHOST), BF16),) * 2,
            in_specs=[hbm] * n,
            out_specs=(hbm, hbm),
            scratch_shapes=[
                pltpu.VMEM((n, WIDTH + EXTRA, ATOM_DEV), BF16),
                pltpu.VMEM((n, WIDTH, GHOST), BF16),
                pltpu.VMEM((n, WIDTH, GHOST), BF16),
                pltpu.SemaphoreType.DMA((3, n)),
            ],
            compiler_params=PARAMS,
            cost_estimate=cost(2e8, 4e5),
            name="pick",
        )(*blocks)
        return near_rows, far_rows

    base, rout_t = pl.pallas_call(
        base_kernel,
        out_shape=(shape((WIDTH, ATOM_DEV), F32), shape((3 * C, C), BF16)),
        in_specs=[vmem()] * 4,
        out_specs=(vmem(), vmem()),
        compiler_params=PARAMS,
        cost_estimate=cost(1e9, 2e6),
        name="base",
    )(radial_sum, radial_out, embedding, mix_weight)

    def main(low, ghosts, owns, part, name, n_pick=0, final=False):
        dims, kind = ((ATOM_DEV, WIDTH), BF16) if final else ((WIDTH, ATOM_DEV), F32)
        n_ghost = half if ghosts else 0
        count_all = n_ghost + len(owns)
        return pl.pallas_call(
            functools.partial(
                main_kernel,
                low=low,
                n_ghost=n_ghost,
                n_own=len(owns),
                n_pick=n_pick,
                final=final,
            ),
            out_shape=(shape(dims, kind),)
            + ((shape((n_pick, WIDTH, GHOST), BF16),) * 2 if n_pick else ()),
            in_specs=[smem()] + [hbm] * (len(ghosts) + len(owns) + 3) + [vmem()] * 2,
            out_specs=(vmem(),) + ((hbm, hbm) if n_pick else ()),
            scratch_shapes=[
                pltpu.VMEM((2, PER, BE, C), BF16),
                pltpu.VMEM((2, PER, BE, C), BF16),
                pltpu.VMEM((PER * BE, ATOM_DEV), BF16),
                pltpu.VMEM((WIDTH, PER * BE), BF16),
                pltpu.VMEM((count_all, WIDTH, ATOM_DEV), BF16),
                pltpu.SemaphoreType.DMA((2, PER, 2)),
                pltpu.SemaphoreType.DMA((2 * n_ghost + len(owns),)),
                pltpu.SemaphoreType.DMA,
            ]
            + ([pltpu.VMEM((WIDTH, ATOM_DEV), F32)] if final else [])
            + (
                [
                    pltpu.VMEM((n_pick, EXTRA, ATOM_DEV), BF16),
                    pltpu.VMEM((n_pick, WIDTH, GHOST), BF16),
                    pltpu.VMEM((n_pick, WIDTH, GHOST), BF16),
                    pltpu.SemaphoreType.DMA((3, n_pick)),
                ]
                if n_pick
                else []
            ),
            compiler_params=PARAMS,
            cost_estimate=cost(1e8 * count_all, 1e5 * count_all),
            name=name,
        )(span, *ghosts, *owns, radial_sorted, target_sorted, part, source_sorted, rout_t)

    together = lax.optimization_barrier

    def to_ring(rows):
        return lax.ppermute(rows, "tile", ring)

    def to_flip(rows):
        return lax.ppermute(rows, "tile", flip)

    def to_back(rows):
        return lax.ppermute(rows, "tile", back)

    few = half // 2
    ahead = [mixed, to_ring(mixed)]
    flips = [to_flip(together((mixed, span))[0])]
    ahead[1], radial, base, own = together((ahead[1], radial, base, mixed))
    while len(ahead) <= few:
        ahead.append(to_ring(ahead[-1]))
    flips.append(to_flip(ahead[1]))
    behind = [to_back(own)]
    while len(behind) < n_ring - 1 - few:
        behind.append(to_back(behind[-1]))
    radial_sorted, target_sorted, source_sorted = place(radial)
    ahead[2], flips[0], radial_sorted = together((ahead[2], flips[0], radial_sorted))
    rings = ahead + behind
    flips += [to_flip(rows) for rows in ahead[2:]]
    other = flips[0]
    for _ in behind:
        other = to_back(other)
        flips.append(other)
    owns = [rows for pair in zip(rings, flips) for rows in pair]

    def exchange_after(blocks, part):
        near_rows, far_rows = pick(blocks)
        near_rows, part = together((near_rows, part))
        return [lax.ppermute(near_rows, "dom", near), lax.ppermute(far_rows, "dom", far)], part

    ghosts_a, base = exchange_after(owns[:half], base)
    (part,) = main(0, [], owns[:half] + rings[few:], base, "main_one")
    last = owns[half:]
    last[0], part = together((last[0], part))
    ghosts_b, part = exchange_after(last, part)
    (part,) = main(half + few, ghosts_a, flips[few:], part, "main_two")
    return main(n_tile + half, ghosts_b, [], part, "main_three", final=True)[0]


def solution(mesh):
    both = ("dom", "tile")
    return jax.shard_map(
        body,
        mesh=mesh,
        in_specs=(
            P(both, None),
            P(both),
            P("dom", None),
            P(both),
            P(both),
            P(both, None),
            P(),
            P(),
            P(),
        ),
        out_specs=P(both, None),
        check_vma=False,
    )
```

```python
import functools
import jax
import jax.numpy as jnp
from jax import lax
from jax.experimental import pallas as pl
from jax.experimental.pallas import tpu as pltpu
from jax.sharding import PartitionSpec as P

C = 128
K = 9
ATOM_DEV = 256
GHOST = 128
TE = 128
BE = 256
CHUNK = 256
CHUNK_BITS = 8
WIDTH = K * C
EXTRA = 16
PER = 4
degree_of = (0, 1, 1, 1, 2, 2, 2, 2, 2)
inv_scale = 0.125

F32 = jnp.float32
BF16 = jnp.bfloat16
I32 = jnp.int32

PARAMS = pltpu.CompilerParams(vmem_limit_bytes=64 * 1024 * 1024)


def vmem():
    return pl.BlockSpec(memory_space=pltpu.VMEM)


def smem():
    return pl.BlockSpec(memory_space=pltpu.SMEM)


def cols(k):
    return slice(k * C, (k + 1) * C)


def iota(shape, dim):
    return lax.broadcasted_iota(I32, shape, dim)


def as_bf16(mask):
    return jnp.where(mask, 1.0, 0.0).astype(BF16)


def dot(a, b):
    return jnp.dot(a, b, preferred_element_type=F32)


def mix_kernel(x_ref, mix_ref, pick_ref, mixed_ref):
    for k in range(K):
        mixed = dot(x_ref[:, cols(k)], mix_ref[degree_of[k], :C])
        mixed_ref[cols(k), :] = mixed.T.astype(BF16)
    picks = jnp.broadcast_to(pick_ref[...].astype(F32), (EXTRA, ATOM_DEV))
    mixed_ref[WIDTH:, :] = picks.astype(BF16)


def pick_rows(table, picks, near_ref, far_ref):
    even = (lax.axis_index("dom") & 1) == 0
    picks = picks.astype(F32)[:1, :].astype(I32)
    down, up = picks[:, :GHOST], picks[:, GHOST:]
    row_id = iota((ATOM_DEV, GHOST), 0)
    chosen = jnp.concatenate(
        [
            as_bf16(row_id == jnp.where(even, up, down)),
            as_bf16(row_id == jnp.where(even, down, up)),
        ],
        axis=1,
    )
    rows = dot(table, chosen).astype(BF16)
    near_ref[...] = rows[:, :GHOST]
    far_ref[...] = rows[:, GHOST:]


def pick_kernel(*refs, n):
    blocks, refs = refs[:n], refs[n:]
    near_hbm, far_hbm, inside, near, far, sems = refs
    loads = [
        pltpu.make_async_copy(block, inside.at[i], sems.at[0, i]) for i, block in enumerate(blocks)
    ]
    saves = []
    for load in loads:
        load.start()
    for load in loads:
        load.wait()
    for i in range(n):
        pick_rows(inside[i, :WIDTH, :], inside[i, WIDTH:, :], near.at[i], far.at[i])
    for i in range(n):
        for side, (src, dst) in enumerate(((near, near_hbm), (far, far_hbm))):
            save = pltpu.make_async_copy(src.at[i], dst.at[i], sems.at[1 + side, i])
            save.start()
            saves.append(save)
    for save in saves:
        save.wait()


def base_kernel(rsum_ref, rout_ref, x_ref, mix_ref, base_ref, rout_t_ref):
    rout = rout_ref[...].astype(F32)
    rout_t_ref[...] = rout.T.astype(BF16)
    gate_sum = jnp.dot(
        rsum_ref[...], rout, preferred_element_type=F32, precision=lax.Precision.HIGHEST
    )
    for k in range(K):
        own = dot(x_ref[:, cols(k)], mix_ref[degree_of[k], C:])
        base_ref[cols(k), :] = (own * gate_sum[:, cols(degree_of[k])]).T


def live_tiles(count_ref):
    return count_ref[0, lax.axis_index("tile")]


def rank_kernel(count_ref, src_ref, pos_ref, span_ref, oh_ref, cum_ref, *, slots):
    tiles = src_ref.shape[0]
    nb = span_ref.shape[0] // 3
    count = live_tiles(count_ref)
    half, few = nb // 4, nb // 8
    order = iota((nb, TE), 0)
    ghost = ((order >= half + few) & (order < 2 * half + few)) | (order >= 3 * half)
    index = order
    index = jnp.where(order >= half, half + 2 * (order - half), index)
    index = jnp.where(order >= half + few, order - (half + few), index)
    index = jnp.where(order >= 2 * half + few, half + 2 * (order - (2 * half + few)) + 1, index)
    index = jnp.where(order >= 3 * half, order - 2 * half, index)
    tile_pos = lax.axis_index("tile")
    step = index >> 1
    ahead = half // 2
    ring_pos = (tile_pos >> 1) + jnp.where(step <= ahead, -step, step - ahead)
    ring_pos = jnp.where(ring_pos < 0, ring_pos + half, ring_pos)
    ring_pos = jnp.where(ring_pos >= half, ring_pos - half, ring_pos)
    label = 2 * (2 * ring_pos + ((tile_pos & 1) ^ (index & 1))) + jnp.where(ghost, 1, 0)

    def mark(t, carry):
        bucket = src_ref[pl.ds(t, 1), :] >> CHUNK_BITS
        bucket = jnp.where(t < count, bucket, -1)
        oh_ref[pl.ds(pl.multiple_of(t * nb, nb), nb), :] = as_bf16(label == bucket)
        return carry

    lax.fori_loop(0, tiles, mark, 0, unroll=8)
    upto = as_bf16(iota((TE, TE), 0) <= iota((TE, TE), 1))
    both = jnp.concatenate([upto, jnp.ones((TE, TE), BF16)], axis=1)
    step = 256
    for r in range(0, tiles * nb, step):
        cum_ref[r : r + step, :] = dot(oh_ref[r : r + step, :], both)

    def add(t, total):
        return total + cum_ref[pl.ds(pl.multiple_of(t * nb, nb), nb), TE:]

    total = lax.fori_loop(0, tiles, add, jnp.zeros((nb, TE), F32), unroll=8)
    blocks = jnp.floor((total + (BE - 1)) * (1.0 / BE))
    below = as_bf16(iota((nb, nb), 1) < iota((nb, nb), 0))
    first = dot(below, blocks.astype(BF16))
    span_ref[:nb, :] = first.astype(I32)
    span_ref[nb : 2 * nb, :] = blocks.astype(I32)
    passed = jnp.where(iota((nb, TE), 1).astype(F32) >= first + blocks, 1.0, 0.0)
    chunk_of = jnp.minimum(jnp.sum(passed, axis=0, keepdims=True), nb - 1.0)
    span_ref[2 * nb :, :] = jnp.broadcast_to(chunk_of, (nb, TE)).astype(I32)

    def place(t, run):
        rows = pl.ds(pl.multiple_of(t * nb, nb), nb)
        oh = oh_ref[rows, :].astype(F32)
        value = oh * (cum_ref[rows, :TE] + run)
        place_of = jnp.sum(value, axis=0, keepdims=True).astype(I32)
        pos_ref[pl.ds(t, 1), :] = jnp.where(t < count, 2 * place_of, 2 * slots)
        return run + cum_ref[rows, TE:]

    lax.fori_loop(0, tiles, place, first * BE - 1.0, unroll=8)


def radial_kernel(count_ref, tgt_ref, feat_ref, rin_ref, rad_ref, rsum_ref):
    tiles = tgt_ref.shape[0]
    count = live_tiles(count_ref)
    rsum_ref[...] = jnp.zeros_like(rsum_ref)
    group = 8
    atom_id = iota((ATOM_DEV, TE), 0)

    def rows_of(i):
        return pl.ds(pl.multiple_of(i * (group * TE), group * TE), group * TE)

    def hidden_layer(i):
        hidden = 0.5 * dot(feat_ref[rows_of(i), :], rin_ref[...])
        rad_ref[rows_of(i), :] = (hidden + hidden * jnp.tanh(hidden)).astype(BF16)

    def add_up(i):
        land = []
        for q in range(group):
            t = i * group + q
            tgt = jnp.where(t < count, tgt_ref[pl.ds(t, 1), :], -1)
            land.append(as_bf16(atom_id == tgt))
        rsum_ref[...] += dot(jnp.concatenate(land, axis=1), rad_ref[rows_of(i), :])

    hidden_layer(0)
    groups = (count + group - 1) // group

    def step(i, carry):
        add_up(i)
        hidden_layer(i + 1)
        return carry

    lax.fori_loop(0, groups - 1, step, 0)
    add_up(groups - 1)


def place_kernel(
    count_ref,
    pos_ref,
    span_ref,
    src_ref,
    tgt_ref,
    rin_hbm,
    rad_hbm,
    tgt_hbm,
    srcs_ref,
    pairs,
    even,
    odd,
    rad_out,
    tgt_out,
    rin_ref,
    rin_sems,
    sems,
):
    tiles = src_ref.shape[0]
    head = min(16, tiles) * TE
    loads = [
        pltpu.make_async_copy(rin_hbm.at[rows, :], rin_ref.at[rows, :], rin_sems.at[i])
        for i, rows in enumerate((pl.ds(0, head), pl.ds(head, tiles * TE - head)))
    ]
    for load in loads:
        load.start()
    nb = span_ref.shape[0] // 3
    count = live_tiles(count_ref)
    flip = jnp.where((lax.axis_index("dom") & 1) == 0, GHOST, 0)
    blank = jnp.where((iota((2 * BE, C), 0) & 1) == 1, -1.0, 0.0)

    def clear(b, carry):
        blocks = span_ref[nb + b, 0]

        @pl.when(blocks > 0)
        def _():
            last = pl.multiple_of((span_ref[b, 0] + blocks - 1) * (2 * BE), 2 * BE)
            pairs[pl.ds(last, 2 * BE), :] = blank

        return carry

    lax.fori_loop(0, nb, clear, 0)
    eye = iota((TE, TE), 0) == iota((TE, TE), 1)
    spread = jnp.concatenate(
        [jnp.ones((TE, C), BF16), jnp.full((TE, C), float(CHUNK), BF16)], axis=0
    )

    def compute(t, out):
        t = jnp.minimum(t, tiles - 1)
        rows = pl.ds(pl.multiple_of(t * TE, TE), TE)
        out[pl.ds(0, TE, stride=2), :] = rin_ref[rows, :].astype(F32)
        src = src_ref[pl.ds(t, 1), :]
        src = (src & (CHUNK - 1)) ^ jnp.where((src & CHUNK) != 0, flip, 0)
        tgt = tgt_ref[pl.ds(t, 1), :]
        diag_s = jnp.where(eye, src.astype(F32), 0.0).astype(BF16)
        diag_t = jnp.where(eye, tgt.astype(F32), 0.0).astype(BF16)
        code = dot(jnp.concatenate([diag_s, diag_t], axis=1), spread)
        out[pl.ds(1, TE, stride=2), :] = code

    def scatter(t, data):
        for e in range(TE):
            pairs[pl.ds(pos_ref[t, e], 2), :] = data[2 * e : 2 * e + 2, :]

    loads[0].wait()
    compute(0, even)

    def step(i, carry):
        compute(2 * i + 1, odd)
        scatter(2 * i, even)
        compute(2 * i + 2, even)
        scatter(2 * i + 1, odd)
        return carry

    steps = (count + 1) // 2
    split = jnp.minimum(steps, head // (2 * TE) - 1)
    lax.fori_loop(0, split, step, 0)
    loads[1].wait()
    lax.fori_loop(split, steps, step, 0)

    def saves(j):
        rows = pl.ds(pl.multiple_of(j * BE, BE), BE)
        return (
            pltpu.make_async_copy(rad_out.at[rows, :], rad_hbm.at[rows, :], sems.at[0, j]),
            pltpu.make_async_copy(tgt_out.at[rows, :], tgt_hbm.at[rows, :], sems.at[1, j]),
        )

    def finish(pair, carry):
        for h in range(2 * BE // TE):
            row = pair * (2 * BE // TE) + h
            rows = pl.ds(pl.multiple_of(row * TE, TE), TE)
            base = pl.multiple_of(row * (2 * TE), 2 * TE)
            rad_out[rows, :] = pairs[pl.ds(base, TE, stride=2), :].astype(BF16)
            code = pairs[pl.ds(base + 1, TE, stride=2), :]
            tgt = jnp.floor(code * (1.0 / CHUNK))
            tgt_out[rows, :] = tgt.astype(BF16)
            src = jnp.where(eye, code - CHUNK * tgt, 0.0)
            srcs_ref[pl.ds(row, 1), :] = jnp.sum(src, axis=0, keepdims=True).astype(I32)
        for h in range(2):
            for save in saves(2 * pair + h):
                save.start()
        return carry

    used = span_ref[nb - 1, 0] + span_ref[2 * nb - 1, 0]
    lax.fori_loop(0, (used + 1) // 2, finish, 0)

    def drain(j, carry):
        for save in saves(j):
            save.wait()
        return carry

    lax.fori_loop(0, 2 * ((used + 1) // 2), drain, 0)


def main_kernel(*refs, low, n_ghost, n_own, n_pick, final):
    span_ref, *refs = refs
    ghosts, refs = refs[: 2 * (n_ghost > 0)], refs[2 * (n_ghost > 0) :]
    owns, refs = refs[:n_own], refs[n_own:]
    rad_hbm, tgt_hbm, part_hbm, src_ref, rout_ref, *refs = refs
    out_ref, *refs = refs
    if n_pick:
        near_hbm, far_hbm, *refs = refs
    rbuf, tbuf, land_ref, message_ref, tables, sems, table_sems, part_sem, *refs = refs
    acc_ref = refs[0] if final else out_ref
    if n_pick:
        picks, near, far, pick_sems = refs
    count = n_ghost + n_own
    nb = span_ref.shape[0] // 3
    begin = span_ref[low, 0]
    end = span_ref[low + count - 1, 0] + span_ref[nb + low + count - 1, 0]
    groups = (end - begin + PER - 1) // PER

    loads = []
    for i, own in enumerate(owns):
        loads.append((own.at[:WIDTH, :], tables.at[n_ghost + i]))
    for i in range(n_ghost):
        for side in range(2):
            half = tables.at[i, :, side * GHOST : (side + 1) * GHOST]
            loads.append((ghosts[side].at[i], half))
    loads = [
        pltpu.make_async_copy(src, dst, table_sems.at[i]) for i, (src, dst) in enumerate(loads)
    ]
    for i in range(n_pick):
        load = pltpu.make_async_copy(owns[i].at[WIDTH:, :], picks.at[i], pick_sems.at[0, i])
        loads.append(load)
    def copies(p, slot):
        moves = []
        for h in range(PER):
            j = jnp.minimum(begin + PER * p + h, end - 1)
            rows = pl.ds(pl.multiple_of(j * BE, BE), BE)
            moves.append(
                pltpu.make_async_copy(rad_hbm.at[rows, :], rbuf.at[slot, h], sems.at[0, h, slot])
            )
            moves.append(
                pltpu.make_async_copy(tgt_hbm.at[rows, :], tbuf.at[slot, h], sems.at[1, h, slot])
            )
        return moves

    def fetch(p):
        @pl.when(p < groups)
        def _():
            for copy in copies(p, p & 1):
                copy.start()

    def arrive(p):
        @pl.when(p < groups)
        def _():
            for copy in copies(p, p & 1):
                copy.wait()

    fetch(0)
    for load in loads:
        load.start()
    part_load = pltpu.make_async_copy(part_hbm, acc_ref, part_sem)
    part_load.start()
    rout_t = rout_ref[...]
    atom_id = iota((BE, TE), 1).astype(F32)
    row_id = iota((CHUNK, TE), 0)

    def gather(p):
        for h in range(PER):
            j = begin + PER * p + h
            off = jnp.where(j < end, 0.0, 4096.0)
            j = jnp.maximum(jnp.minimum(j, end - 1), 0)
            c = jnp.clip(span_ref[2 * nb, j] - low, 0, count - 1)
            gate = lax.dot_general(
                rout_t, rbuf[p & 1, h], (((1,), (1,)), ((), ())), preferred_element_type=F32
            )
            pick = jnp.concatenate(
                [
                    as_bf16(row_id == src_ref[pl.ds(j * (BE // TE) + q, 1), :])
                    for q in range(BE // TE)
                ],
                axis=1,
            )
            rows = dot(tables[c], pick)
            for k in range(K):
                message = rows[cols(k), :] * gate[cols(degree_of[k]), :]
                message_ref[cols(k), h * BE : (h + 1) * BE] = message.astype(BF16)
            tgt = tbuf[p & 1, h].astype(F32) + off
            for q in range(ATOM_DEV // TE):
                land_ref[h * BE : (h + 1) * BE, q * TE : (q + 1) * TE] = as_bf16(
                    tgt == atom_id + float(q * TE)
                )

    def add_up():
        acc_ref[...] += dot(message_ref[...], land_ref[...])

    for load in loads:
        load.wait()
    saves = []
    for i in range(n_pick):
        pick_rows(tables[i], picks[i], near.at[i], far.at[i])
    for i in range(n_pick):
        for side, (src, dst) in enumerate(((near, near_hbm), (far, far_hbm))):
            save = pltpu.make_async_copy(src.at[i], dst.at[i], pick_sems.at[1 + side, i])
            save.start()
            saves.append(save)
    arrive(0)
    fetch(1)
    gather(0)
    part_load.wait()

    def step(p, carry):
        arrive(p + 1)
        fetch(p + 2)
        add_up()
        gather(p + 1)
        return carry

    lax.fori_loop(0, groups - 1, step, 0)

    @pl.when(groups > 0)
    def _():
        add_up()

    for save in saves:
        save.wait()
    if final:
        for k in range(K):
            out_ref[:, cols(k)] = (inv_scale * acc_ref[cols(k), :]).T.astype(BF16)


def shape(dims, kind):
    return jax.ShapeDtypeStruct(dims, kind)


def cost(flops, size):
    return pl.CostEstimate(flops=int(flops), bytes_accessed=int(size), transcendentals=0)


def body(
    embedding,
    ghost_index,
    tile_count,
    edge_source,
    edge_target,
    edge_features,
    radial_in,
    radial_out,
    mix_weight,
):
    n_dom, n_tile = lax.axis_size("dom"), lax.axis_size("tile")
    tiles = edge_source.shape[0] // TE
    nb = 2 * n_tile
    slots = (tiles * TE // BE + nb) * BE
    count = tile_count
    source = edge_source.reshape(tiles, TE)
    target = edge_target.reshape(tiles, TE)
    hbm = pl.BlockSpec(memory_space=pl.ANY)

    mixed = pl.pallas_call(
        mix_kernel,
        out_shape=shape((WIDTH + EXTRA, ATOM_DEV), BF16),
        in_specs=[vmem(), vmem(), vmem()],
        out_specs=vmem(),
        compiler_params=PARAMS,
        cost_estimate=cost(256 * 256 * 1152, 2e6),
        name="mix",
    )(embedding, mix_weight, ghost_index.reshape(1, ATOM_DEV))
    ring = [(t, (t + 2) % n_tile) for t in range(n_tile)]
    back = [(target, source) for source, target in ring]
    flip = [(t, t ^ 1) for t in range(n_tile)]
    near = [(i, i ^ 1) for i in range(n_dom)]
    far = [(i, i + 1) for i in range(1, n_dom - 1, 2)]
    far += [(j, i) for i, j in far]
    n_ring = n_tile // 2
    half = n_tile // 2

    pos, span = pl.pallas_call(
        functools.partial(rank_kernel, slots=slots),
        out_shape=(shape((tiles, TE), I32), shape((3 * nb, TE), I32)),
        in_specs=[smem(), vmem()],
        out_specs=(vmem(), vmem()),
        scratch_shapes=[
            pltpu.VMEM((tiles * nb, TE), BF16),
            pltpu.VMEM((tiles * nb, 2 * TE), F32),
        ],
        compiler_params=PARAMS,
        cost_estimate=cost(4e9, 1e6),
        name="rank",
    )(count, source)
    radial, radial_sum = pl.pallas_call(
        radial_kernel,
        out_shape=(shape((tiles * TE, C), BF16), shape((ATOM_DEV, C), F32)),
        in_specs=[smem(), vmem(), vmem(), vmem()],
        out_specs=(vmem(), vmem()),
        compiler_params=PARAMS,
        cost_estimate=cost(10e9, 6e6),
        name="radial",
    )(count, target, edge_features, radial_in)

    def place(radial):
        return pl.pallas_call(
            place_kernel,
            out_shape=(
                shape((slots, C), BF16),
                shape((slots, C), BF16),
                shape((slots // TE, TE), I32),
            ),
            in_specs=[smem(), smem(), smem(), vmem(), vmem(), hbm],
            out_specs=(hbm, hbm, vmem()),
            scratch_shapes=[
                pltpu.VMEM((2 * slots + 8, C), F32),
                pltpu.VMEM((2 * TE, C), F32),
                pltpu.VMEM((2 * TE, C), F32),
                pltpu.VMEM((slots, C), BF16),
                pltpu.VMEM((slots, C), BF16),
                pltpu.VMEM((tiles * TE, C), BF16),
                pltpu.SemaphoreType.DMA((2,)),
                pltpu.SemaphoreType.DMA((2, slots // BE)),
            ],
            compiler_params=PARAMS,
            cost_estimate=cost(20e9, 12e6),
            name="place",
        )(count, pos, span, source, target, radial)

    def pick(blocks):
        n = len(blocks)
        near_rows, far_rows = pl.pallas_call(
            functools.partial(pick_kernel, n=n),
            out_shape=(shape((n, WIDTH, GHOST), BF16),) * 2,
            in_specs=[hbm] * n,
            out_specs=(hbm, hbm),
            scratch_shapes=[
                pltpu.VMEM((n, WIDTH + EXTRA, ATOM_DEV), BF16),
                pltpu.VMEM((n, WIDTH, GHOST), BF16),
                pltpu.VMEM((n, WIDTH, GHOST), BF16),
                pltpu.SemaphoreType.DMA((3, n)),
            ],
            compiler_params=PARAMS,
            cost_estimate=cost(2e8, 4e5),
            name="pick",
        )(*blocks)
        return near_rows, far_rows

    base, rout_t = pl.pallas_call(
        base_kernel,
        out_shape=(shape((WIDTH, ATOM_DEV), F32), shape((3 * C, C), BF16)),
        in_specs=[vmem()] * 4,
        out_specs=(vmem(), vmem()),
        compiler_params=PARAMS,
        cost_estimate=cost(1e9, 2e6),
        name="base",
    )(radial_sum, radial_out, embedding, mix_weight)

    def main(low, ghosts, owns, part, name, n_pick=0, final=False):
        dims, kind = ((ATOM_DEV, WIDTH), BF16) if final else ((WIDTH, ATOM_DEV), F32)
        n_ghost = half if ghosts else 0
        count_all = n_ghost + len(owns)
        return pl.pallas_call(
            functools.partial(
                main_kernel,
                low=low,
                n_ghost=n_ghost,
                n_own=len(owns),
                n_pick=n_pick,
                final=final,
            ),
            out_shape=(shape(dims, kind),)
            + ((shape((n_pick, WIDTH, GHOST), BF16),) * 2 if n_pick else ()),
            in_specs=[smem()] + [hbm] * (len(ghosts) + len(owns) + 3) + [vmem()] * 2,
            out_specs=(vmem(),) + ((hbm, hbm) if n_pick else ()),
            scratch_shapes=[
                pltpu.VMEM((2, PER, BE, C), BF16),
                pltpu.VMEM((2, PER, BE, C), BF16),
                pltpu.VMEM((PER * BE, ATOM_DEV), BF16),
                pltpu.VMEM((WIDTH, PER * BE), BF16),
                pltpu.VMEM((count_all, WIDTH, ATOM_DEV), BF16),
                pltpu.SemaphoreType.DMA((2, PER, 2)),
                pltpu.SemaphoreType.DMA((2 * n_ghost + len(owns),)),
                pltpu.SemaphoreType.DMA,
            ]
            + ([pltpu.VMEM((WIDTH, ATOM_DEV), F32)] if final else [])
            + (
                [
                    pltpu.VMEM((n_pick, EXTRA, ATOM_DEV), BF16),
                    pltpu.VMEM((n_pick, WIDTH, GHOST), BF16),
                    pltpu.VMEM((n_pick, WIDTH, GHOST), BF16),
                    pltpu.SemaphoreType.DMA((3, n_pick)),
                ]
                if n_pick
                else []
            ),
            compiler_params=PARAMS,
            cost_estimate=cost(1e8 * count_all, 1e5 * count_all),
            name=name,
        )(span, *ghosts, *owns, radial_sorted, target_sorted, part, source_sorted, rout_t)

    together = lax.optimization_barrier

    def to_ring(rows):
        return lax.ppermute(rows, "tile", ring)

    def to_flip(rows):
        return lax.ppermute(rows, "tile", flip)

    def to_back(rows):
        return lax.ppermute(rows, "tile", back)

    few = half // 2
    ahead = [mixed, to_ring(mixed)]
    flips = [to_flip(together((mixed, span))[0])]
    ahead[1], radial, base, own = together((ahead[1], radial, base, mixed))
    while len(ahead) <= few:
        ahead.append(to_ring(ahead[-1]))
    flips.append(to_flip(ahead[1]))
    behind = [to_back(own)]
    while len(behind) < n_ring - 1 - few:
        behind.append(to_back(behind[-1]))
    radial_sorted, target_sorted, source_sorted = place(radial)
    ahead[2], flips[0], radial_sorted = together((ahead[2], flips[0], radial_sorted))
    rings = ahead + behind
    flips += [to_flip(rows) for rows in ahead[2:]]
    other = flips[0]
    for _ in behind:
        other = to_back(other)
        flips.append(other)
    owns = [rows for pair in zip(rings, flips) for rows in pair]

    def exchange_after(blocks, part):
        near_rows, far_rows = pick(blocks)
        near_rows, part = together((near_rows, part))
        return [lax.ppermute(near_rows, "dom", near), lax.ppermute(far_rows, "dom", far)], part

    ghosts_a, base = exchange_after(owns[:half], base)
    (part,) = main(0, [], owns[:half] + rings[few:], base, "main_one")
    last = owns[half:]
    last[0], part = together((last[0], part))
    ghosts_b, part = exchange_after(last, part)
    (part,) = main(half + few, ghosts_a, flips[few:], part, "main_two")
    return main(n_tile + half, ghosts_b, [], part, "main_three", final=True)[0]


def solution(mesh):
    both = ("dom", "tile")
    return jax.shard_map(
        body,
        mesh=mesh,
        in_specs=(
            P(both, None),
            P(both),
            P("dom", None),
            P(both),
            P(both),
            P(both, None),
            P(),
            P(),
            P(),
        ),
        out_specs=P(both, None),
        check_vma=False,
    )
```

```python
import functools
import jax
import jax.numpy as jnp
from jax import lax
from jax.experimental import pallas as pl
from jax.experimental.pallas import tpu as pltpu
from jax.sharding import PartitionSpec as P

C = 128
K = 9
ATOM_DEV = 256
GHOST = 128
TE = 128
BE = 256
CHUNK = 256
CHUNK_BITS = 8
WIDTH = K * C
EXTRA = 16
PER = 3
degree_of = (0, 1, 1, 1, 2, 2, 2, 2, 2)
inv_scale = 0.125

F32 = jnp.float32
BF16 = jnp.bfloat16
I32 = jnp.int32

PARAMS = pltpu.CompilerParams(vmem_limit_bytes=64 * 1024 * 1024)


def vmem():
    return pl.BlockSpec(memory_space=pltpu.VMEM)


def smem():
    return pl.BlockSpec(memory_space=pltpu.SMEM)


def cols(k):
    return slice(k * C, (k + 1) * C)


def iota(shape, dim):
    return lax.broadcasted_iota(I32, shape, dim)


def as_bf16(mask):
    return jnp.where(mask, 1.0, 0.0).astype(BF16)


def dot(a, b):
    return jnp.dot(a, b, preferred_element_type=F32)


def mix_kernel(x_ref, mix_ref, pick_ref, mixed_ref):
    for k in range(K):
        mixed = dot(x_ref[:, cols(k)], mix_ref[degree_of[k], :C])
        mixed_ref[cols(k), :] = mixed.T.astype(BF16)
    picks = jnp.broadcast_to(pick_ref[...].astype(F32), (EXTRA, ATOM_DEV))
    mixed_ref[WIDTH:, :] = picks.astype(BF16)


def pick_rows(table, picks, near_ref, far_ref):
    even = (lax.axis_index("dom") & 1) == 0
    picks = picks.astype(F32)[:1, :].astype(I32)
    down, up = picks[:, :GHOST], picks[:, GHOST:]
    row_id = iota((ATOM_DEV, GHOST), 0)
    chosen = jnp.concatenate(
        [
            as_bf16(row_id == jnp.where(even, up, down)),
            as_bf16(row_id == jnp.where(even, down, up)),
        ],
        axis=1,
    )
    rows = dot(table, chosen).astype(BF16)
    near_ref[...] = rows[:, :GHOST]
    far_ref[...] = rows[:, GHOST:]


def pick_kernel(*refs, n):
    blocks, refs = refs[:n], refs[n:]
    near_hbm, far_hbm, inside, near, far, sems = refs
    loads = [
        pltpu.make_async_copy(block, inside.at[i], sems.at[0, i]) for i, block in enumerate(blocks)
    ]
    saves = []
    for load in loads:
        load.start()
    for load in loads:
        load.wait()
    for i in range(n):
        pick_rows(inside[i, :WIDTH, :], inside[i, WIDTH:, :], near.at[i], far.at[i])
    for i in range(n):
        for side, (src, dst) in enumerate(((near, near_hbm), (far, far_hbm))):
            save = pltpu.make_async_copy(src.at[i], dst.at[i], sems.at[1 + side, i])
            save.start()
            saves.append(save)
    for save in saves:
        save.wait()


def base_kernel(rsum_ref, rout_ref, x_ref, mix_ref, base_ref, rout_t_ref):
    rout = rout_ref[...].astype(F32)
    rout_t_ref[...] = rout.T.astype(BF16)
    gate_sum = jnp.dot(
        rsum_ref[...], rout, preferred_element_type=F32, precision=lax.Precision.HIGHEST
    )
    for k in range(K):
        own = dot(x_ref[:, cols(k)], mix_ref[degree_of[k], C:])
        base_ref[cols(k), :] = (own * gate_sum[:, cols(degree_of[k])]).T


def live_tiles(count_ref):
    return count_ref[0, lax.axis_index("tile")]


def rank_kernel(count_ref, src_ref, pos_ref, span_ref, oh_ref, cum_ref, *, slots):
    tiles = src_ref.shape[0]
    nb = span_ref.shape[0] // 3
    count = live_tiles(count_ref)
    half, few = nb // 4, nb // 8
    order = iota((nb, TE), 0)
    ghost = ((order >= half + few) & (order < 2 * half + few)) | (order >= 3 * half)
    index = order
    index = jnp.where(order >= half, half + 2 * (order - half), index)
    index = jnp.where(order >= half + few, order - (half + few), index)
    index = jnp.where(order >= 2 * half + few, half + 2 * (order - (2 * half + few)) + 1, index)
    index = jnp.where(order >= 3 * half, order - 2 * half, index)
    tile_pos = lax.axis_index("tile")
    step = index >> 1
    ahead = half // 2
    ring_pos = (tile_pos >> 1) + jnp.where(step <= ahead, -step, step - ahead)
    ring_pos = jnp.where(ring_pos < 0, ring_pos + half, ring_pos)
    ring_pos = jnp.where(ring_pos >= half, ring_pos - half, ring_pos)
    label = 2 * (2 * ring_pos + ((tile_pos & 1) ^ (index & 1))) + jnp.where(ghost, 1, 0)

    def mark(t, carry):
        bucket = src_ref[pl.ds(t, 1), :] >> CHUNK_BITS
        bucket = jnp.where(t < count, bucket, -1)
        oh_ref[pl.ds(pl.multiple_of(t * nb, nb), nb), :] = as_bf16(label == bucket)
        return carry

    lax.fori_loop(0, tiles, mark, 0, unroll=8)
    upto = as_bf16(iota((TE, TE), 0) <= iota((TE, TE), 1))
    both = jnp.concatenate([upto, jnp.ones((TE, TE), BF16)], axis=1)
    step = 256
    for r in range(0, tiles * nb, step):
        cum_ref[r : r + step, :] = dot(oh_ref[r : r + step, :], both)

    def add(t, total):
        return total + cum_ref[pl.ds(pl.multiple_of(t * nb, nb), nb), TE:]

    total = lax.fori_loop(0, tiles, add, jnp.zeros((nb, TE), F32), unroll=8)
    blocks = jnp.floor((total + (BE - 1)) * (1.0 / BE))
    below = as_bf16(iota((nb, nb), 1) < iota((nb, nb), 0))
    first = dot(below, blocks.astype(BF16))
    span_ref[:nb, :] = first.astype(I32)
    span_ref[nb : 2 * nb, :] = blocks.astype(I32)
    passed = jnp.where(iota((nb, TE), 1).astype(F32) >= first + blocks, 1.0, 0.0)
    chunk_of = jnp.minimum(jnp.sum(passed, axis=0, keepdims=True), nb - 1.0)
    span_ref[2 * nb :, :] = jnp.broadcast_to(chunk_of, (nb, TE)).astype(I32)

    def place(t, run):
        rows = pl.ds(pl.multiple_of(t * nb, nb), nb)
        oh = oh_ref[rows, :].astype(F32)
        value = oh * (cum_ref[rows, :TE] + run)
        place_of = jnp.sum(value, axis=0, keepdims=True).astype(I32)
        pos_ref[pl.ds(t, 1), :] = jnp.where(t < count, 2 * place_of, 2 * slots)
        return run + cum_ref[rows, TE:]

    lax.fori_loop(0, tiles, place, first * BE - 1.0, unroll=8)


def radial_kernel(count_ref, tgt_ref, feat_ref, rin_ref, rad_ref, rsum_ref):
    tiles = tgt_ref.shape[0]
    count = live_tiles(count_ref)
    rsum_ref[...] = jnp.zeros_like(rsum_ref)
    group = 8
    atom_id = iota((ATOM_DEV, TE), 0)

    def rows_of(i):
        return pl.ds(pl.multiple_of(i * (group * TE), group * TE), group * TE)

    def hidden_layer(i):
        hidden = 0.5 * dot(feat_ref[rows_of(i), :], rin_ref[...])
        rad_ref[rows_of(i), :] = (hidden + hidden * jnp.tanh(hidden)).astype(BF16)

    def add_up(i):
        land = []
        for q in range(group):
            t = i * group + q
            tgt = jnp.where(t < count, tgt_ref[pl.ds(t, 1), :], -1)
            land.append(as_bf16(atom_id == tgt))
        rsum_ref[...] += dot(jnp.concatenate(land, axis=1), rad_ref[rows_of(i), :])

    hidden_layer(0)
    groups = (count + group - 1) // group

    def step(i, carry):
        add_up(i)
        hidden_layer(i + 1)
        return carry

    lax.fori_loop(0, groups - 1, step, 0)
    add_up(groups - 1)


def place_kernel(
    count_ref,
    pos_ref,
    span_ref,
    src_ref,
    tgt_ref,
    rin_hbm,
    rad_hbm,
    tgt_hbm,
    srcs_ref,
    pairs,
    even,
    odd,
    rad_out,
    tgt_out,
    rin_ref,
    rin_sems,
    sems,
):
    tiles = src_ref.shape[0]
    head = min(16, tiles) * TE
    loads = [
        pltpu.make_async_copy(rin_hbm.at[rows, :], rin_ref.at[rows, :], rin_sems.at[i])
        for i, rows in enumerate((pl.ds(0, head), pl.ds(head, tiles * TE - head)))
    ]
    for load in loads:
        load.start()
    nb = span_ref.shape[0] // 3
    count = live_tiles(count_ref)
    flip = jnp.where((lax.axis_index("dom") & 1) == 0, GHOST, 0)
    blank = jnp.where((iota((2 * BE, C), 0) & 1) == 1, -1.0, 0.0)

    def clear(b, carry):
        blocks = span_ref[nb + b, 0]

        @pl.when(blocks > 0)
        def _():
            last = pl.multiple_of((span_ref[b, 0] + blocks - 1) * (2 * BE), 2 * BE)
            pairs[pl.ds(last, 2 * BE), :] = blank

        return carry

    lax.fori_loop(0, nb, clear, 0)
    eye = iota((TE, TE), 0) == iota((TE, TE), 1)
    spread = jnp.concatenate(
        [jnp.ones((TE, C), BF16), jnp.full((TE, C), float(CHUNK), BF16)], axis=0
    )

    def compute(t, out):
        t = jnp.minimum(t, tiles - 1)
        rows = pl.ds(pl.multiple_of(t * TE, TE), TE)
        out[pl.ds(0, TE, stride=2), :] = rin_ref[rows, :].astype(F32)
        src = src_ref[pl.ds(t, 1), :]
        src = (src & (CHUNK - 1)) ^ jnp.where((src & CHUNK) != 0, flip, 0)
        tgt = tgt_ref[pl.ds(t, 1), :]
        diag_s = jnp.where(eye, src.astype(F32), 0.0).astype(BF16)
        diag_t = jnp.where(eye, tgt.astype(F32), 0.0).astype(BF16)
        code = dot(jnp.concatenate([diag_s, diag_t], axis=1), spread)
        out[pl.ds(1, TE, stride=2), :] = code

    def scatter(t, data):
        for e in range(TE):
            pairs[pl.ds(pos_ref[t, e], 2), :] = data[2 * e : 2 * e + 2, :]

    loads[0].wait()
    compute(0, even)

    def step(i, carry):
        compute(2 * i + 1, odd)
        scatter(2 * i, even)
        compute(2 * i + 2, even)
        scatter(2 * i + 1, odd)
        return carry

    steps = (count + 1) // 2
    split = jnp.minimum(steps, head // (2 * TE) - 1)
    lax.fori_loop(0, split, step, 0)
    loads[1].wait()
    lax.fori_loop(split, steps, step, 0)

    def saves(j):
        rows = pl.ds(pl.multiple_of(j * BE, BE), BE)
        return (
            pltpu.make_async_copy(rad_out.at[rows, :], rad_hbm.at[rows, :], sems.at[0, j]),
            pltpu.make_async_copy(tgt_out.at[rows, :], tgt_hbm.at[rows, :], sems.at[1, j]),
        )

    def finish(pair, carry):
        for h in range(2 * BE // TE):
            row = pair * (2 * BE // TE) + h
            rows = pl.ds(pl.multiple_of(row * TE, TE), TE)
            base = pl.multiple_of(row * (2 * TE), 2 * TE)
            rad_out[rows, :] = pairs[pl.ds(base, TE, stride=2), :].astype(BF16)
            code = pairs[pl.ds(base + 1, TE, stride=2), :]
            tgt = jnp.floor(code * (1.0 / CHUNK))
            tgt_out[rows, :] = tgt.astype(BF16)
            src = jnp.where(eye, code - CHUNK * tgt, 0.0)
            srcs_ref[pl.ds(row, 1), :] = jnp.sum(src, axis=0, keepdims=True).astype(I32)
        for h in range(2):
            for save in saves(2 * pair + h):
                save.start()
        return carry

    used = span_ref[nb - 1, 0] + span_ref[2 * nb - 1, 0]
    lax.fori_loop(0, (used + 1) // 2, finish, 0)

    def drain(j, carry):
        for save in saves(j):
            save.wait()
        return carry

    lax.fori_loop(0, 2 * ((used + 1) // 2), drain, 0)


def main_kernel(*refs, low, n_ghost, n_own, n_pick, final):
    span_ref, *refs = refs
    ghosts, refs = refs[: 2 * (n_ghost > 0)], refs[2 * (n_ghost > 0) :]
    owns, refs = refs[:n_own], refs[n_own:]
    rad_hbm, tgt_hbm, part_hbm, src_ref, rout_ref, *refs = refs
    out_ref, *refs = refs
    if n_pick:
        near_hbm, far_hbm, *refs = refs
    rbuf, tbuf, land_ref, message_ref, tables, sems, table_sems, part_sem, *refs = refs
    acc_ref = refs[0] if final else out_ref
    if n_pick:
        picks, near, far, pick_sems = refs
    count = n_ghost + n_own
    nb = span_ref.shape[0] // 3
    begin = span_ref[low, 0]
    end = span_ref[low + count - 1, 0] + span_ref[nb + low + count - 1, 0]
    groups = (end - begin + PER - 1) // PER

    loads = []
    for i, own in enumerate(owns):
        loads.append((own.at[:WIDTH, :], tables.at[n_ghost + i]))
    for i in range(n_ghost):
        for side in range(2):
            half = tables.at[i, :, side * GHOST : (side + 1) * GHOST]
            loads.append((ghosts[side].at[i], half))
    loads = [
        pltpu.make_async_copy(src, dst, table_sems.at[i]) for i, (src, dst) in enumerate(loads)
    ]
    for i in range(n_pick):
        load = pltpu.make_async_copy(owns[i].at[WIDTH:, :], picks.at[i], pick_sems.at[0, i])
        loads.append(load)
    def copies(p, slot):
        moves = []
        for h in range(PER):
            j = jnp.minimum(begin + PER * p + h, end - 1)
            rows = pl.ds(pl.multiple_of(j * BE, BE), BE)
            moves.append(
                pltpu.make_async_copy(rad_hbm.at[rows, :], rbuf.at[slot, h], sems.at[0, h, slot])
            )
            moves.append(
                pltpu.make_async_copy(tgt_hbm.at[rows, :], tbuf.at[slot, h], sems.at[1, h, slot])
            )
        return moves

    def fetch(p):
        @pl.when(p < groups)
        def _():
            for copy in copies(p, p & 1):
                copy.start()

    def arrive(p):
        @pl.when(p < groups)
        def _():
            for copy in copies(p, p & 1):
                copy.wait()

    fetch(0)
    for load in loads:
        load.start()
    part_load = pltpu.make_async_copy(part_hbm, acc_ref, part_sem)
    part_load.start()
    rout_t = rout_ref[...]
    atom_id = iota((BE, TE), 1).astype(F32)
    row_id = iota((CHUNK, TE), 0)

    def gather(p):
        for h in range(PER):
            j = begin + PER * p + h
            off = jnp.where(j < end, 0.0, 4096.0)
            j = jnp.maximum(jnp.minimum(j, end - 1), 0)
            c = jnp.clip(span_ref[2 * nb, j] - low, 0, count - 1)
            gate = lax.dot_general(
                rout_t, rbuf[p & 1, h], (((1,), (1,)), ((), ())), preferred_element_type=F32
            )
            pick = jnp.concatenate(
                [
                    as_bf16(row_id == src_ref[pl.ds(j * (BE // TE) + q, 1), :])
                    for q in range(BE // TE)
                ],
                axis=1,
            )
            rows = dot(tables[c], pick)
            for k in range(K):
                message = rows[cols(k), :] * gate[cols(degree_of[k]), :]
                message_ref[cols(k), h * BE : (h + 1) * BE] = message.astype(BF16)
            tgt = tbuf[p & 1, h].astype(F32) + off
            for q in range(ATOM_DEV // TE):
                land_ref[h * BE : (h + 1) * BE, q * TE : (q + 1) * TE] = as_bf16(
                    tgt == atom_id + float(q * TE)
                )

    def add_up():
        acc_ref[...] += dot(message_ref[...], land_ref[...])

    for load in loads:
        load.wait()
    saves = []
    for i in range(n_pick):
        pick_rows(tables[i], picks[i], near.at[i], far.at[i])
    for i in range(n_pick):
        for side, (src, dst) in enumerate(((near, near_hbm), (far, far_hbm))):
            save = pltpu.make_async_copy(src.at[i], dst.at[i], pick_sems.at[1 + side, i])
            save.start()
            saves.append(save)
    arrive(0)
    fetch(1)
    gather(0)
    part_load.wait()

    def step(p, carry):
        arrive(p + 1)
        fetch(p + 2)
        add_up()
        gather(p + 1)
        return carry

    lax.fori_loop(0, groups - 1, step, 0)

    @pl.when(groups > 0)
    def _():
        add_up()

    for save in saves:
        save.wait()
    if final:
        for k in range(K):
            out_ref[:, cols(k)] = (inv_scale * acc_ref[cols(k), :]).T.astype(BF16)


def shape(dims, kind):
    return jax.ShapeDtypeStruct(dims, kind)


def cost(flops, size):
    return pl.CostEstimate(flops=int(flops), bytes_accessed=int(size), transcendentals=0)


def body(
    embedding,
    ghost_index,
    tile_count,
    edge_source,
    edge_target,
    edge_features,
    radial_in,
    radial_out,
    mix_weight,
):
    n_dom, n_tile = lax.axis_size("dom"), lax.axis_size("tile")
    tiles = edge_source.shape[0] // TE
    nb = 2 * n_tile
    slots = (tiles * TE // BE + nb) * BE
    count = tile_count
    source = edge_source.reshape(tiles, TE)
    target = edge_target.reshape(tiles, TE)
    hbm = pl.BlockSpec(memory_space=pl.ANY)

    mixed = pl.pallas_call(
        mix_kernel,
        out_shape=shape((WIDTH + EXTRA, ATOM_DEV), BF16),
        in_specs=[vmem(), vmem(), vmem()],
        out_specs=vmem(),
        compiler_params=PARAMS,
        cost_estimate=cost(256 * 256 * 1152, 2e6),
        name="mix",
    )(embedding, mix_weight, ghost_index.reshape(1, ATOM_DEV))
    ring = [(t, (t + 2) % n_tile) for t in range(n_tile)]
    back = [(target, source) for source, target in ring]
    flip = [(t, t ^ 1) for t in range(n_tile)]
    near = [(i, i ^ 1) for i in range(n_dom)]
    far = [(i, i + 1) for i in range(1, n_dom - 1, 2)]
    far += [(j, i) for i, j in far]
    n_ring = n_tile // 2
    half = n_tile // 2

    pos, span = pl.pallas_call(
        functools.partial(rank_kernel, slots=slots),
        out_shape=(shape((tiles, TE), I32), shape((3 * nb, TE), I32)),
        in_specs=[smem(), vmem()],
        out_specs=(vmem(), vmem()),
        scratch_shapes=[
            pltpu.VMEM((tiles * nb, TE), BF16),
            pltpu.VMEM((tiles * nb, 2 * TE), F32),
        ],
        compiler_params=PARAMS,
        cost_estimate=cost(4e9, 1e6),
        name="rank",
    )(count, source)
    radial, radial_sum = pl.pallas_call(
        radial_kernel,
        out_shape=(shape((tiles * TE, C), BF16), shape((ATOM_DEV, C), F32)),
        in_specs=[smem(), vmem(), vmem(), vmem()],
        out_specs=(vmem(), vmem()),
        compiler_params=PARAMS,
        cost_estimate=cost(10e9, 6e6),
        name="radial",
    )(count, target, edge_features, radial_in)

    def place(radial):
        return pl.pallas_call(
            place_kernel,
            out_shape=(
                shape((slots, C), BF16),
                shape((slots, C), BF16),
                shape((slots // TE, TE), I32),
            ),
            in_specs=[smem(), smem(), smem(), vmem(), vmem(), hbm],
            out_specs=(hbm, hbm, vmem()),
            scratch_shapes=[
                pltpu.VMEM((2 * slots + 8, C), F32),
                pltpu.VMEM((2 * TE, C), F32),
                pltpu.VMEM((2 * TE, C), F32),
                pltpu.VMEM((slots, C), BF16),
                pltpu.VMEM((slots, C), BF16),
                pltpu.VMEM((tiles * TE, C), BF16),
                pltpu.SemaphoreType.DMA((2,)),
                pltpu.SemaphoreType.DMA((2, slots // BE)),
            ],
            compiler_params=PARAMS,
            cost_estimate=cost(20e9, 12e6),
            name="place",
        )(count, pos, span, source, target, radial)

    def pick(blocks):
        n = len(blocks)
        near_rows, far_rows = pl.pallas_call(
            functools.partial(pick_kernel, n=n),
            out_shape=(shape((n, WIDTH, GHOST), BF16),) * 2,
            in_specs=[hbm] * n,
            out_specs=(hbm, hbm),
            scratch_shapes=[
                pltpu.VMEM((n, WIDTH + EXTRA, ATOM_DEV), BF16),
                pltpu.VMEM((n, WIDTH, GHOST), BF16),
                pltpu.VMEM((n, WIDTH, GHOST), BF16),
                pltpu.SemaphoreType.DMA((3, n)),
            ],
            compiler_params=PARAMS,
            cost_estimate=cost(2e8, 4e5),
            name="pick",
        )(*blocks)
        return near_rows, far_rows

    base, rout_t = pl.pallas_call(
        base_kernel,
        out_shape=(shape((WIDTH, ATOM_DEV), F32), shape((3 * C, C), BF16)),
        in_specs=[vmem()] * 4,
        out_specs=(vmem(), vmem()),
        compiler_params=PARAMS,
        cost_estimate=cost(1e9, 2e6),
        name="base",
    )(radial_sum, radial_out, embedding, mix_weight)

    def main(low, ghosts, owns, part, name, n_pick=0, final=False):
        dims, kind = ((ATOM_DEV, WIDTH), BF16) if final else ((WIDTH, ATOM_DEV), F32)
        n_ghost = half if ghosts else 0
        count_all = n_ghost + len(owns)
        return pl.pallas_call(
            functools.partial(
                main_kernel,
                low=low,
                n_ghost=n_ghost,
                n_own=len(owns),
                n_pick=n_pick,
                final=final,
            ),
            out_shape=(shape(dims, kind),)
            + ((shape((n_pick, WIDTH, GHOST), BF16),) * 2 if n_pick else ()),
            in_specs=[smem()] + [hbm] * (len(ghosts) + len(owns) + 3) + [vmem()] * 2,
            out_specs=(vmem(),) + ((hbm, hbm) if n_pick else ()),
            scratch_shapes=[
                pltpu.VMEM((2, PER, BE, C), BF16),
                pltpu.VMEM((2, PER, BE, C), BF16),
                pltpu.VMEM((PER * BE, ATOM_DEV), BF16),
                pltpu.VMEM((WIDTH, PER * BE), BF16),
                pltpu.VMEM((count_all, WIDTH, ATOM_DEV), BF16),
                pltpu.SemaphoreType.DMA((2, PER, 2)),
                pltpu.SemaphoreType.DMA((2 * n_ghost + len(owns),)),
                pltpu.SemaphoreType.DMA,
            ]
            + ([pltpu.VMEM((WIDTH, ATOM_DEV), F32)] if final else [])
            + (
                [
                    pltpu.VMEM((n_pick, EXTRA, ATOM_DEV), BF16),
                    pltpu.VMEM((n_pick, WIDTH, GHOST), BF16),
                    pltpu.VMEM((n_pick, WIDTH, GHOST), BF16),
                    pltpu.SemaphoreType.DMA((3, n_pick)),
                ]
                if n_pick
                else []
            ),
            compiler_params=PARAMS,
            cost_estimate=cost(1e8 * count_all, 1e5 * count_all),
            name=name,
        )(span, *ghosts, *owns, radial_sorted, target_sorted, part, source_sorted, rout_t)

    together = lax.optimization_barrier

    def to_ring(rows):
        return lax.ppermute(rows, "tile", ring)

    def to_flip(rows):
        return lax.ppermute(rows, "tile", flip)

    def to_back(rows):
        return lax.ppermute(rows, "tile", back)

    few = half // 2
    ahead = [mixed, to_ring(mixed)]
    flips = [to_flip(together((mixed, span))[0])]
    ahead[1], radial, base, own = together((ahead[1], radial, base, mixed))
    while len(ahead) <= few:
        ahead.append(to_ring(ahead[-1]))
    flips.append(to_flip(ahead[1]))
    behind = [to_back(own)]
    while len(behind) < n_ring - 1 - few:
        behind.append(to_back(behind[-1]))
    radial_sorted, target_sorted, source_sorted = place(radial)
    ahead[2], flips[0], radial_sorted = together((ahead[2], flips[0], radial_sorted))
    rings = ahead + behind
    flips += [to_flip(rows) for rows in ahead[2:]]
    other = flips[0]
    for _ in behind:
        other = to_back(other)
        flips.append(other)
    owns = [rows for pair in zip(rings, flips) for rows in pair]

    def exchange_after(blocks, part):
        near_rows, far_rows = pick(blocks)
        near_rows, part = together((near_rows, part))
        return [lax.ppermute(near_rows, "dom", near), lax.ppermute(far_rows, "dom", far)], part

    ghosts_a, base = exchange_after(owns[:half], base)
    (part,) = main(0, [], owns[:half] + rings[few:], base, "main_one")
    last = owns[half:]
    last[0], part = together((last[0], part))
    ghosts_b, part = exchange_after(last, part)
    (part,) = main(half + few, ghosts_a, flips[few:], part, "main_two")
    return main(n_tile + half, ghosts_b, [], part, "main_three", final=True)[0]


def solution(mesh):
    both = ("dom", "tile")
    return jax.shard_map(
        body,
        mesh=mesh,
        in_specs=(
            P(both, None),
            P(both),
            P("dom", None),
            P(both),
            P(both),
            P(both, None),
            P(),
            P(),
            P(),
        ),
        out_specs=P(both, None),
        check_vma=False,
    )
```
